32 devices in a mesh: sec: 8 (over z, x), op: 4 (over y, core).
Axes of the slice: x: 2, y: 2, z: 4, core: 2. Of those that a mesh axis runs over, the one named last changes fastest.
Arguments:
- wavefunction: bfloat16 [16, 512, 512], P('sec'), may hold values from -24 to 24
- left_blocks: bfloat16 [16, 16, 512, 512], P('op', 'sec'), may hold values from -5 to 5
- right_blocks: bfloat16 [16, 512, 512], P('op'), may hold values from -1 to 1
- charge_shifts: int32 [16], P('op'), may hold values from -2 to 2, as said below
- sector_rows: int32 [16], replicated, may hold values from 64 to 512, as said below
Outputs:
- next_vector: bfloat16 [16, 512, 512], P('sec')
- lanczos_coefficients: float32 [2, 3], replicated
The draws below stay inside these ranges and needn't reach their ends.
Inputs may be any that keep to these rules, and one draw needn't show every extreme that they name: `charge_shifts`: some term has offset 2, some has offset -2, and some has offset 0. `sector_rows`: multiples of 64; some sector has 512 rows.
All inputs are finite; a program needn't handle non-finite values.
Results may differ from the reference program's by a relative error of at most 0.025.
Values may be sent and summed in bfloat16 or wider, within the bound.
No kernel may reach another device: no remote copies, remote signals or barrier semaphores. Data moves between devices by JAX's collectives and lax.ppermute only.
A program may use at most 64 MiB of HBM per device.

```python
import jax
import jax.numpy as jnp
from jax import lax

BLK = 512
NR = 512
TERM_DEV = 4
PRODUCTS = 3
SECTORS = 16
TERMS = 16
DMAX = 2
N_OP = 4


def draw_charge_shifts(key, part):
    key_values, key_placed = jax.random.split(jax.random.fold_in(key, 11))
    values = jax.random.randint(key_values, (TERMS,), -DMAX, DMAX + 1)
    placed = jax.random.permutation(key_placed, TERMS)
    values = values.at[placed[0]].set(DMAX).at[placed[1]].set(-DMAX).at[placed[2]].set(0)
    return values.astype(jnp.int32)


def draw_sector_rows(key, part):
    key_units, key_full = jax.random.split(jax.random.fold_in(key, 23))
    units = jax.random.randint(key_units, (SECTORS,), 1, 9)
    picked = jax.random.randint(key_full, (), 0, SECTORS)
    units = units.at[picked].set(8)
    return (units * (BLK // 8)).astype(jnp.int32)


def sector_ramp(low, ratio):
    place = jnp.arange(SECTORS, dtype=jnp.float32) / jnp.float32(SECTORS - 1)
    return low * jnp.exp(place * jnp.log(jnp.float32(ratio)))


def falling_ramp(low, ratio):
    place = 1.0 - jnp.arange(SECTORS, dtype=jnp.float32) / jnp.float32(SECTORS - 1)
    return low * jnp.exp(place * jnp.log(jnp.float32(ratio)))


def draw_wavefunction(key, part):
    inner = jax.random.fold_in(key, 31)
    noise = jnp.clip(jax.random.normal(inner, (SECTORS, BLK, NR), jnp.float32), -4.0, 4.0)
    ramp = falling_ramp(0.5, 6.0)
    return (noise * ramp[:, None, None]).astype(jnp.bfloat16)


def draw_left_blocks(key, part):
    inner = jax.random.fold_in(key, 37)
    noise = jnp.clip(jax.random.normal(inner, (TERMS, SECTORS, BLK, BLK), jnp.float32), -4.0, 4.0)
    ramp = sector_ramp(0.5, 8.0)
    rows = jnp.arange(BLK, dtype=jnp.int32)
    eye = (rows[:, None] == rows[None, :]).astype(jnp.float32)
    return (noise / jnp.sqrt(jnp.float32(BLK)) + ramp[None, :, None, None] * eye[None, None, :, :]).astype(jnp.bfloat16)


def draw_right_blocks(key, part):
    inner = jax.random.fold_in(key, 41)
    noise = jnp.clip(jax.random.normal(inner, (TERMS, NR, NR), jnp.float32), -4.0, 4.0)
    strength = 2.0
    rows = jnp.arange(NR, dtype=jnp.int32)
    eye = (rows[:, None] == rows[None, :]).astype(jnp.float32)
    return (noise / jnp.sqrt(jnp.float32(NR * TERMS)) + strength / TERMS * eye[None, :, :]).astype(jnp.bfloat16)


def setup_inputs(seed: int = 0) -> dict:
    key_list = jax.random.split(jax.random.key(seed), 6)
    wavefunction = draw_wavefunction(jax.random.fold_in(key_list[5], 71), 0)
    left_blocks = draw_left_blocks(jax.random.fold_in(key_list[5], 71), 0)
    right_blocks = draw_right_blocks(jax.random.fold_in(key_list[5], 71), 0)
    charge_shifts = draw_charge_shifts(jax.random.fold_in(key_list[5], 71), 0)
    sector_rows = draw_sector_rows(jax.random.fold_in(key_list[5], 71), 0)
    return dict(wavefunction=wavefunction, left_blocks=left_blocks, right_blocks=right_blocks, charge_shifts=charge_shifts, sector_rows=sector_rows)


def apply_terms(vector, left_blocks, right_blocks, charge_shifts, row_mask):
    zeros_pad = jnp.zeros((DMAX, BLK, NR), jnp.bfloat16)
    padded = jnp.concatenate([zeros_pad, vector, zeros_pad], axis=0)
    total = jnp.zeros((SECTORS, BLK, NR), jnp.float32)
    for group in range(N_OP):

        def one_term(carry, term):
            shift = lax.dynamic_index_in_dim(charge_shifts, term, 0, keepdims=False)
            window = lax.dynamic_slice_in_dim(padded, (DMAX - shift).astype(jnp.int32), SECTORS, 0)
            right_mat = lax.dynamic_index_in_dim(right_blocks, term, 0, keepdims=False)
            left_mat = lax.dynamic_index_in_dim(left_blocks, term, 0, keepdims=False)
            right_part = jnp.einsum('sbn,nm->sbm', window.astype(jnp.float32), right_mat.astype(jnp.float32)).astype(jnp.bfloat16)
            return (carry + jnp.einsum('sab,sbm->sam', left_mat.astype(jnp.float32), right_part.astype(jnp.float32)), None)
        terms_list = jnp.arange(TERM_DEV, dtype=jnp.int32) + group * TERM_DEV
        partial_value, _ = lax.scan(one_term, jnp.zeros((SECTORS, BLK, NR), jnp.float32), terms_list)
        rounded = lax.optimization_barrier(partial_value.astype(jnp.bfloat16))
        total = total + rounded.astype(jnp.float32)
    return total * row_mask

def reference(wavefunction, left_blocks, right_blocks, charge_shifts, sector_rows):
    positions = jnp.arange(BLK, dtype=jnp.int32)
    row_mask = (positions[None, :] < sector_rows[:, None]).astype(jnp.float32)[:, :, None]
    live_count = NR * jnp.sum(sector_rows).astype(jnp.float32)
    masked_start = wavefunction.astype(jnp.float32) * row_mask
    vector = (masked_start / jnp.sqrt(jnp.sum(masked_start * masked_start) / live_count)).astype(jnp.bfloat16)
    previous = jnp.zeros((SECTORS, BLK, NR), jnp.float32)
    beta = jnp.float32(0.0)
    alphas = []
    betas = []
    for product in range(PRODUCTS):
        image = apply_terms(vector, left_blocks, right_blocks, charge_shifts, row_mask)
        current = vector.astype(jnp.float32)
        alpha = jnp.sum(current * image) / live_count
        residual = image - alpha * current - beta * previous
        beta = jnp.sqrt(jnp.sum(residual * residual) / live_count)
        previous = current
        vector = (residual / beta).astype(jnp.bfloat16)
        alphas.append(alpha)
        betas.append(beta)
    return (vector, jnp.stack([jnp.stack(alphas), jnp.stack(betas)]))
```

```python
import functools

import jax
import jax.numpy as jnp
from jax import lax
from jax.experimental import pallas as pl
from jax.experimental.pallas import tpu as pltpu
from jax.sharding import PartitionSpec as P

PRODUCTS = 3
F32 = jnp.float32
BF16 = jnp.bfloat16
VMEM = pl.BlockSpec(memory_space=pltpu.VMEM)
SMEM = pl.BlockSpec(memory_space=pltpu.SMEM)
CORE, SEC, LIVE, ROWS, SHIFTS = 0, 1, 2, 3, 5


def call(kernel, name, out, scratch, *operands, flops=0):
    moved = sum(a.size * a.dtype.itemsize for a in operands)
    return pl.pallas_call(
        kernel,
        name=name,
        out_shape=out,
        in_specs=[SMEM] + [VMEM] * (len(operands) - 1),
        out_specs=jax.tree.map(lambda _: VMEM, out),
        scratch_shapes=scratch,
        compiler_params=pltpu.CompilerParams(vmem_limit_bytes=24 << 20),
        cost_estimate=pl.CostEstimate(flops=flops, bytes_accessed=moved, transcendentals=0),
    )(*operands)


def lane_sums(value):
    rows, columns = value.shape
    folded = sum(value[:, i : i + 128] for i in range(0, columns, 128))
    return jnp.sum(folded, axis=0, keepdims=True)


def total(stats_ref, row, live):
    return jnp.sum(stats_ref[row : row + 1, :], axis=1, keepdims=True) / live


def write_sums(stats_ref, values):
    rows = stats_ref.shape[0]
    parts = [lane_sums(v) for v in values]
    parts += [jnp.zeros((1, 128), F32)] * (rows - len(parts))
    stats_ref[...] = jnp.concatenate(parts, axis=0)


def coefficients(stats, live):
    norm = jnp.sqrt(total(stats[0], 0, live))
    alphas, betas = [], []
    for k, ref in enumerate(stats[1:]):
        alpha = total(ref, 1, live)
        square = total(ref, 0, live) - alpha * alpha
        if k:
            square = square - 2.0 * betas[-1] * total(ref, 2, live) + betas[-1] * betas[-1]
        alphas.append(alpha)
        betas.append(jnp.sqrt(jnp.maximum(square, 0.0)))
    return norm, alphas, betas


def lanczos_vectors(start, images, norm, alphas, betas):
    vectors = [start / norm]
    for k, beta in enumerate(betas):
        residual = images[k] - alphas[k] * vectors[k]
        if k:
            residual = residual - betas[k - 1] * vectors[k - 1]
        vectors.append(residual / beta)
    return vectors


def start_kernel(info, x_ref, *refs):
    *halves, stats_ref = refs
    sectors, block_rows, _ = x_ref.shape
    half = block_rows // 2
    core = info[CORE]
    square = 0.0
    for t in range(sectors):
        for which in range(2):
            first = pl.multiple_of((core if which == 0 else 1 - core) * half, half)
            value = x_ref[t, pl.ds(first, half), :]
            rows = lax.broadcasted_iota(jnp.int32, value.shape, 0) + first
            value = jnp.where(rows < info[ROWS + t], value, jnp.zeros_like(value))
            halves[2 * t + which][...] = value
            if which == 0:
                wide = value.astype(F32)
                square = square + wide * wide
    write_sums(stats_ref, [square])


def select_source(info, block, refs, v_ref):
    half = refs[0].shape[0]
    core = info[CORE]
    even = info[SEC] % 2 == 0
    mine = pl.ds(pl.multiple_of(core * half, half), half)
    other = pl.ds(pl.multiple_of((1 - core) * half, half), half)
    from_pair = (block == 1) == even
    for k, here in enumerate(
        (block == 0, (block != 0) & from_pair, (block != 0) & jnp.logical_not(from_pair))
    ):

        @pl.when(here)
        def _():
            v_ref[mine, :] = refs[2 * k][...]
            v_ref[other, :] = refs[2 * k + 1][...]


def apply_term(info, w, target, refs, left_ref, right_ref, v_ref, acc_ref):
    select_source(info, (target - info[SHIFTS + w]) >> 1, refs, v_ref)
    part = jnp.dot(v_ref[...], right_ref[w], preferred_element_type=F32).astype(BF16)
    acc_ref[...] += jnp.dot(left_ref[w, target], part, preferred_element_type=F32)


def first_kernel(info, *refs):
    *sources, left_ref, right_ref, acc_ref, v_ref = refs
    acc_ref[...] = jnp.zeros_like(acc_ref)

    def step(w, carry):
        target = info[SHIFTS + w] & 1
        apply_term(info, w, target, sources, left_ref, right_ref, v_ref, acc_ref.at[target])
        return carry

    lax.fori_loop(0, left_ref.shape[0], step, 0)


def second_kernel(target, info, *refs):
    *sources, left_ref, right_ref, sum_ref, mine_ref, other_ref, v_ref, acc_ref = refs
    half = mine_ref.shape[0]
    acc_ref[...] = sum_ref[target]

    def step(w, carry):
        @pl.when(((info[SHIFTS + w] + 1) & 1) == target)
        def _():
            apply_term(info, w, target, sources, left_ref, right_ref, v_ref, acc_ref)

        return carry

    lax.fori_loop(0, left_ref.shape[0], step, 0)
    core = info[CORE]
    mine_ref[...] = acc_ref[pl.ds(pl.multiple_of(core * half, half), half), :].astype(BF16)
    other_ref[...] = acc_ref[pl.ds(pl.multiple_of((1 - core) * half, half), half), :].astype(BF16)


def add_kernel(info, a_ref, b_ref, out_ref):
    out_ref[...] = (a_ref[...].astype(F32) + b_ref[...].astype(F32)).astype(BF16)


def image_kernel(product, target, info, *refs):
    a_ref, b_ref, start_ref = refs[:3]
    images = [r[...].astype(F32) for r in refs[3 : 3 + product]]
    stats = refs[3 + product : 4 + 2 * product]
    out_ref, stats_ref = refs[4 + 2 * product :]
    columns = out_ref.shape[1]
    live = info[LIVE].astype(F32) * columns
    norm, alphas, betas = coefficients(stats, live)
    vectors = lanczos_vectors(start_ref[...].astype(F32), images, norm, alphas, betas)
    value = a_ref[...].astype(F32) + b_ref[...].astype(F32)
    if product == 0:
        value = value / norm
    else:
        value = value - alphas[-1] * images[-1]
        if product > 1:
            value = value - betas[-2] * images[-2]
        value = value / betas[-1]
    rows = lax.broadcasted_iota(jnp.int32, value.shape, 0) + info[CORE] * value.shape[0]
    value = jnp.where(rows < info[ROWS + target], value, 0.0)
    out_ref[...] = value.astype(BF16)
    value = value.astype(BF16).astype(F32)
    sums = [value * value, value * vectors[-1]]
    if product:
        sums.append(value * vectors[-2])
    write_sums(stats_ref, sums)


def last_kernel(products, info, *refs):
    per_sector = 2 * (products + 1)
    stats = refs[-3 - products : -2]
    out_ref, coef_ref = refs[-2:]
    sectors, block_rows, columns = out_ref.shape
    half = block_rows // 2
    live = info[LIVE].astype(F32) * columns
    norm, alphas, betas = coefficients(stats, live)
    for t in range(sectors):
        for which in range(2):
            basis = [
                refs[t * per_sector + 2 * k + which][...].astype(F32) for k in range(products + 1)
            ]
            vector = lanczos_vectors(basis[0], basis[1:], norm, alphas, betas)[-1]
            core = info[CORE] if which == 0 else 1 - info[CORE]
            out_ref[t, pl.ds(pl.multiple_of(core * half, half), half), :] = vector.astype(BF16)
    row = lax.broadcasted_iota(jnp.int32, coef_ref.shape, 0)
    column = lax.broadcasted_iota(jnp.int32, coef_ref.shape, 1)
    value = jnp.zeros(coef_ref.shape, F32)
    for k in range(products):
        value = jnp.where((row == 0) & (column == k), alphas[k], value)
        value = jnp.where((row == 1) & (column == k), betas[k], value)
    coef_ref[...] = value


def on_device(wavefunction, left_blocks, right_blocks, charge_shifts, sector_rows):
    sectors, block_rows, columns = wavefunction.shape
    half = block_rows // 2
    n_sec, n_op = lax.axis_size("sec"), lax.axis_size("op")
    assert sectors == 2 and n_sec % 2 == 0 and n_op % 2 == 0
    sec, op = lax.axis_index("sec"), lax.axis_index("op")
    core_pairs = [(i, i ^ 1) for i in range(n_op)]
    pairs = [(i, i ^ 1) for i in range(n_sec)]
    onward = [(i, i + 2) for i in range(0, n_sec - 2, 2)]
    onward += [(i, i - 2) for i in range(3, n_sec, 2)]

    def across_cores(value):
        return lax.ppermute(value, "op", core_pairs)

    def sum_all(stats):
        stats = stats + across_cores(stats)
        bit = 1
        while bit < n_sec:
            stats = stats + lax.ppermute(stats, "sec", [(i, i ^ bit) for i in range(n_sec)])
            bit *= 2
        return stats

    local_rows = lax.dynamic_slice_in_dim(sector_rows, sec * sectors, sectors, 0)
    info = jnp.concatenate(
        [
            jnp.stack([op % 2, sec, jnp.sum(sector_rows)]).astype(jnp.int32),
            local_rows,
            charge_shifts,
        ]
    )
    half_type = jax.ShapeDtypeStruct((half, columns), BF16)
    stats_type = jax.ShapeDtypeStruct((8, 128), F32)
    acc_type = jax.ShapeDtypeStruct((sectors, block_rows, columns), F32)
    v_scratch = pltpu.VMEM((block_rows, columns), BF16)
    acc_scratch = pltpu.VMEM((block_rows, columns), F32)

    *halves, start_stats = call(
        start_kernel, "start", [half_type] * (2 * sectors) + [stats_type], [], info, wavefunction
    )
    basis = [[(halves[0], halves[1]), (halves[2], halves[3])]]
    stats = [sum_all(start_stats)]
    pair_flops = 4 * block_rows * block_rows * columns
    terms = left_blocks.shape[0]

    for product in range(PRODUCTS):
        sources = []
        for t in range(sectors):
            mine, other = basis[-1][t]
            pair = lax.ppermute(mine, "sec", pairs)
            far = lax.ppermute(pair, "sec", onward)
            sources.append((mine, other, pair, across_cores(pair), far, across_cores(far)))
        acc = call(
            first_kernel, "first", acc_type, [v_scratch],
            info, *sources[0], left_blocks, right_blocks, flops=terms * pair_flops,
        )
        image = []
        sums = []
        for t in range(sectors):
            mine, other = call(
                functools.partial(second_kernel, t), "second", [half_type] * 2,
                [v_scratch, acc_scratch],
                info, *sources[1], left_blocks, right_blocks, acc, flops=terms * pair_flops // 2,
            )
            value = call(add_kernel, "add", half_type, [], info, mine, across_cores(other))
            bit = 2
            while 2 * bit < n_op:
                arrived = lax.ppermute(value, "op", [(i, i ^ bit) for i in range(n_op)])
                value = call(add_kernel, "add", half_type, [], info, value, arrived)
                bit *= 2
            arrived = lax.ppermute(value, "op", [(i, i ^ bit) for i in range(n_op)])
            mine, part = call(
                functools.partial(image_kernel, product, t), "image", [half_type, stats_type], [],
                info, value, arrived, *[b[t][0] for b in basis], *stats,
            )
            image.append((mine, across_cores(mine)))
            sums.append(part)
        basis.append(image)
        stats.append(sum_all(sums[0] + sums[1]))

    flat = [h for t in range(sectors) for b in basis for h in b[t]]
    vector_type = jax.ShapeDtypeStruct(wavefunction.shape, BF16)
    coef_type = jax.ShapeDtypeStruct((2, PRODUCTS), F32)
    vector, coef = call(
        functools.partial(last_kernel, PRODUCTS), "last", [vector_type, coef_type], [],
        info, *flat, *stats,
    )
    return vector, coef


def solution(mesh):
    in_specs = (P("sec", None, None), P("op", "sec", None, None), P("op", None, None), P("op"), P())
    out_specs = (P("sec", None, None), P())
    return jax.shard_map(
        on_device, mesh=mesh, in_specs=in_specs, out_specs=out_specs, check_vma=False
    )
```

```python
import functools

import jax
import jax.numpy as jnp
from jax import lax
from jax.experimental import pallas as pl
from jax.experimental.pallas import tpu as pltpu
from jax.sharding import PartitionSpec as P

PRODUCTS = 3
F32 = jnp.float32
BF16 = jnp.bfloat16
VMEM = pl.BlockSpec(memory_space=pltpu.VMEM)
SMEM = pl.BlockSpec(memory_space=pltpu.SMEM)


class Info:
    def __init__(self, shifts_ref, rows_ref, sectors):
        self.core = lax.axis_index("op") % 2
        self.sec = lax.axis_index("sec")
        self.shift = lambda w: shifts_ref[w]
        self.rows = lambda t: rows_ref[self.sec * sectors + t]
        self.live = lambda: sum(rows_ref[i] for i in range(rows_ref.shape[0])).astype(F32)

    def part(self, which, half):
        return pl.ds(pl.multiple_of((self.core if which == 0 else 1 - self.core) * half, half), half)


def after(value, *others):
    return lax.optimization_barrier((value, *others))[0]


def call(kernel, name, out, scratch, *operands, flops=0):
    moved = sum(a.size * a.dtype.itemsize for a in operands)
    return pl.pallas_call(
        kernel,
        name=name,
        out_shape=out,
        in_specs=[SMEM, SMEM] + [VMEM] * (len(operands) - 2),
        out_specs=jax.tree.map(lambda _: VMEM, out),
        scratch_shapes=scratch,
        compiler_params=pltpu.CompilerParams(vmem_limit_bytes=24 << 20),
        cost_estimate=pl.CostEstimate(flops=flops, bytes_accessed=moved, transcendentals=0),
    )(*operands)


def lane_sums(value):
    rows, columns = value.shape
    folded = sum(value[:, i : i + 128] for i in range(0, columns, 128))
    return jnp.sum(folded, axis=0, keepdims=True)


def total(stats_ref, row, live):
    return jnp.sum(stats_ref[row : row + 1, :], axis=1, keepdims=True) / live


def write_sums(stats_ref, values):
    rows = stats_ref.shape[0]
    parts = [lane_sums(v) for v in values]
    parts += [jnp.zeros((1, 128), F32)] * (rows - len(parts))
    stats_ref[...] = jnp.concatenate(parts, axis=0)


def coefficients(stats, live):
    norm = jnp.sqrt(total(stats[0], 0, live))
    alphas, betas = [], []
    for k, ref in enumerate(stats[1:]):
        alpha = total(ref, 1, live)
        square = total(ref, 0, live) - alpha * alpha
        if k:
            square = square - 2.0 * betas[-1] * total(ref, 2, live) + betas[-1] * betas[-1]
        alphas.append(alpha)
        betas.append(jnp.sqrt(jnp.maximum(square, 0.0)))
    return norm, alphas, betas


def lanczos_vectors(norm, alphas, betas):
    vectors = [[1.0 / norm]]
    for k, beta in enumerate(betas):
        scale = 1.0 / beta
        one = [-alphas[k] * c for c in vectors[k]] + [1.0]
        if k:
            for i, c in enumerate(vectors[k - 1]):
                one[i] = one[i] - betas[k - 1] * c
        vectors.append([c * scale for c in one])
    return vectors


def combine(coefs, blocks):
    return sum(c * block for c, block in zip(coefs, blocks))


def start_kernel(shifts_ref, rows_ref, x_ref, *refs):
    *halves, stats_ref = refs
    sectors, block_rows, _ = x_ref.shape
    half = block_rows // 2
    info = Info(shifts_ref, rows_ref, sectors)
    square = 0.0
    for t in range(sectors):
        for which in range(2):
            part = info.part(which, half)
            value = x_ref[t, part, :]
            rows = lax.broadcasted_iota(jnp.int32, value.shape, 0) + part.start
            value = jnp.where(rows < info.rows(t), value, jnp.zeros_like(value))
            halves[2 * t + which][...] = value
            if which == 0:
                wide = value.astype(F32)
                square = square + wide * wide
    write_sums(stats_ref, [square])


def select_source(info, block, refs, v_ref):
    half = refs[0].shape[0]
    even = info.sec % 2 == 0
    mine, other = info.part(0, half), info.part(1, half)
    from_pair = (block == 1) == even
    for k, here in enumerate(
        (block == 0, (block != 0) & from_pair, (block != 0) & jnp.logical_not(from_pair))
    ):

        @pl.when(here)
        def _():
            v_ref[mine, :] = refs[2 * k][...]
            v_ref[other, :] = refs[2 * k + 1][...]


def apply_term(info, w, target, refs, left_ref, right_ref, v_ref, acc_ref):
    select_source(info, (target - info.shift(w)) >> 1, refs, v_ref)
    part = jnp.dot(v_ref[...], right_ref[w], preferred_element_type=F32).astype(BF16)
    acc_ref[...] += jnp.dot(left_ref[w, target], part, preferred_element_type=F32)


def first_kernel(shifts_ref, rows_ref, *refs):
    *sources, left_ref, right_ref, acc_ref, v_ref = refs
    info = Info(shifts_ref, rows_ref, left_ref.shape[1])
    acc_ref[...] = jnp.zeros_like(acc_ref)

    def step(w, carry):
        target = info.shift(w) & 1
        apply_term(info, w, target, sources, left_ref, right_ref, v_ref, acc_ref.at[target])
        return carry

    lax.fori_loop(0, left_ref.shape[0], step, 0)


def second_kernel(target, shifts_ref, rows_ref, *refs):
    *sources, left_ref, right_ref, sum_ref, mine_ref, other_ref, v_ref, acc_ref = refs
    half = mine_ref.shape[0]
    info = Info(shifts_ref, rows_ref, left_ref.shape[1])
    acc_ref[...] = sum_ref[target]

    def step(w, carry):
        @pl.when(((info.shift(w) + 1) & 1) == target)
        def _():
            apply_term(info, w, target, sources, left_ref, right_ref, v_ref, acc_ref)

        return carry

    lax.fori_loop(0, left_ref.shape[0], step, 0)
    mine_ref[...] = acc_ref[info.part(0, half), :].astype(BF16)
    other_ref[...] = acc_ref[info.part(1, half), :].astype(BF16)


def add_kernel(shifts_ref, rows_ref, a_ref, b_ref, out_ref):
    out_ref[...] = (a_ref[...].astype(F32) + b_ref[...].astype(F32)).astype(BF16)


def image_kernel(product, target, sectors, shifts_ref, rows_ref, *refs):
    a_ref, b_ref = refs[:2]
    basis = [r[...].astype(F32) for r in refs[2 : 3 + product]]
    stats = refs[3 + product : 4 + 2 * product]
    out_ref, stats_ref = refs[4 + 2 * product :]
    half, columns = out_ref.shape
    info = Info(shifts_ref, rows_ref, sectors)
    live = info.live() * columns
    norm, alphas, betas = coefficients(stats, live)
    vectors = [combine(c, basis) for c in lanczos_vectors(norm, alphas, betas)[-2:]]
    value = a_ref[...].astype(F32) + b_ref[...].astype(F32)
    if product == 0:
        value = value * (1.0 / norm)
    else:
        value = value - alphas[-1] * basis[-1]
        if product > 1:
            value = value - betas[-2] * basis[-2]
        value = value * (1.0 / betas[-1])
    rows = lax.broadcasted_iota(jnp.int32, value.shape, 0) + info.core * half
    value = jnp.where(rows < info.rows(target), value, 0.0).astype(BF16)
    out_ref[...] = value
    value = value.astype(F32)
    write_sums(stats_ref, [value * value] + [value * v for v in vectors[::-1]])


def last_kernel(products, shifts_ref, rows_ref, *refs):
    per_sector = 2 * (products + 1)
    stats = refs[-3 - products : -2]
    out_ref, coef_ref = refs[-2:]
    sectors, block_rows, columns = out_ref.shape
    half = block_rows // 2
    info = Info(shifts_ref, rows_ref, sectors)
    norm, alphas, betas = coefficients(stats, info.live() * columns)
    coefs = lanczos_vectors(norm, alphas, betas)[-1]
    for t in range(sectors):
        for which in range(2):
            basis = [
                refs[t * per_sector + 2 * k + which][...].astype(F32) for k in range(products + 1)
            ]
            out_ref[t, info.part(which, half), :] = combine(coefs, basis).astype(BF16)
    row = lax.broadcasted_iota(jnp.int32, coef_ref.shape, 0)
    column = lax.broadcasted_iota(jnp.int32, coef_ref.shape, 1)
    value = jnp.zeros(coef_ref.shape, F32)
    for k in range(products):
        value = jnp.where((row == 0) & (column == k), alphas[k], value)
        value = jnp.where((row == 1) & (column == k), betas[k], value)
    coef_ref[...] = value


def on_device(wavefunction, left_blocks, right_blocks, charge_shifts, sector_rows):
    sectors, block_rows, columns = wavefunction.shape
    half = block_rows // 2
    n_sec, n_op = lax.axis_size("sec"), lax.axis_size("op")
    assert sectors == 2 and n_sec % 2 == 0 and n_op % 2 == 0
    core_pairs = [(i, i ^ 1) for i in range(n_op)]
    pairs = [(i, i ^ 1) for i in range(n_sec)]
    onward = [(i, i + 2) for i in range(0, n_sec - 2, 2)]
    onward += [(i, i - 2) for i in range(3, n_sec, 2)]

    def across_cores(value):
        return lax.ppermute(value, "op", core_pairs)

    def sum_steps(stats):
        stats = stats + across_cores(stats)
        bit = 1
        while bit < n_sec:
            stats = stats + lax.ppermute(stats, "sec", [(i, i ^ bit) for i in range(n_sec)])
            yield stats
            bit *= 2

    place = (charge_shifts, sector_rows)
    half_type = jax.ShapeDtypeStruct((half, columns), BF16)
    stats_type = jax.ShapeDtypeStruct((8, 128), F32)
    acc_type = jax.ShapeDtypeStruct((sectors, block_rows, columns), F32)
    v_scratch = pltpu.VMEM((block_rows, columns), BF16)
    acc_scratch = pltpu.VMEM((block_rows, columns), F32)

    *halves, start_stats = call(
        start_kernel, "start", [half_type] * (2 * sectors) + [stats_type], [], *place, wavefunction
    )
    basis = [[(halves[0], halves[1]), (halves[2], halves[3])]]
    stats = []
    sums = start_stats
    pair_flops = 4 * block_rows * block_rows * columns
    terms = left_blocks.shape[0]

    for product in range(PRODUCTS):
        steps = list(sum_steps(sums))
        stats.append(steps[-1])
        (mine_0, other_0), (mine_1, other_1) = basis[-1]
        pair_0 = lax.ppermute(mine_0, "sec", pairs)
        pair_1 = lax.ppermute(mine_1, "sec", pairs)
        pair_0 = after(pair_0, steps[0])
        far_0 = lax.ppermute(pair_0, "sec", onward)
        if len(steps) > 1:
            pair_1 = after(pair_1, steps[1])
        far_1 = lax.ppermute(pair_1, "sec", onward)
        acc = call(
            first_kernel, "first", acc_type, [v_scratch], *place,
            mine_0, other_0, pair_0, across_cores(pair_0), far_0, across_cores(far_0),
            left_blocks, right_blocks, flops=terms * pair_flops,
        )
        far_1 = after(far_1, acc)
        sources = (mine_1, other_1, pair_1, across_cores(pair_1), far_1, across_cores(far_1))
        image = []
        sums = []
        for t in range(sectors):
            mine, other = call(
                functools.partial(second_kernel, t), "second", [half_type] * 2,
                [v_scratch, acc_scratch], *place,
                *sources, left_blocks, right_blocks, acc, flops=terms * pair_flops // 2,
            )
            value = call(add_kernel, "add", half_type, [], *place, mine, across_cores(other))
            bit = 2
            while 2 * bit < n_op:
                arrived = lax.ppermute(value, "op", [(i, i ^ bit) for i in range(n_op)])
                value = call(add_kernel, "add", half_type, [], *place, value, arrived)
                bit *= 2
            arrived = lax.ppermute(value, "op", [(i, i ^ bit) for i in range(n_op)])
            mine, part = call(
                functools.partial(image_kernel, product, t, sectors), "image",
                [half_type, stats_type], [], *place,
                value, arrived, *[b[t][0] for b in basis], *stats,
            )
            image.append((mine, across_cores(mine)))
            sums.append(part)
        basis.append(image)
        sums = sums[0] + sums[1]
    stats.append(list(sum_steps(sums))[-1])

    flat = [h for t in range(sectors) for b in basis for h in b[t]]
    vector_type = jax.ShapeDtypeStruct(wavefunction.shape, BF16)
    coef_type = jax.ShapeDtypeStruct((2, PRODUCTS), F32)
    vector, coef = call(
        functools.partial(last_kernel, PRODUCTS), "last", [vector_type, coef_type], [],
        *place, *flat, *stats,
    )
    return vector, coef


def solution(mesh):
    in_specs = (P("sec", None, None), P("op", "sec", None, None), P("op", None, None), P("op"), P())
    out_specs = (P("sec", None, None), P())
    return jax.shard_map(
        on_device, mesh=mesh, in_specs=in_specs, out_specs=out_specs, check_vma=False
    )
```

```python
import functools

import jax
import jax.numpy as jnp
from jax import lax
from jax.experimental import pallas as pl
from jax.experimental.pallas import tpu as pltpu
from jax.sharding import PartitionSpec as P

F32 = jnp.float32
BF16 = jnp.bfloat16
VMEM = pl.BlockSpec(memory_space=pltpu.VMEM)
SMEM = pl.BlockSpec(memory_space=pltpu.SMEM)


def call(kernel, name, out, scratch, *operands, flops=0):
    moved = sum(a.size * a.dtype.itemsize for a in operands)
    return pl.pallas_call(
        kernel,
        name=name,
        out_shape=out,
        in_specs=[SMEM if a.dtype == jnp.int32 else VMEM for a in operands],
        out_specs=jax.tree.map(lambda _: VMEM, out),
        scratch_shapes=scratch,
        compiler_params=pltpu.CompilerParams(vmem_limit_bytes=24 << 20),
        cost_estimate=pl.CostEstimate(flops=flops, bytes_accessed=moved, transcendentals=0),
    )(*operands)


def after(value, *others):
    return lax.optimization_barrier((value, *others))[0]


def my_core():
    return lax.axis_index("op") % 2


def half_of(which, half):
    core = my_core()
    return pl.ds(pl.multiple_of((core if which == 0 else 1 - core) * half, half), half)


def rows_of(rows_ref, target, sectors):
    return rows_ref[lax.axis_index("sec") * sectors + target]


def live_entries(rows_ref, columns):
    return sum(rows_ref[i] for i in range(rows_ref.shape[0])).astype(F32) * columns


def masked(value, rows):
    return jnp.where(lax.broadcasted_iota(jnp.int32, value.shape, 0) < rows, value, 0.0)


def inner(stats_ref, row, live):
    return jnp.sum(stats_ref[row : row + 1, :], axis=1, keepdims=True) / live


def write_sums(stats_ref, values, first=0):
    parts = [jnp.zeros((1, 128), F32)] * stats_ref.shape[0]
    for k, value in enumerate(values):
        folded = sum(value[:, i : i + 128] for i in range(0, value.shape[1], 128))
        parts[first + k] = jnp.sum(folded, axis=0, keepdims=True)
    stats_ref[...] = jnp.concatenate(parts, axis=0)


def first_scalars(start_stats, image_stats, live):
    norm = jnp.sqrt(inner(start_stats, 0, live))
    alpha = inner(image_stats, 1, live)
    beta = jnp.sqrt(jnp.maximum(inner(image_stats, 0, live) - alpha * alpha, 0.0))
    return norm, alpha, beta


def form(gram, a, b):
    return sum(a[i] * b[j] * gram[min(i, j)][max(i, j)] for i in a for j in b)


def plus(scale, *terms):
    out = {}
    for c, vector in terms:
        for i, v in vector.items():
            out[i] = out[i] + c * v if i in out else c * v
    return {i: scale * v for i, v in out.items()}


def start_kernel(rows_ref, x_ref, *refs):
    *halves, stats_ref = refs
    sectors, _, columns = x_ref.shape
    square = 0.0
    for t in range(sectors):
        for which in range(2):
            value = x_ref[t, :, half_of(which, columns // 2)].astype(F32)
            value = masked(value, rows_of(rows_ref, t, sectors))
            halves[2 * t + which][...] = value.astype(BF16)
            if which == 0:
                square = square + value * value
    write_sums(stats_ref, [square])


def gather_sources(refs, v_ref):
    half = refs[0].shape[1]
    even = lax.axis_index("sec") % 2 == 0
    pair = jnp.where(even, 2, 0)
    for k, place in enumerate((1, pair, 2 - pair)):
        for which in range(2):
            v_ref[place, :, half_of(which, half)] = refs[2 * k + which][...]


def apply_term(shift, target, left, right, v_ref, acc_ref):
    half = acc_ref.shape[1]
    part = jnp.dot(
        v_ref[((target - shift) >> 1) + 1],
        right[:, half_of(0, half)],
        preferred_element_type=F32,
    ).astype(BF16)
    acc_ref[...] += jnp.dot(left[target], part, preferred_element_type=F32)


def first_kernel(*refs):
    shifts, blocks, sources = refs[:2], refs[2:6], refs[6:12]
    acc_ref, v_ref = refs[12:]
    gather_sources(sources, v_ref)
    acc_ref[...] = jnp.zeros_like(acc_ref)
    for shift_ref, left_ref, right_ref in zip(shifts, blocks[:2], blocks[2:]):

        def step(w, carry):
            shift = shift_ref[w]
            target = shift & 1
            apply_term(
                shift, target, left_ref.at[w], right_ref.at[w], v_ref, acc_ref.at[target]
            )
            return carry

        lax.fori_loop(0, left_ref.shape[0], step, 0)


def second_kernel(target, *refs):
    shifts, blocks, sources = refs[:2], refs[2:6], refs[6:12]
    sum_ref, out_ref, v_ref, acc_ref = refs[12:]
    gather_sources(sources, v_ref)
    acc_ref[...] = sum_ref[target]
    for shift_ref, left_ref, right_ref in zip(shifts, blocks[:2], blocks[2:]):

        def step(w, carry):
            shift = shift_ref[w]

            @pl.when(((shift + 1) & 1) == target)
            def _():
                apply_term(shift, target, left_ref.at[w], right_ref.at[w], v_ref, acc_ref)

            return carry

        lax.fori_loop(0, left_ref.shape[0], step, 0)
    out_ref[...] = acc_ref[...].astype(BF16)


def add_kernel(a_ref, b_ref, out_ref):
    out_ref[...] = (a_ref[...].astype(F32) + b_ref[...].astype(F32)).astype(BF16)


def image_kernel(product, target, sectors, rows_ref, a_ref, b_ref, *refs):
    basis = [r[...].astype(F32) for r in refs[: product + 1]]
    *stats, out_ref, stats_ref = refs[product + 1 :]
    live = live_entries(rows_ref, 2 * out_ref.shape[1])
    value = a_ref[...].astype(F32) + b_ref[...].astype(F32)
    if product == 0:
        scale = 1.0 / jnp.sqrt(inner(stats[0], 0, live))
        value = value * scale
        others = [basis[0] * scale]
    else:
        norm, alpha, beta = first_scalars(*stats, live)
        zeroth = basis[0] * (1.0 / norm)
        scale = 1.0 / beta
        first = (basis[1] - alpha * zeroth) * scale
        if product == 1:
            value = value - alpha * basis[1]
            others = [first, zeroth]
        else:
            others = [basis[2], first, zeroth]
        value = value * scale
    value = masked(value, rows_of(rows_ref, target, sectors)).astype(BF16)
    out_ref[...] = value
    value = value.astype(F32)
    write_sums(stats_ref, [value * v for v in [value] + others], 3 if product == 2 else 0)


def last_kernel(rows_ref, *refs):
    out_ref, coef_ref = refs[-2:]
    start_stats, image_stats, last_stats = refs[-5:-2]
    sectors, _, columns = out_ref.shape
    live = live_entries(rows_ref, columns)
    norm, alpha0, beta0 = first_scalars(start_stats, image_stats, live)
    one, none = jnp.ones_like(norm), jnp.zeros_like(norm)
    w11, w1q1, w1q0, zz, zw1, zq1, zq0 = (inner(last_stats, k, live) for k in range(7))
    gram = [[one, none, w1q0, zq0], [None, one, w1q1, zq1], [None, None, w11, zw1], [None] * 3 + [zz]]
    q0, q1, w1 = {0: one}, {1: one}, {2: one}
    alpha1 = w1q1
    r1 = plus(one, (one, w1), (-alpha1, q1), (-beta0, q0))
    beta1 = jnp.sqrt(jnp.maximum(form(gram, r1, r1), 0.0))
    q2 = plus(1.0 / beta1, (one, r1))
    w0 = {0: alpha0, 1: beta0}
    w2 = plus(1.0 / beta1, (beta0, {3: one}), (-alpha1, w1), (-beta0, w0))
    alpha2 = form(gram, q2, w2)
    r2 = plus(one, (one, w2), (-alpha2, q2), (-beta1, q1))
    beta2 = jnp.sqrt(jnp.maximum(form(gram, r2, r2), 0.0))
    q3 = plus(1.0 / beta2, (one, r2))
    c1 = q3[1] / beta0
    coefs = [(q3[0] - alpha0 * c1) / norm, c1, q3[2], q3[3]]
    for t in range(sectors):
        for which in range(2):
            blocks = [refs[8 * t + 2 * k + which][...].astype(F32) for k in range(4)]
            vector = sum(c * block for c, block in zip(coefs, blocks))
            out_ref[t, :, half_of(which, columns // 2)] = vector.astype(BF16)
    row = lax.broadcasted_iota(jnp.int32, coef_ref.shape, 0)
    column = lax.broadcasted_iota(jnp.int32, coef_ref.shape, 1)
    value = jnp.zeros(coef_ref.shape, F32)
    for k, (alpha, beta) in enumerate(((alpha0, beta0), (alpha1, beta1), (alpha2, beta2))):
        value = jnp.where((row == 0) & (column == k), alpha, value)
        value = jnp.where((row == 1) & (column == k), beta, value)
    coef_ref[...] = value


def on_device(wavefunction, left_blocks, right_blocks, charge_shifts, sector_rows):
    sectors, block_rows, columns = wavefunction.shape
    half = columns // 2
    n_sec, n_op = lax.axis_size("sec"), lax.axis_size("op")
    assert sectors == 2 and n_sec % 2 == 0 and n_op % 4 == 0
    core_pairs = [(i, i ^ 1) for i in range(n_op)]
    pairs = [(i, i ^ 1) for i in range(n_sec)]
    onward = [(i, i + 2) for i in range(0, n_sec - 2, 2)]
    onward += [(i, i - 2) for i in range(3, n_sec, 2)]

    def across_cores(value):
        return lax.ppermute(value, "op", core_pairs)

    def sum_steps(stats):
        stats = stats + across_cores(stats)
        steps = []
        bit = 1
        while bit < n_sec:
            flips = [bit] if bit == 1 or 2 * bit >= n_sec else [bit, 2 * bit, 3 * bit]
            arrived = [
                lax.ppermute(stats, "sec", [(i, i ^ f) for i in range(n_sec)]) for f in flips
            ]
            if len(arrived) == 1:
                stats = stats + arrived[0]
            else:
                stats = (stats + arrived[0]) + (arrived[1] + arrived[2])
            steps.append(stats)
            bit <<= len(flips) - len(flips) // 2
        return steps

    half_type = jax.ShapeDtypeStruct((block_rows, half), BF16)
    stats_type = jax.ShapeDtypeStruct((8, 128), F32)
    acc_type = jax.ShapeDtypeStruct((sectors, block_rows, half), F32)
    v_scratch = pltpu.VMEM((3, block_rows, columns), BF16)
    acc_scratch = pltpu.VMEM((block_rows, half), F32)

    *halves, sums = call(
        start_kernel, "start", [half_type] * (2 * sectors) + [stats_type], [],
        sector_rows, wavefunction,
    )
    basis = [[(halves[0], halves[1]), (halves[2], halves[3])]]
    operators = (
        charge_shifts, across_cores(charge_shifts),
        left_blocks, across_cores(left_blocks), right_blocks, across_cores(right_blocks),
    )
    stats = []
    pair_flops = 2 * block_rows * half * (block_rows + columns)
    terms = 2 * left_blocks.shape[0]

    for product in range(3):
        (mine_0, other_0), (mine_1, other_1) = basis[-1]
        pair_0 = lax.ppermute(mine_0, "sec", pairs)
        pair_1 = lax.ppermute(mine_1, "sec", pairs)
        far_0 = lax.ppermute(pair_0, "sec", onward)
        far_1 = lax.ppermute(pair_1, "sec", onward)
        if product < 2:
            steps = sum_steps(sums)
            far_0 = after(far_0, steps[0])
            stats.append(steps[-1])
        acc = call(
            first_kernel, "first", acc_type, [v_scratch], *operators,
            mine_0, other_0, pair_0, across_cores(pair_0), far_0, across_cores(far_0),
            flops=terms * pair_flops,
        )
        far_1 = after(far_1, acc)
        sources = (mine_1, other_1, pair_1, across_cores(pair_1), far_1, across_cores(far_1))
        image = []
        parts = []
        for t in range(sectors):
            value = call(
                functools.partial(second_kernel, t), "second", half_type,
                [v_scratch, acc_scratch], *operators, *sources, acc,
                flops=terms * pair_flops // 2,
            )
            bit = 2
            while 2 * bit < n_op:
                arrived = lax.ppermute(value, "op", [(i, i ^ bit) for i in range(n_op)])
                value = call(add_kernel, "add", half_type, [], value, arrived)
                bit *= 2
            arrived = lax.ppermute(value, "op", [(i, i ^ bit) for i in range(n_op)])
            mine, part = call(
                functools.partial(image_kernel, product, t, sectors), "image",
                [half_type, stats_type], [], sector_rows,
                value, arrived, *[b[t][0] for b in basis], *stats,
            )
            image.append((mine, across_cores(mine)))
            parts.append(part)
        basis.append(image)
        if product < 2:
            sums = parts[0] + parts[1]
        else:
            sums = sums + (parts[0] + parts[1])
    stats.append(sum_steps(sums)[-1])

    flat = [h for t in range(sectors) for b in basis for h in b[t]]
    vector_type = jax.ShapeDtypeStruct(wavefunction.shape, BF16)
    coef_type = jax.ShapeDtypeStruct((2, 3), F32)
    vector, coef = call(
        last_kernel, "last", [vector_type, coef_type], [], sector_rows, *flat, *stats
    )
    return vector, coef


def solution(mesh):
    in_specs = (P("sec", None, None), P("op", "sec", None, None), P("op", None, None), P("op"), P())
    out_specs = (P("sec", None, None), P())
    return jax.shard_map(
        on_device, mesh=mesh, in_specs=in_specs, out_specs=out_specs, check_vma=False
    )
```

```python
import functools

import jax
import jax.numpy as jnp
from jax import lax
from jax.experimental import pallas as pl
from jax.experimental.pallas import tpu as pltpu
from jax.sharding import PartitionSpec as P

F32 = jnp.float32
BF16 = jnp.bfloat16
VMEM = pl.BlockSpec(memory_space=pltpu.VMEM)
SMEM = pl.BlockSpec(memory_space=pltpu.SMEM)


def call(kernel, name, out, scratch, *operands, flops=0):
    moved = sum(a.size * a.dtype.itemsize for a in operands)
    return pl.pallas_call(
        kernel,
        name=name,
        out_shape=out,
        in_specs=[SMEM if a.dtype == jnp.int32 else VMEM for a in operands],
        out_specs=jax.tree.map(lambda _: VMEM, out),
        scratch_shapes=scratch,
        compiler_params=pltpu.CompilerParams(vmem_limit_bytes=24 << 20),
        cost_estimate=pl.CostEstimate(flops=flops, bytes_accessed=moved, transcendentals=0),
    )(*operands)


def after(value, *others):
    return lax.optimization_barrier((value, *others))[0]


def my_core():
    return lax.axis_index("op") % 2


def half_of(which, half):
    core = my_core()
    return pl.ds(pl.multiple_of((core if which == 0 else 1 - core) * half, half), half)


def rows_of(rows_ref, target, sectors):
    return rows_ref[lax.axis_index("sec") * sectors + target]


def live_entries(rows_ref, columns):
    return sum(rows_ref[i] for i in range(rows_ref.shape[0])).astype(F32) * columns


def masked(value, first, rows):
    return jnp.where(lax.broadcasted_iota(jnp.int32, value.shape, 0) + first < rows, value, 0.0)


def inner(stats_ref, row, live):
    return jnp.sum(stats_ref[row : row + 1, :], axis=1, keepdims=True) / live


def write_sums(stats_ref, values, first=0):
    parts = [jnp.zeros((1, 128), F32)] * stats_ref.shape[0]
    for k, value in enumerate(values):
        folded = sum(value[:, i : i + 128] for i in range(0, value.shape[1], 128))
        parts[first + k] = jnp.sum(folded, axis=0, keepdims=True)
    stats_ref[...] = jnp.concatenate(parts, axis=0)


def first_scalars(start_stats, image_stats, live):
    norm = jnp.sqrt(inner(start_stats, 0, live))
    alpha = inner(image_stats, 1, live)
    beta = jnp.sqrt(jnp.maximum(inner(image_stats, 0, live) - alpha * alpha, 0.0))
    return norm, alpha, beta


def form(gram, a, b):
    return sum(a[i] * b[j] * gram[min(i, j)][max(i, j)] for i in a for j in b)


def plus(scale, *terms):
    out = {}
    for c, vector in terms:
        for i, v in vector.items():
            out[i] = out[i] + c * v if i in out else c * v
    return {i: scale * v for i, v in out.items()}


def start_kernel(rows_ref, x_ref, *refs):
    *halves, stats_ref = refs
    sectors, block_rows, _ = x_ref.shape
    square = 0.0
    for t in range(sectors):
        for which in range(2):
            part = half_of(which, block_rows // 2)
            value = x_ref[t, part, :].astype(F32)
            value = masked(value, part.start, rows_of(rows_ref, t, sectors))
            halves[2 * t + which][...] = value.astype(BF16)
            if which == 0:
                square = square + value * value
    write_sums(stats_ref, [square])


def split_kernel(left_ref, keep_ref, give_ref):
    half = keep_ref.shape[2]
    for w in range(left_ref.shape[0]):
        for t in range(left_ref.shape[1]):
            keep_ref[w, t] = left_ref[w, t, half_of(0, half), :]
            give_ref[w, t] = left_ref[w, t, half_of(1, half), :]


def gather_sources(refs, v_ref):
    half = refs[0].shape[0]
    even = lax.axis_index("sec") % 2 == 0
    pair = jnp.where(even, 2, 0)
    for k, place in enumerate((1, pair, 2 - pair)):
        for which in range(2):
            v_ref[place, half_of(which, half), :] = refs[2 * k + which][...]


def add_terms(parity, target, shifts_ref, left_ref, right_ref, v_ref, list_ref, acc_ref):
    count = jnp.int32(0)
    for w in range(shifts_ref.shape[0]):
        here = ((shifts_ref[w] + parity) & 1) == target

        @pl.when(here)
        def _():
            list_ref[count] = w

        count = count + here.astype(jnp.int32)

    def product(position):
        w = list_ref[position]
        source = v_ref[((target - shifts_ref[w]) >> 1) + 1]
        part = jnp.dot(left_ref[w, target], source, preferred_element_type=F32).astype(BF16)
        return jnp.dot(part, right_ref[w], preferred_element_type=F32)

    def two(k, carry):
        acc_ref[...] += product(2 * k) + product(2 * k + 1)
        return carry

    lax.fori_loop(0, count >> 1, two, 0)

    @pl.when(count & 1 == 1)
    def _():
        acc_ref[...] += product(count - 1)


def first_kernel(shifts_ref, left_ref, right_ref, *refs):
    *sources, acc_ref, v_ref, list_ref = refs
    gather_sources(sources, v_ref)
    for target in range(acc_ref.shape[0]):
        acc_ref[target] = jnp.zeros(acc_ref.shape[1:], F32)
        add_terms(
            0, target, shifts_ref, left_ref, right_ref, v_ref, list_ref, acc_ref.at[target]
        )


def second_kernel(target, shifts_ref, left_ref, right_ref, *refs):
    *sources, sum_ref, out_ref, v_ref, list_ref, acc_ref = refs
    gather_sources(sources, v_ref)
    acc_ref[...] = sum_ref[target]
    add_terms(1, target, shifts_ref, left_ref, right_ref, v_ref, list_ref, acc_ref)
    out_ref[...] = acc_ref[...].astype(BF16)


def add_kernel(a_ref, b_ref, out_ref):
    out_ref[...] = (a_ref[...].astype(F32) + b_ref[...].astype(F32)).astype(BF16)


def image_kernel(product, target, sectors, rows_ref, a_ref, b_ref, *refs):
    basis = [r[...].astype(F32) for r in refs[: product + 1]]
    *stats, out_ref, stats_ref = refs[product + 1 :]
    half, columns = out_ref.shape
    live = live_entries(rows_ref, columns)
    value = a_ref[...].astype(F32) + b_ref[...].astype(F32)
    if product == 0:
        scale = 1.0 / jnp.sqrt(inner(stats[0], 0, live))
        value = value * scale
        others = [basis[0] * scale]
    else:
        norm, alpha, beta = first_scalars(*stats, live)
        zeroth = basis[0] * (1.0 / norm)
        scale = 1.0 / beta
        first = (basis[1] - alpha * zeroth) * scale
        if product == 1:
            value = value - alpha * basis[1]
            others = [first, zeroth]
        else:
            others = [basis[2], first, zeroth]
        value = value * scale
    value = masked(value, my_core() * half, rows_of(rows_ref, target, sectors)).astype(BF16)
    out_ref[...] = value
    value = value.astype(F32)
    write_sums(stats_ref, [value * v for v in [value] + others], 3 if product == 2 else 0)


def last_kernel(rows_ref, *refs):
    out_ref, coef_ref = refs[-2:]
    start_stats, image_stats, last_stats = refs[-5:-2]
    sectors, block_rows, columns = out_ref.shape
    live = live_entries(rows_ref, columns)
    norm, alpha0, beta0 = first_scalars(start_stats, image_stats, live)
    one, none = jnp.ones_like(norm), jnp.zeros_like(norm)
    w11, w1q1, w1q0, zz, zw1, zq1, zq0 = (inner(last_stats, k, live) for k in range(7))
    gram = [[one, none, w1q0, zq0], [None, one, w1q1, zq1], [None, None, w11, zw1], [None] * 3 + [zz]]
    q0, q1, w1 = {0: one}, {1: one}, {2: one}
    alpha1 = w1q1
    r1 = plus(one, (one, w1), (-alpha1, q1), (-beta0, q0))
    beta1 = jnp.sqrt(jnp.maximum(form(gram, r1, r1), 0.0))
    q2 = plus(1.0 / beta1, (one, r1))
    w0 = {0: alpha0, 1: beta0}
    w2 = plus(1.0 / beta1, (beta0, {3: one}), (-alpha1, w1), (-beta0, w0))
    alpha2 = form(gram, q2, w2)
    r2 = plus(one, (one, w2), (-alpha2, q2), (-beta1, q1))
    beta2 = jnp.sqrt(jnp.maximum(form(gram, r2, r2), 0.0))
    q3 = plus(1.0 / beta2, (one, r2))
    c1 = q3[1] / beta0
    coefs = [(q3[0] - alpha0 * c1) / norm, c1, q3[2], q3[3]]
    for t in range(sectors):
        for which in range(2):
            blocks = [refs[8 * t + 2 * k + which][...].astype(F32) for k in range(4)]
            vector = sum(c * block for c, block in zip(coefs, blocks))
            out_ref[t, half_of(which, block_rows // 2), :] = vector.astype(BF16)
    row = lax.broadcasted_iota(jnp.int32, coef_ref.shape, 0)
    column = lax.broadcasted_iota(jnp.int32, coef_ref.shape, 1)
    value = jnp.zeros(coef_ref.shape, F32)
    for k, (alpha, beta) in enumerate(((alpha0, beta0), (alpha1, beta1), (alpha2, beta2))):
        value = jnp.where((row == 0) & (column == k), alpha, value)
        value = jnp.where((row == 1) & (column == k), beta, value)
    coef_ref[...] = value


def on_device(wavefunction, left_blocks, right_blocks, charge_shifts, sector_rows):
    sectors, block_rows, columns = wavefunction.shape
    half = block_rows // 2
    n_sec, n_op = lax.axis_size("sec"), lax.axis_size("op")
    assert sectors == 2 and n_sec % 2 == 0 and n_op % 4 == 0
    core_pairs = [(i, i ^ 1) for i in range(n_op)]
    pairs = [(i, i ^ 1) for i in range(n_sec)]
    onward = [(i, i + 2) for i in range(0, n_sec - 2, 2)]
    onward += [(i, i - 2) for i in range(3, n_sec, 2)]

    def across_cores(value):
        return lax.ppermute(value, "op", core_pairs)

    def sum_steps(stats):
        stats = stats + across_cores(stats)
        steps = []
        bit = 1
        while bit < n_sec:
            flips = [bit] if bit == 1 or 2 * bit >= n_sec else [bit, 2 * bit, 3 * bit]
            arrived = [
                lax.ppermute(stats, "sec", [(i, i ^ f) for i in range(n_sec)]) for f in flips
            ]
            if len(arrived) == 1:
                stats = stats + arrived[0]
            else:
                stats = (stats + arrived[0]) + (arrived[1] + arrived[2])
            steps.append(stats)
            bit <<= len(flips) - len(flips) // 2
        return steps

    half_type = jax.ShapeDtypeStruct((half, columns), BF16)
    stats_type = jax.ShapeDtypeStruct((8, 128), F32)
    acc_type = jax.ShapeDtypeStruct((sectors, half, columns), F32)
    terms = 2 * left_blocks.shape[0]
    term_scratch = [pltpu.VMEM((3, block_rows, columns), BF16), pltpu.SMEM((terms,), jnp.int32)]
    acc_scratch = pltpu.VMEM((half, columns), F32)

    *halves, sums = call(
        start_kernel, "start", [half_type] * (2 * sectors) + [stats_type], [],
        sector_rows, wavefunction,
    )
    basis = [[(halves[0], halves[1]), (halves[2], halves[3])]]
    half_left = jax.ShapeDtypeStruct((terms // 2, sectors, half, block_rows), BF16)
    keep, give = call(split_kernel, "split", [half_left] * 2, [], left_blocks)
    operators = [
        jnp.concatenate([mine, other])
        for mine, other in (
            (charge_shifts, across_cores(charge_shifts)),
            (keep, across_cores(give)),
            (right_blocks, across_cores(right_blocks)),
        )
    ]
    stats = []
    pair_flops = 2 * half * columns * (block_rows + columns)

    for product in range(3):
        (mine_0, other_0), (mine_1, other_1) = basis[-1]
        pair_0 = lax.ppermute(mine_0, "sec", pairs)
        pair_1 = lax.ppermute(mine_1, "sec", pairs)
        far_0 = lax.ppermute(pair_0, "sec", onward)
        far_1 = lax.ppermute(pair_1, "sec", onward)
        if product < 2:
            steps = sum_steps(after(sums, pair_1))
            stats.append(steps[-1])
        acc = call(
            first_kernel, "first", acc_type, term_scratch, *operators,
            mine_0, other_0, pair_0, across_cores(pair_0), far_0, across_cores(far_0),
            flops=terms * pair_flops,
        )
        far_1 = after(far_1, acc, steps[0]) if product < 2 else after(far_1, acc)
        sources = (mine_1, other_1, pair_1, across_cores(pair_1), far_1, across_cores(far_1))
        image = []
        parts = []
        for t in range(sectors):
            value = call(
                functools.partial(second_kernel, t), "second", half_type,
                term_scratch + [acc_scratch], *operators, *sources, acc,
                flops=terms * pair_flops // 2,
            )
            bit = 2
            while 2 * bit < n_op:
                arrived = lax.ppermute(value, "op", [(i, i ^ bit) for i in range(n_op)])
                value = call(add_kernel, "add", half_type, [], value, arrived)
                bit *= 2
            arrived = lax.ppermute(value, "op", [(i, i ^ bit) for i in range(n_op)])
            mine, part = call(
                functools.partial(image_kernel, product, t, sectors), "image",
                [half_type, stats_type], [], sector_rows,
                value, arrived, *[b[t][0] for b in basis], *stats,
            )
            image.append((mine, across_cores(mine)))
            parts.append(part)
        basis.append(image)
        if product < 2:
            sums = parts[0] + parts[1]
        else:
            sums = sums + (parts[0] + parts[1])
    stats.append(sum_steps(sums)[-1])

    flat = [h for t in range(sectors) for b in basis for h in b[t]]
    vector_type = jax.ShapeDtypeStruct(wavefunction.shape, BF16)
    coef_type = jax.ShapeDtypeStruct((2, 3), F32)
    vector, coef = call(
        last_kernel, "last", [vector_type, coef_type], [], sector_rows, *flat, *stats
    )
    return vector, coef


def solution(mesh):
    in_specs = (P("sec", None, None), P("op", "sec", None, None), P("op", None, None), P("op"), P())
    out_specs = (P("sec", None, None), P())
    return jax.shard_map(
        on_device, mesh=mesh, in_specs=in_specs, out_specs=out_specs, check_vma=False
    )
```

```python
import functools

import jax
import jax.numpy as jnp
from jax import lax
from jax.experimental import pallas as pl
from jax.experimental.pallas import tpu as pltpu
from jax.sharding import PartitionSpec as P

F32 = jnp.float32
BF16 = jnp.bfloat16
VMEM = pl.BlockSpec(memory_space=pltpu.VMEM)
SMEM = pl.BlockSpec(memory_space=pltpu.SMEM)


def call(kernel, name, out, scratch, *operands, flops=0):
    moved = sum(a.size * a.dtype.itemsize for a in operands)
    return pl.pallas_call(
        kernel,
        name=name,
        out_shape=out,
        in_specs=[SMEM if a.dtype == jnp.int32 else VMEM for a in operands],
        out_specs=jax.tree.map(lambda _: VMEM, out),
        scratch_shapes=scratch,
        compiler_params=pltpu.CompilerParams(vmem_limit_bytes=24 << 20),
        cost_estimate=pl.CostEstimate(flops=flops, bytes_accessed=moved, transcendentals=0),
    )(*operands)


def after(value, *others):
    return lax.optimization_barrier((value, *others))[0]


def my_core():
    return lax.axis_index("op") % 2


def half_of(which, half):
    core = my_core()
    return pl.ds(pl.multiple_of((core if which == 0 else 1 - core) * half, half), half)


def rows_of(rows_ref, target, sectors):
    return rows_ref[lax.axis_index("sec") * sectors + target]


def live_entries(rows_ref, columns):
    return sum(rows_ref[i] for i in range(rows_ref.shape[0])).astype(F32) * columns


def masked(value, first, rows):
    return jnp.where(lax.broadcasted_iota(jnp.int32, value.shape, 0) + first < rows, value, 0.0)


def inner(stats_ref, row, live):
    return jnp.sum(stats_ref[row : row + 1, :], axis=1, keepdims=True) / live


def write_sums(stats_ref, values, first=0):
    parts = [jnp.zeros((1, 128), F32)] * stats_ref.shape[0]
    for k, value in enumerate(values):
        folded = sum(value[:, i : i + 128] for i in range(0, value.shape[1], 128))
        parts[first + k] = jnp.sum(folded, axis=0, keepdims=True)
    stats_ref[...] = jnp.concatenate(parts, axis=0)


def first_scalars(start_stats, image_stats, live):
    norm = jnp.sqrt(inner(start_stats, 0, live))
    alpha = inner(image_stats, 1, live)
    beta = jnp.sqrt(jnp.maximum(inner(image_stats, 0, live) - alpha * alpha, 0.0))
    return norm, alpha, beta


def form(gram, a, b):
    return sum(a[i] * b[j] * gram[min(i, j)][max(i, j)] for i in a for j in b)


def plus(scale, *terms):
    out = {}
    for c, vector in terms:
        for i, v in vector.items():
            out[i] = out[i] + c * v if i in out else c * v
    return {i: scale * v for i, v in out.items()}


def start_kernel(rows_ref, x_ref, *refs):
    *halves, stats_ref = refs
    sectors, block_rows, _ = x_ref.shape
    square = 0.0
    for t in range(sectors):
        for which in range(2):
            part = half_of(which, block_rows // 2)
            value = x_ref[t, part, :].astype(F32)
            value = masked(value, part.start, rows_of(rows_ref, t, sectors))
            halves[2 * t + which][...] = value.astype(BF16)
            if which == 0:
                square = square + value * value
    write_sums(stats_ref, [square])


def split_kernel(left_ref, keep_ref, give_ref):
    half = keep_ref.shape[2]
    for w in range(left_ref.shape[0]):
        for t in range(left_ref.shape[1]):
            keep_ref[w, t] = left_ref[w, t, half_of(0, half), :]
            give_ref[w, t] = left_ref[w, t, half_of(1, half), :]


def place_of(k):
    pair = jnp.where(lax.axis_index("sec") % 2 == 0, 2, 0)
    return (1, pair, 2 - pair)[k]


def gather_sources(kinds, refs, v_ref):
    half = refs[0].shape[0]
    for i, k in enumerate(kinds):
        for which in range(2):
            v_ref[place_of(k), half_of(which, half), :] = refs[2 * i + which][...]


def add_terms(
    parity, kinds, target, shifts_ref, left_ref, right_ref, v_ref, list_ref, acc_ref
):
    far = place_of(2)
    count = jnp.int32(0)
    for w in range(shifts_ref.shape[0]):
        here = ((shifts_ref[w] + parity) & 1) == target
        if 2 not in kinds:
            here = here & (((target - shifts_ref[w]) >> 1) + 1 != far)
        elif kinds == (2,):
            here = here & (((target - shifts_ref[w]) >> 1) + 1 == far)

        @pl.when(here)
        def _():
            list_ref[count] = w

        count = count + here.astype(jnp.int32)

    def product(position):
        w = list_ref[position]
        source = v_ref[((target - shifts_ref[w]) >> 1) + 1]
        part = jnp.dot(left_ref[w, target], source, preferred_element_type=F32).astype(BF16)
        return jnp.dot(part, right_ref[w], preferred_element_type=F32)

    def two(k, carry):
        acc_ref[...] += product(2 * k) + product(2 * k + 1)
        return carry

    lax.fori_loop(0, count >> 1, two, 0)

    @pl.when(count & 1 == 1)
    def _():
        acc_ref[...] += product(count - 1)


def first_kernel(shifts_ref, left_ref, right_ref, *refs):
    *sources, acc_ref, v_ref, list_ref = refs
    gather_sources((0, 1, 2), sources, v_ref)
    for target in range(acc_ref.shape[0]):
        acc_ref[target] = jnp.zeros(acc_ref.shape[1:], F32)
        add_terms(
            0, (0, 1, 2), target, shifts_ref, left_ref, right_ref, v_ref, list_ref,
            acc_ref.at[target],
        )


def near_kernel(shifts_ref, left_ref, right_ref, *refs):
    *sources, sum_ref, acc_ref, v_ref, list_ref = refs
    gather_sources((0, 1), sources, v_ref)
    for target in range(acc_ref.shape[0]):
        acc_ref[target] = sum_ref[target]
        add_terms(
            1, (0, 1), target, shifts_ref, left_ref, right_ref, v_ref, list_ref,
            acc_ref.at[target],
        )


def far_kernel(target, shifts_ref, left_ref, right_ref, *refs):
    *sources, sum_ref, out_ref, v_ref, list_ref, acc_ref = refs
    gather_sources((2,), sources, v_ref)
    acc_ref[...] = sum_ref[target]
    add_terms(1, (2,), target, shifts_ref, left_ref, right_ref, v_ref, list_ref, acc_ref)
    out_ref[...] = acc_ref[...].astype(BF16)


def add_kernel(a_ref, b_ref, out_ref):
    out_ref[...] = (a_ref[...].astype(F32) + b_ref[...].astype(F32)).astype(BF16)


def image_kernel(product, target, sectors, rows_ref, a_ref, b_ref, *refs):
    basis = [r[...].astype(F32) for r in refs[: product + 1]]
    *stats, out_ref, stats_ref = refs[product + 1 :]
    half, columns = out_ref.shape
    live = live_entries(rows_ref, columns)
    value = a_ref[...].astype(F32) + b_ref[...].astype(F32)
    if product == 0:
        scale = 1.0 / jnp.sqrt(inner(stats[0], 0, live))
        value = value * scale
        others = [basis[0] * scale]
    else:
        norm, alpha, beta = first_scalars(*stats, live)
        zeroth = basis[0] * (1.0 / norm)
        scale = 1.0 / beta
        first = (basis[1] - alpha * zeroth) * scale
        if product == 1:
            value = value - alpha * basis[1]
            others = [first, zeroth]
        else:
            others = [basis[2], first, zeroth]
        value = value * scale
    value = masked(value, my_core() * half, rows_of(rows_ref, target, sectors)).astype(BF16)
    out_ref[...] = value
    value = value.astype(F32)
    write_sums(stats_ref, [value * v for v in [value] + others], 3 if product == 2 else 0)


def last_kernel(rows_ref, *refs):
    out_ref, coef_ref = refs[-2:]
    start_stats, image_stats, last_stats = refs[-5:-2]
    sectors, block_rows, columns = out_ref.shape
    live = live_entries(rows_ref, columns)
    norm, alpha0, beta0 = first_scalars(start_stats, image_stats, live)
    one, none = jnp.ones_like(norm), jnp.zeros_like(norm)
    w11, w1q1, w1q0, zz, zw1, zq1, zq0 = (inner(last_stats, k, live) for k in range(7))
    gram = [[one, none, w1q0, zq0], [None, one, w1q1, zq1], [None, None, w11, zw1], [None] * 3 + [zz]]
    q0, q1, w1 = {0: one}, {1: one}, {2: one}
    alpha1 = w1q1
    r1 = plus(one, (one, w1), (-alpha1, q1), (-beta0, q0))
    beta1 = jnp.sqrt(jnp.maximum(form(gram, r1, r1), 0.0))
    q2 = plus(1.0 / beta1, (one, r1))
    w0 = {0: alpha0, 1: beta0}
    w2 = plus(1.0 / beta1, (beta0, {3: one}), (-alpha1, w1), (-beta0, w0))
    alpha2 = form(gram, q2, w2)
    r2 = plus(one, (one, w2), (-alpha2, q2), (-beta1, q1))
    beta2 = jnp.sqrt(jnp.maximum(form(gram, r2, r2), 0.0))
    q3 = plus(1.0 / beta2, (one, r2))
    c1 = q3[1] / beta0
    coefs = [(q3[0] - alpha0 * c1) / norm, c1, q3[2], q3[3]]
    for t in range(sectors):
        for which in range(2):
            blocks = [refs[8 * t + 2 * k + which][...].astype(F32) for k in range(4)]
            vector = sum(c * block for c, block in zip(coefs, blocks))
            out_ref[t, half_of(which, block_rows // 2), :] = vector.astype(BF16)
    row = lax.broadcasted_iota(jnp.int32, coef_ref.shape, 0)
    column = lax.broadcasted_iota(jnp.int32, coef_ref.shape, 1)
    value = jnp.zeros(coef_ref.shape, F32)
    for k, (alpha, beta) in enumerate(((alpha0, beta0), (alpha1, beta1), (alpha2, beta2))):
        value = jnp.where((row == 0) & (column == k), alpha, value)
        value = jnp.where((row == 1) & (column == k), beta, value)
    coef_ref[...] = value


def on_device(wavefunction, left_blocks, right_blocks, charge_shifts, sector_rows):
    sectors, block_rows, columns = wavefunction.shape
    half = block_rows // 2
    n_sec, n_op = lax.axis_size("sec"), lax.axis_size("op")
    assert sectors == 2 and n_sec % 2 == 0 and n_op % 4 == 0
    core_pairs = [(i, i ^ 1) for i in range(n_op)]
    pairs = [(i, i ^ 1) for i in range(n_sec)]
    onward = [(i, i + 2) for i in range(0, n_sec - 2, 2)]
    onward += [(i, i - 2) for i in range(3, n_sec, 2)]

    def across_cores(value):
        return lax.ppermute(value, "op", core_pairs)

    def sum_near(stats):
        stats = stats + across_cores(stats)
        return stats + lax.ppermute(stats, "sec", pairs)

    def sum_far(stats):
        bit = 2
        while bit < n_sec:
            flips = [bit] if 2 * bit >= n_sec else [bit, 2 * bit, 3 * bit]
            arrived = [
                lax.ppermute(stats, "sec", [(i, i ^ f) for i in range(n_sec)]) for f in flips
            ]
            if len(arrived) == 1:
                stats = stats + arrived[0]
            else:
                stats = (stats + arrived[0]) + (arrived[1] + arrived[2])
            bit *= len(flips) + 1
        return stats

    half_type = jax.ShapeDtypeStruct((half, columns), BF16)
    stats_type = jax.ShapeDtypeStruct((8, 128), F32)
    acc_type = jax.ShapeDtypeStruct((sectors, half, columns), F32)
    terms = 2 * left_blocks.shape[0]
    term_scratch = [pltpu.VMEM((3, block_rows, columns), BF16), pltpu.SMEM((terms,), jnp.int32)]
    acc_scratch = pltpu.VMEM((half, columns), F32)

    *halves, sums = call(
        start_kernel, "start", [half_type] * (2 * sectors) + [stats_type], [],
        sector_rows, wavefunction,
    )
    basis = [[(halves[0], halves[1]), (halves[2], halves[3])]]
    half_left = jax.ShapeDtypeStruct((terms // 2, sectors, half, block_rows), BF16)
    keep, give = call(split_kernel, "split", [half_left] * 2, [], after(left_blocks, sums))
    operators = [
        jnp.concatenate([mine, other])
        for mine, other in (
            (charge_shifts, across_cores(charge_shifts)),
            (keep, across_cores(give)),
            (right_blocks, across_cores(right_blocks)),
        )
    ]
    stats = []
    pair_flops = 2 * half * columns * (block_rows + columns)

    for product in range(3):
        (mine_0, other_0), (mine_1, other_1) = basis[-1]
        pair_0 = lax.ppermute(mine_0, "sec", pairs)
        pair_1 = lax.ppermute(after(mine_1, pair_0), "sec", pairs)
        far_0 = lax.ppermute(pair_0, "sec", onward)
        far_1 = lax.ppermute(pair_1, "sec", onward)
        if product < 2:
            near = sum_near(sums)
            far_0 = after(far_0, near)
        acc = call(
            first_kernel, "first", acc_type, term_scratch, *operators,
            mine_0, other_0, pair_0, across_cores(pair_0), far_0, across_cores(far_0),
            flops=terms * pair_flops,
        )
        acc = call(
            near_kernel, "near", acc_type, term_scratch, *operators,
            mine_1, other_1, pair_1, across_cores(pair_1), acc, flops=terms * pair_flops // 2,
        )
        far_1 = after(far_1, acc)
        sources = (far_1, across_cores(far_1))
        values = [
            call(
                functools.partial(far_kernel, t), "far", half_type,
                term_scratch + [acc_scratch], *operators, *sources, acc,
                flops=terms * pair_flops // 4,
            )
            for t in range(sectors)
        ]
        if product < 2:
            stats.append(sum_far(after(near, values[-1])))
        image = []
        parts = []
        for t, value in enumerate(values):
            bit = 2
            while 2 * bit < n_op:
                arrived = lax.ppermute(value, "op", [(i, i ^ bit) for i in range(n_op)])
                value = call(add_kernel, "add", half_type, [], value, arrived)
                bit *= 2
            arrived = lax.ppermute(value, "op", [(i, i ^ bit) for i in range(n_op)])
            mine, part = call(
                functools.partial(image_kernel, product, t, sectors), "image",
                [half_type, stats_type], [], sector_rows,
                value, arrived, *[b[t][0] for b in basis], *stats,
            )
            image.append((mine, across_cores(mine)))
            parts.append(part)
        basis.append(image)
        if product < 2:
            sums = parts[0] + parts[1]
        else:
            sums = sums + (parts[0] + parts[1])
    stats.append(sum_far(sum_near(sums)))

    flat = [h for t in range(sectors) for b in basis for h in b[t]]
    vector_type = jax.ShapeDtypeStruct(wavefunction.shape, BF16)
    coef_type = jax.ShapeDtypeStruct((2, 3), F32)
    vector, coef = call(
        last_kernel, "last", [vector_type, coef_type], [], sector_rows, *flat, *stats
    )
    return vector, coef


def solution(mesh):
    in_specs = (P("sec", None, None), P("op", "sec", None, None), P("op", None, None), P("op"), P())
    out_specs = (P("sec", None, None), P())
    return jax.shard_map(
        on_device, mesh=mesh, in_specs=in_specs, out_specs=out_specs, check_vma=False
    )
```

```python
import functools

import jax
import jax.numpy as jnp
from jax import lax
from jax.experimental import pallas as pl
from jax.experimental.pallas import tpu as pltpu
from jax.sharding import PartitionSpec as P

F32 = jnp.float32
BF16 = jnp.bfloat16
VMEM = pl.BlockSpec(memory_space=pltpu.VMEM)
SMEM = pl.BlockSpec(memory_space=pltpu.SMEM)


def call(kernel, name, out, scratch, *operands, flops=0):
    moved = sum(a.size * a.dtype.itemsize for a in operands)
    return pl.pallas_call(
        kernel,
        name=name,
        out_shape=out,
        in_specs=[SMEM if a.dtype == jnp.int32 else VMEM for a in operands],
        out_specs=jax.tree.map(lambda _: VMEM, out),
        scratch_shapes=scratch,
        compiler_params=pltpu.CompilerParams(vmem_limit_bytes=24 << 20),
        cost_estimate=pl.CostEstimate(flops=flops, bytes_accessed=moved, transcendentals=0),
    )(*operands)


def after(value, *others):
    return lax.optimization_barrier((value, *others))[0]


def my_core():
    return lax.axis_index("op") % 2


def half_of(which, half):
    core = my_core()
    return pl.ds(pl.multiple_of((core if which == 0 else 1 - core) * half, half), half)


def rows_of(rows_ref, target, sectors):
    return rows_ref[lax.axis_index("sec") * sectors + target]


def live_entries(rows_ref, columns):
    return sum(rows_ref[i] for i in range(rows_ref.shape[0])).astype(F32) * columns


def masked(value, first, rows):
    return jnp.where(lax.broadcasted_iota(jnp.int32, value.shape, 0) + first < rows, value, 0.0)


def inner(stats_ref, row, live):
    return jnp.sum(stats_ref[row : row + 1, :], axis=1, keepdims=True) / live


def write_sums(stats_ref, values, before=None):
    parts = [jnp.zeros((1, 128), F32)] * 8
    for k, value in enumerate(values):
        folded = sum(value[:, i : i + 128] for i in range(0, value.shape[1], 128))
        parts[k] = jnp.sum(folded, axis=0, keepdims=True)
    rows = jnp.concatenate(parts, axis=0)
    if stats_ref.shape[0] > 8:
        stats_ref[...] = jnp.zeros_like(stats_ref)
    stats_ref[:8] = rows if before is None else rows + before[:8]


def first_scalars(start_stats, image_stats, live):
    norm = jnp.sqrt(inner(start_stats, 0, live))
    alpha = inner(image_stats, 1, live)
    beta = jnp.sqrt(jnp.maximum(inner(image_stats, 0, live) - alpha * alpha, 0.0))
    return norm, alpha, beta


def form(gram, a, b):
    return sum(a[i] * b[j] * gram[min(i, j)][max(i, j)] for i in a for j in b)


def plus(scale, *terms):
    out = {}
    for c, vector in terms:
        for i, v in vector.items():
            out[i] = out[i] + c * v if i in out else c * v
    return {i: scale * v for i, v in out.items()}


def start_kernel(rows_ref, x_ref, *refs):
    *halves, stats_ref = refs
    sectors, block_rows, _ = x_ref.shape
    square = 0.0
    for t in range(sectors):
        for which in range(2):
            part = half_of(which, block_rows // 2)
            value = x_ref[t, part, :].astype(F32)
            value = masked(value, part.start, rows_of(rows_ref, t, sectors))
            halves[2 * t + which][...] = value.astype(BF16)
            square = square + value * value
    write_sums(stats_ref, [square])


def split_kernel(left_ref, keep_ref, give_ref):
    half = keep_ref.shape[2]
    for w in range(left_ref.shape[0]):
        for t in range(left_ref.shape[1]):
            keep_ref[w, t] = left_ref[w, t, half_of(0, half), :]
            give_ref[w, t] = left_ref[w, t, half_of(1, half), :]


def place_of(k):
    pair = jnp.where(lax.axis_index("sec") % 2 == 0, 2, 0)
    return (1, pair, 2 - pair)[k]


def gather_sources(kinds, refs, scalars, v_ref):
    half = refs[0].shape[0]
    if scalars:
        rows_ref, *stats = scalars
        scale = 1.0 / first_scalars(*stats, live_entries(rows_ref, v_ref.shape[2]))[2]
    for i, k in enumerate(kinds):
        for which in range(2):
            value = refs[2 * i + which][...]
            if scalars:
                value = (value.astype(F32) * scale).astype(BF16)
            v_ref[place_of(k), half_of(which, half), :] = value


def add_terms(
    parity, kinds, target, shifts_ref, left_ref, right_ref, v_ref, list_ref, acc_ref
):
    far = place_of(2)
    count = jnp.int32(0)
    for w in range(shifts_ref.shape[0]):
        here = ((shifts_ref[w] + parity) & 1) == target
        if 2 not in kinds:
            here = here & (((target - shifts_ref[w]) >> 1) + 1 != far)
        elif kinds == (2,):
            here = here & (((target - shifts_ref[w]) >> 1) + 1 == far)

        @pl.when(here)
        def _():
            list_ref[count] = w

        count = count + here.astype(jnp.int32)

    def product(position):
        w = list_ref[position]
        source = v_ref[((target - shifts_ref[w]) >> 1) + 1]
        part = jnp.dot(left_ref[w, target], source, preferred_element_type=F32).astype(BF16)
        return jnp.dot(part, right_ref[w], preferred_element_type=F32)

    def two(k, carry):
        acc_ref[...] += product(2 * k) + product(2 * k + 1)
        return carry

    lax.fori_loop(0, count >> 1, two, 0)

    @pl.when(count & 1 == 1)
    def _():
        acc_ref[...] += product(count - 1)


def first_kernel(shifts_ref, left_ref, right_ref, *refs):
    sources, (*scalars, acc_ref, v_ref, list_ref) = refs[:6], refs[6:]
    gather_sources((0, 1, 2), sources, scalars, v_ref)
    for target in range(acc_ref.shape[0]):
        acc_ref[target] = jnp.zeros(acc_ref.shape[1:], F32)
        add_terms(
            0, (0, 1, 2), target, shifts_ref, left_ref, right_ref, v_ref, list_ref,
            acc_ref.at[target],
        )


def near_kernel(shifts_ref, left_ref, right_ref, *refs):
    sources, sum_ref, (*scalars, acc_ref, v_ref, list_ref) = refs[:4], refs[4], refs[5:]
    gather_sources((0, 1), sources, scalars, v_ref)
    for target in range(acc_ref.shape[0]):
        acc_ref[target] = sum_ref[target]
        add_terms(
            1, (0, 1), target, shifts_ref, left_ref, right_ref, v_ref, list_ref,
            acc_ref.at[target],
        )


def far_kernel(target, shifts_ref, left_ref, right_ref, *refs):
    sources, sum_ref, (*scalars, out_ref, v_ref, list_ref, acc_ref) = refs[:2], refs[2], refs[3:]
    gather_sources((2,), sources, scalars, v_ref)
    acc_ref[...] = sum_ref[target]
    add_terms(1, (2,), target, shifts_ref, left_ref, right_ref, v_ref, list_ref, acc_ref)
    out_ref[...] = acc_ref[...].astype(BF16)


def add_kernel(a_ref, b_ref, out_ref):
    out_ref[...] = (a_ref[...].astype(F32) + b_ref[...].astype(F32)).astype(BF16)


def image_kernel(product, target, sectors, rows_ref, a_ref, b_ref, *refs):
    out_ref = refs[-2] if product != 1 else refs[-1]
    half, columns = out_ref.shape
    value = a_ref[...].astype(F32) + b_ref[...].astype(F32)
    rows = rows_of(rows_ref, target, sectors)
    if product == 1:
        out_ref[...] = masked(value, my_core() * half, rows).astype(BF16)
        return
    stats_ref = refs[-1]
    basis = [r[...].astype(F32) for r in refs[: product + 1]]
    stats, before = refs[product + 1 : -2], None
    if target:
        *stats, before = stats
    live = live_entries(rows_ref, columns)
    if product == 0:
        scale = 1.0 / jnp.sqrt(inner(stats[0], 0, live))
        value = value * scale
        known, others = [], [basis[0] * scale]
    else:
        norm, alpha, beta = first_scalars(*stats, live)
        scale = 1.0 / beta
        zeroth = basis[0] * (1.0 / norm)
        first = (basis[1] - alpha * zeroth) * scale
        image = (basis[2] - alpha * basis[1]) * scale
        value = (value - (alpha * scale) * basis[2]) * scale
        known, others = [image * image, image * first, image * zeroth], [image, first, zeroth]
    value = masked(value, my_core() * half, rows).astype(BF16)
    out_ref[...] = value
    value = value.astype(F32)
    write_sums(stats_ref, known + [value * v for v in [value] + others], before)


def last_kernel(rows_ref, *refs):
    out_ref, coef_ref = refs[-2:]
    start_stats, image_stats, last_stats = refs[-5:-2]
    sectors, block_rows, columns = out_ref.shape
    live = live_entries(rows_ref, columns)
    norm, alpha0, beta0 = first_scalars(start_stats, image_stats, live)
    one, none = jnp.ones_like(norm), jnp.zeros_like(norm)
    w11, w1q1, w1q0, zz, zw1, zq1, zq0 = (inner(last_stats, k, live) for k in range(7))
    gram = [[one, none, w1q0, zq0], [None, one, w1q1, zq1], [None, None, w11, zw1], [None] * 3 + [zz]]
    q0, q1, w1 = {0: one}, {1: one}, {2: one}
    alpha1 = w1q1
    r1 = plus(one, (one, w1), (-alpha1, q1), (-beta0, q0))
    beta1 = jnp.sqrt(jnp.maximum(form(gram, r1, r1), 0.0))
    q2 = plus(1.0 / beta1, (one, r1))
    w0 = {0: alpha0, 1: beta0}
    w2 = plus(1.0 / beta1, (beta0, {3: one}), (-alpha1, w1), (-beta0, w0))
    alpha2 = form(gram, q2, w2)
    r2 = plus(one, (one, w2), (-alpha2, q2), (-beta1, q1))
    beta2 = jnp.sqrt(jnp.maximum(form(gram, r2, r2), 0.0))
    q3 = plus(1.0 / beta2, (one, r2))
    c1 = q3[1] / beta0
    c2 = q3[2] / beta0
    coefs = [(q3[0] - alpha0 * c1) / norm, c1 - alpha0 * c2, c2, q3[3]]
    for t in range(sectors):
        for which in range(2):
            blocks = [refs[8 * t + 2 * k + which][...].astype(F32) for k in range(4)]
            vector = sum(c * block for c, block in zip(coefs, blocks))
            out_ref[t, half_of(which, block_rows // 2), :] = vector.astype(BF16)
    row = lax.broadcasted_iota(jnp.int32, coef_ref.shape, 0)
    column = lax.broadcasted_iota(jnp.int32, coef_ref.shape, 1)
    value = jnp.zeros(coef_ref.shape, F32)
    for k, (alpha, beta) in enumerate(((alpha0, beta0), (alpha1, beta1), (alpha2, beta2))):
        value = jnp.where((row == 0) & (column == k), alpha, value)
        value = jnp.where((row == 1) & (column == k), beta, value)
    coef_ref[...] = value


def on_device(wavefunction, left_blocks, right_blocks, charge_shifts, sector_rows):
    sectors, block_rows, columns = wavefunction.shape
    half = block_rows // 2
    n_sec, n_op = lax.axis_size("sec"), lax.axis_size("op")
    assert sectors == 2 and n_sec % 2 == 0 and n_op % 4 == 0
    core_pairs = [(i, i ^ 1) for i in range(n_op)]
    pairs = [(i, i ^ 1) for i in range(n_sec)]
    onward = [(i, i + 2) for i in range(0, n_sec - 2, 2)]
    onward += [(i, i - 2) for i in range(3, n_sec, 2)]

    def across_cores(value):
        return lax.ppermute(value, "op", core_pairs)

    def gathered(stats):
        parts = lax.all_gather(stats, "sec")
        return jnp.sum(parts[:, :8], axis=0)

    def sum_near(stats):
        stats = stats + across_cores(stats)
        return stats + lax.ppermute(stats, "sec", pairs)

    def sum_far(stats):
        bit = 2
        while bit < n_sec:
            flips = [bit] if 2 * bit >= n_sec else [bit, 2 * bit, 3 * bit]
            arrived = [
                lax.ppermute(stats, "sec", [(i, i ^ f) for i in range(n_sec)]) for f in flips
            ]
            if len(arrived) == 1:
                stats = stats + arrived[0]
            else:
                stats = (stats + arrived[0]) + (arrived[1] + arrived[2])
            bit *= len(flips) + 1
        return stats

    half_type = jax.ShapeDtypeStruct((half, columns), BF16)
    stats_type = jax.ShapeDtypeStruct((8, 128), F32)
    tall_type = jax.ShapeDtypeStruct((128, 128), F32)
    acc_type = jax.ShapeDtypeStruct((sectors, half, columns), F32)
    terms = 2 * left_blocks.shape[0]
    term_scratch = [pltpu.VMEM((3, block_rows, columns), BF16), pltpu.SMEM((terms,), jnp.int32)]
    acc_scratch = pltpu.VMEM((half, columns), F32)

    *halves, sums = call(
        start_kernel, "start", [half_type] * (2 * sectors) + [tall_type], [],
        sector_rows, wavefunction,
    )
    basis = [[(halves[0], halves[1]), (halves[2], halves[3])]]
    pair_0 = lax.ppermute(halves[0], "sec", pairs)
    half_left = jax.ShapeDtypeStruct((terms // 2, sectors, half, block_rows), BF16)
    keep, give = call(split_kernel, "split", [half_left] * 2, [], after(left_blocks, pair_0))
    operators = [
        jnp.concatenate([mine, other])
        for mine, other in (
            (charge_shifts, across_cores(charge_shifts)),
            (keep, across_cores(give)),
            (right_blocks, across_cores(right_blocks)),
        )
    ]
    stats = [gathered(sums)]
    pair_flops = 2 * half * columns * (block_rows + columns)

    for product in range(3):
        (mine_0, other_0), (mine_1, other_1) = basis[-1]
        if product:
            pair_0 = lax.ppermute(mine_0, "sec", pairs)
        pair_1 = lax.ppermute(after(mine_1, pair_0), "sec", pairs)
        far_0 = lax.ppermute(pair_0, "sec", onward)
        far_1 = lax.ppermute(pair_1, "sec", onward)
        scalars = (sector_rows, *stats) if product == 2 else ()
        acc = call(
            first_kernel, "first", acc_type, term_scratch, *operators,
            mine_0, other_0, pair_0, across_cores(pair_0), far_0, across_cores(far_0),
            *scalars, flops=terms * pair_flops,
        )
        acc = call(
            near_kernel, "near", acc_type, term_scratch, *operators,
            mine_1, other_1, pair_1, across_cores(pair_1), acc,
            *scalars, flops=terms * pair_flops // 2,
        )
        far_1 = after(far_1, acc)
        sources = (far_1, across_cores(far_1))
        values = [
            call(
                functools.partial(far_kernel, t), "far", half_type,
                term_scratch + [acc_scratch], *operators, *sources, acc,
                *scalars, flops=terms * pair_flops // 4,
            )
            for t in range(sectors)
        ]
        image = []
        sums = []
        for t, value in enumerate(values):
            bit = 2
            while 2 * bit < n_op:
                arrived = lax.ppermute(value, "op", [(i, i ^ bit) for i in range(n_op)])
                value = call(add_kernel, "add", half_type, [], value, arrived)
                bit *= 2
            arrived = lax.ppermute(value, "op", [(i, i ^ bit) for i in range(n_op)])
            out = [half_type] if product == 1 else [half_type, (tall_type, None, stats_type)[product]]
            needed = () if product == 1 else (*[b[t][0] for b in basis], *stats, *sums)
            mine, *sums = call(
                functools.partial(image_kernel, product, t, sectors), "image", out, [],
                sector_rows, value, arrived, *needed,
            )
            image.append((mine, across_cores(mine)))
        basis.append(image)
        if product == 0:
            total = gathered(sums[0])
            stats.append(total + across_cores(total))
    sums = sums[0]
    stats.append(sum_far(sum_near(sums)))

    flat = [h for t in range(sectors) for b in basis for h in b[t]]
    vector_type = jax.ShapeDtypeStruct(wavefunction.shape, BF16)
    coef_type = jax.ShapeDtypeStruct((2, 3), F32)
    vector, coef = call(
        last_kernel, "last", [vector_type, coef_type], [], sector_rows, *flat, *stats
    )
    return vector, coef


def solution(mesh):
    in_specs = (P("sec", None, None), P("op", "sec", None, None), P("op", None, None), P("op"), P())
    out_specs = (P("sec", None, None), P())
    return jax.shard_map(
        on_device, mesh=mesh, in_specs=in_specs, out_specs=out_specs, check_vma=False
    )
```

```python
import functools

import jax
import jax.numpy as jnp
from jax import lax
from jax.experimental import pallas as pl
from jax.experimental.pallas import tpu as pltpu
from jax.sharding import PartitionSpec as P

F32 = jnp.float32
BF16 = jnp.bfloat16
VMEM = pl.BlockSpec(memory_space=pltpu.VMEM)
SMEM = pl.BlockSpec(memory_space=pltpu.SMEM)


def call(kernel, name, out, scratch, *operands):
    return pl.pallas_call(
        kernel,
        name=name,
        out_shape=out,
        in_specs=[SMEM if a.dtype == jnp.int32 else VMEM for a in operands],
        out_specs=jax.tree.map(lambda _: VMEM, out),
        scratch_shapes=scratch,
        compiler_params=pltpu.CompilerParams(vmem_limit_bytes=24 << 20),
        cost_estimate=pl.CostEstimate(flops=0, bytes_accessed=0, transcendentals=0),
    )(*operands)


def after(value, *others):
    return lax.optimization_barrier((value, *others))[0]


def my_core():
    return lax.axis_index("op") % 2


def half_of(which, half):
    core = my_core()
    return pl.ds(pl.multiple_of((core if which == 0 else 1 - core) * half, half), half)


def rows_of(rows_ref, target, sectors):
    return rows_ref[lax.axis_index("sec") * sectors + target]


def live_entries(rows_ref, columns):
    return sum(rows_ref[i] for i in range(rows_ref.shape[0])).astype(F32) * columns


def masked(value, first, rows):
    return jnp.where(lax.broadcasted_iota(jnp.int32, value.shape, 0) + first < rows, value, 0.0)


def inner(stats_ref, row, live):
    return jnp.sum(stats_ref[row : row + 1, :], axis=1, keepdims=True) / live


def write_sums(stats_ref, values, before=None):
    parts = [jnp.zeros((1, 128), F32)] * 8
    for k, value in enumerate(values):
        folded = sum(value[:, i : i + 128] for i in range(0, value.shape[1], 128))
        parts[k] = jnp.sum(folded, axis=0, keepdims=True)
    rows = jnp.concatenate(parts, axis=0)
    stats_ref[...] = rows if before is None else rows + before[...]


def first_scalars(start_stats, image_stats, live):
    norm = jnp.sqrt(inner(start_stats, 0, live))
    alpha = inner(image_stats, 1, live)
    beta = jnp.sqrt(jnp.maximum(inner(image_stats, 0, live) - alpha * alpha, 0.0))
    return norm, alpha, beta


def form(gram, a, b):
    return sum(a[i] * b[j] * gram[min(i, j)][max(i, j)] for i in a for j in b)


def plus(scale, *terms):
    out = {}
    for c, vector in terms:
        for i, v in vector.items():
            out[i] = out[i] + c * v if i in out else c * v
    return {i: scale * v for i, v in out.items()}


def start_kernel(rows_ref, x_ref, *refs):
    *halves, stats_ref = refs
    sectors, block_rows, _ = x_ref.shape
    square = 0.0
    for t in range(sectors):
        for which in range(2):
            part = half_of(which, block_rows // 2)
            value = x_ref[t, part, :].astype(F32)
            value = masked(value, part.start, rows_of(rows_ref, t, sectors))
            halves[2 * t + which][...] = value.astype(BF16)
            square = square + value * value
    write_sums(stats_ref, [square])


def split_kernel(left_ref, keep_ref, give_ref):
    half = keep_ref.shape[2]
    for w in range(left_ref.shape[0]):
        for t in range(left_ref.shape[1]):
            keep_ref[w, t] = left_ref[w, t, half_of(0, half), :]
            give_ref[w, t] = left_ref[w, t, half_of(1, half), :]


def place_of(k):
    pair = jnp.where(lax.axis_index("sec") % 2 == 0, 2, 0)
    return (1, pair, 2 - pair)[k]


def gather_sources(slots, refs, scalars, v_ref):
    half = refs[0].shape[0]
    if scalars:
        rows_ref, *stats = scalars
        scale = 1.0 / first_scalars(*stats, live_entries(rows_ref, v_ref.shape[2]))[2]
    for i, slot in enumerate(slots):
        for which in range(2):
            value = refs[2 * i + which][...]
            if scalars:
                value = (value.astype(F32) * scale).astype(BF16)
            v_ref[slot, half_of(which, half), :] = value


def add_terms(chosen, slot, target, shifts_ref, left_ref, right_ref, v_ref, list_ref, acc_ref):
    count = jnp.int32(0)
    for w in range(shifts_ref.shape[0]):
        here = chosen(shifts_ref[w])

        @pl.when(here)
        def _():
            list_ref[count] = w

        count = count + here.astype(jnp.int32)

    def product(position):
        w = list_ref[position]
        source = v_ref[slot(shifts_ref[w])]
        part = jnp.dot(left_ref[w, target], source, preferred_element_type=F32).astype(BF16)
        return jnp.dot(part, right_ref[w], preferred_element_type=F32)

    def two(k, carry):
        acc_ref[...] += product(2 * k) + product(2 * k + 1)
        return carry

    lax.fori_loop(0, count >> 1, two, 0)

    @pl.when(count & 1 == 1)
    def _():
        acc_ref[...] += product(count - 1)


def near_kernel(shifts_ref, left_ref, right_ref, *refs):
    sources, (*scalars, acc_ref, v_ref, list_ref) = refs[:4], refs[4:]
    gather_sources((place_of(0), place_of(1)), sources, scalars, v_ref)
    far = place_of(2)
    for target in range(acc_ref.shape[0]):
        acc_ref[target] = jnp.zeros(acc_ref.shape[1:], F32)

        def place(shift):
            return ((target - shift) >> 1) + 1

        add_terms(
            lambda shift: ((target - shift) & 1 == 0) & (place(shift) != far), place,
            target, shifts_ref, left_ref, right_ref, v_ref, list_ref, acc_ref.at[target],
        )


def rest_kernel(target, shifts_ref, left_ref, right_ref, *refs):
    sources, sum_ref, (*scalars, out_ref, v_ref, list_ref, acc_ref) = refs[:8], refs[8], refs[9:]
    places = place_of(0), place_of(1), place_of(2)
    gather_sources((*places, 3), sources, scalars, v_ref)
    acc_ref[...] = sum_ref[target]

    def place(shift):
        return ((target - shift) >> 1) + 1

    def second(shift):
        return (target - shift) & 1 == 1

    add_terms(
        lambda shift: second(shift) | (place(shift) == places[2]),
        lambda shift: jnp.where(second(shift), place(shift), 3),
        target, shifts_ref, left_ref, right_ref, v_ref, list_ref, acc_ref,
    )
    out_ref[...] = acc_ref[...].astype(BF16)


def add_kernel(a_ref, b_ref, out_ref):
    out_ref[...] = (a_ref[...].astype(F32) + b_ref[...].astype(F32)).astype(BF16)


def image_kernel(product, target, sectors, rows_ref, a_ref, b_ref, *refs):
    out_ref = refs[-2] if product != 1 else refs[-1]
    half, columns = out_ref.shape
    value = a_ref[...].astype(F32) + b_ref[...].astype(F32)
    rows = rows_of(rows_ref, target, sectors)
    if product == 1:
        out_ref[...] = masked(value, my_core() * half, rows).astype(BF16)
        return
    stats_ref = refs[-1]
    basis = [r[...].astype(F32) for r in refs[: product + 1]]
    stats, before = refs[product + 1 : -2], None
    if target:
        *stats, before = stats
    live = live_entries(rows_ref, columns)
    if product == 0:
        scale = 1.0 / jnp.sqrt(inner(stats[0], 0, live))
        value = value * scale
        known, others = [], [basis[0] * scale]
    else:
        norm, alpha, beta = first_scalars(*stats, live)
        scale = 1.0 / beta
        zeroth = basis[0] * (1.0 / norm)
        first = (basis[1] - alpha * zeroth) * scale
        image = (basis[2] - alpha * basis[1]) * scale
        value = (value - (alpha * scale) * basis[2]) * scale
        known, others = [image * image, image * first, image * zeroth], [image, first, zeroth]
    value = masked(value, my_core() * half, rows).astype(BF16)
    out_ref[...] = value
    value = value.astype(F32)
    write_sums(stats_ref, known + [value * v for v in [value] + others], before)


def last_kernel(rows_ref, *refs):
    out_ref, coef_ref = refs[-2:]
    start_stats, image_stats, last_stats = refs[-5:-2]
    sectors, block_rows, columns = out_ref.shape
    live = live_entries(rows_ref, columns)
    norm, alpha0, beta0 = first_scalars(start_stats, image_stats, live)
    one, none = jnp.ones_like(norm), jnp.zeros_like(norm)
    w11, w1q1, w1q0, zz, zw1, zq1, zq0 = (inner(last_stats, k, live) for k in range(7))
    gram = [[one, none, w1q0, zq0], [None, one, w1q1, zq1], [None, None, w11, zw1], [None] * 3 + [zz]]
    q0, q1, w1 = {0: one}, {1: one}, {2: one}
    alpha1 = w1q1
    r1 = plus(one, (one, w1), (-alpha1, q1), (-beta0, q0))
    beta1 = jnp.sqrt(jnp.maximum(form(gram, r1, r1), 0.0))
    q2 = plus(1.0 / beta1, (one, r1))
    w0 = {0: alpha0, 1: beta0}
    w2 = plus(1.0 / beta1, (beta0, {3: one}), (-alpha1, w1), (-beta0, w0))
    alpha2 = form(gram, q2, w2)
    r2 = plus(one, (one, w2), (-alpha2, q2), (-beta1, q1))
    beta2 = jnp.sqrt(jnp.maximum(form(gram, r2, r2), 0.0))
    q3 = plus(1.0 / beta2, (one, r2))
    c1 = q3[1] / beta0
    c2 = q3[2] / beta0
    coefs = [(q3[0] - alpha0 * c1) / norm, c1 - alpha0 * c2, c2, q3[3]]
    for t in range(sectors):
        for which in range(2):
            blocks = [refs[8 * t + 2 * k + which][...].astype(F32) for k in range(4)]
            vector = sum(c * block for c, block in zip(coefs, blocks))
            out_ref[t, half_of(which, block_rows // 2), :] = vector.astype(BF16)
    row = lax.broadcasted_iota(jnp.int32, coef_ref.shape, 0)
    column = lax.broadcasted_iota(jnp.int32, coef_ref.shape, 1)
    value = jnp.zeros(coef_ref.shape, F32)
    for k, (alpha, beta) in enumerate(((alpha0, beta0), (alpha1, beta1), (alpha2, beta2))):
        value = jnp.where((row == 0) & (column == k), alpha, value)
        value = jnp.where((row == 1) & (column == k), beta, value)
    coef_ref[...] = value


def on_device(wavefunction, left_blocks, right_blocks, charge_shifts, sector_rows):
    sectors, block_rows, columns = wavefunction.shape
    half = block_rows // 2
    n_sec, n_op = lax.axis_size("sec"), lax.axis_size("op")
    assert sectors == 2 and n_sec % 2 == 0 and n_op % 4 == 0
    core_pairs = [(i, i ^ 1) for i in range(n_op)]
    pairs = [(i, i ^ 1) for i in range(n_sec)]
    onward = [(i, i + 2) for i in range(0, n_sec - 2, 2)]
    onward += [(i, i - 2) for i in range(3, n_sec, 2)]
    diagonal = [(i, i + 1) for i in range(1, n_sec - 1, 2)]
    diagonal += [(j, i) for i, j in diagonal]

    def across_cores(value):
        return lax.ppermute(value, "op", core_pairs)

    def flipped_sum(stats, bits):
        for bit in bits:
            stats = stats + lax.ppermute(stats, "sec", [(i, i ^ bit) for i in range(n_sec)])
        return stats

    bits = [1 << k for k in range(n_sec.bit_length() - 1)]

    half_type = jax.ShapeDtypeStruct((half, columns), BF16)
    stats_type = jax.ShapeDtypeStruct((8, 128), F32)
    acc_type = jax.ShapeDtypeStruct((sectors, half, columns), F32)
    terms = 2 * left_blocks.shape[0]
    term_scratch = [pltpu.VMEM((4, block_rows, columns), BF16), pltpu.SMEM((terms,), jnp.int32)]
    acc_scratch = pltpu.VMEM((half, columns), F32)

    *halves, sums = call(
        start_kernel, "start", [half_type] * (2 * sectors) + [stats_type], [],
        sector_rows, wavefunction,
    )
    basis = [[(halves[0], halves[1]), (halves[2], halves[3])]]
    pair_0 = lax.ppermute(halves[0], "sec", pairs)
    start_sums = flipped_sum(sums, bits[:1])
    half_left = jax.ShapeDtypeStruct((terms // 2, sectors, half, block_rows), BF16)
    keep, give = call(split_kernel, "split", [half_left] * 2, [], left_blocks)
    operators = [
        jnp.concatenate([mine, other])
        for mine, other in (
            (charge_shifts, across_cores(charge_shifts)),
            (keep, across_cores(give)),
            (right_blocks, across_cores(right_blocks)),
        )
    ]
    stats = []
    pair_0 = after(pair_0, start_sums, keep)

    for product in range(3):
        (mine_0, other_0), (mine_1, other_1) = basis[-1]
        if product:
            pair_0 = lax.ppermute(mine_0, "sec", pairs)
        if product:
            pair_0 = after(pair_0, mine_1)
        else:
            mine_1 = after(mine_1, pair_0)
        if product == 2:
            image_sums = flipped_sum(after(image_sums, mine_0), bits[2:])
            pair_0 = after(pair_0, image_sums)
            stats.append(image_sums)
        pair_1 = lax.ppermute(mine_1, "sec", pairs)
        far_0 = lax.ppermute(pair_0, "sec", onward)
        far_1 = lax.ppermute(mine_1, "sec", diagonal)
        scalars = (sector_rows, *stats) if product == 2 else ()
        acc = call(
            near_kernel, "near", acc_type, term_scratch, *operators,
            mine_0, other_0, pair_0, across_cores(pair_0), *scalars,
        )
        sources = [mine_1, other_1]
        for part in (pair_1, far_1, far_0):
            sources += [part, across_cores(part)]
        values = [
            call(
                functools.partial(rest_kernel, t), "rest", half_type,
                term_scratch + [acc_scratch], *operators, *sources, acc, *scalars,
            )
            for t in range(sectors)
        ]
        image = []
        earlier = []
        for t, value in enumerate(values):
            bit = 2
            while 2 * bit < n_op:
                arrived = lax.ppermute(value, "op", [(i, i ^ bit) for i in range(n_op)])
                value = call(add_kernel, "add", half_type, [], value, arrived)
                bit *= 2
            arrived = lax.ppermute(value, "op", [(i, i ^ bit) for i in range(n_op)])
            if t == 0 and product == 0:
                stats.append(flipped_sum(after(start_sums, values[-1]), bits[1:]))
            elif t == 0 and product == 1:
                image_sums = sums + across_cores(sums)
                image_sums = flipped_sum(after(image_sums, values[-1]), bits[:2])
                arrived = after(arrived, image_sums)
            elif t == 0:
                arrived = after(arrived, values[-1])
            out = [half_type] if product == 1 else [half_type, stats_type]
            needed = () if product == 1 else (*[b[t][0] for b in basis], *stats, *earlier)
            mine, *earlier = call(
                functools.partial(image_kernel, product, t, sectors), "image", out, [],
                sector_rows, value, arrived, *needed,
            )
            image.append((mine, across_cores(mine)))
        basis.append(image)
        if earlier:
            sums = earlier[0]
    stats.append(flipped_sum(sums + across_cores(sums), bits))

    flat = [h for t in range(sectors) for b in basis for h in b[t]]
    vector_type = jax.ShapeDtypeStruct(wavefunction.shape, BF16)
    coef_type = jax.ShapeDtypeStruct((2, 3), F32)
    vector, coef = call(
        last_kernel, "last", [vector_type, coef_type], [], sector_rows, *flat, *stats
    )
    return vector, coef


def solution(mesh):
    in_specs = (P("sec", None, None), P("op", "sec", None, None), P("op", None, None), P("op"), P())
    out_specs = (P("sec", None, None), P())
    return jax.shard_map(
        on_device, mesh=mesh, in_specs=in_specs, out_specs=out_specs, check_vma=False
    )
```

```python
import functools

import jax
import jax.numpy as jnp
from jax import lax
from jax.experimental import pallas as pl
from jax.experimental.pallas import tpu as pltpu
from jax.sharding import PartitionSpec as P

F32 = jnp.float32
BF16 = jnp.bfloat16
VMEM = pl.BlockSpec(memory_space=pltpu.VMEM)
SMEM = pl.BlockSpec(memory_space=pltpu.SMEM)


def call(kernel, name, out, scratch, *operands):
    return pl.pallas_call(
        kernel,
        name=name,
        out_shape=out,
        in_specs=[SMEM if a.dtype == jnp.int32 else VMEM for a in operands],
        out_specs=jax.tree.map(lambda _: VMEM, out),
        scratch_shapes=scratch,
        compiler_params=pltpu.CompilerParams(vmem_limit_bytes=16 << 20),
        cost_estimate=pl.CostEstimate(flops=0, bytes_accessed=0, transcendentals=0),
    )(*operands)


def after(value, *others):
    return lax.optimization_barrier((value, *others))[0]


def my_core():
    return lax.axis_index("op") % 2


def half_of(which, half):
    core = my_core()
    return pl.ds(pl.multiple_of((core if which == 0 else 1 - core) * half, half), half)


def rows_of(rows_ref, target, sectors):
    return rows_ref[lax.axis_index("sec") * sectors + target]


def live_entries(rows_ref, columns):
    return sum(rows_ref[i] for i in range(rows_ref.shape[0])).astype(F32) * columns


def masked(value, first, rows):
    return jnp.where(lax.broadcasted_iota(jnp.int32, value.shape, 0) + first < rows, value, 0.0)


def inner(stats_ref, row, live):
    return jnp.sum(stats_ref[row : row + 1, :], axis=1, keepdims=True) / live


def write_sums(stats_ref, values, before=None):
    parts = [jnp.zeros((1, 128), F32)] * 8
    for k, value in enumerate(values):
        folded = sum(value[:, i : i + 128] for i in range(0, value.shape[1], 128))
        parts[k] = jnp.sum(folded, axis=0, keepdims=True)
    rows = jnp.concatenate(parts, axis=0)
    stats_ref[...] = rows if before is None else rows + before[...]


def first_scalars(start_stats, image_stats, live):
    norm = jnp.sqrt(inner(start_stats, 0, live))
    alpha = inner(image_stats, 1, live)
    beta = jnp.sqrt(jnp.maximum(inner(image_stats, 0, live) - alpha * alpha, 0.0))
    return norm, alpha, beta


def form(gram, a, b):
    return sum(a[i] * b[j] * gram[min(i, j)][max(i, j)] for i in a for j in b)


def plus(scale, *terms):
    out = {}
    for c, vector in terms:
        for i, v in vector.items():
            out[i] = out[i] + c * v if i in out else c * v
    return {i: scale * v for i, v in out.items()}


def start_kernel(rows_ref, x_ref, *refs):
    *halves, stats_ref = refs
    sectors, block_rows, _ = x_ref.shape
    square = 0.0
    for t in range(sectors):
        for which in range(2):
            part = half_of(which, block_rows // 2)
            value = x_ref[t, part, :].astype(F32)
            value = masked(value, part.start, rows_of(rows_ref, t, sectors))
            halves[2 * t + which][...] = value.astype(BF16)
            square = square + value * value
    write_sums(stats_ref, [square])


def place_of(k):
    pair = jnp.where(lax.axis_index("sec") % 2 == 0, 2, 0)
    return (1, pair, 2 - pair)[k]


def stage_kernel(left_ref, right_ref, left_out, right_out, sems):
    copies = [
        pltpu.make_async_copy(left_ref, left_out, sems.at[0]),
        pltpu.make_async_copy(right_ref, right_out, sems.at[1]),
    ]
    for copy in copies:
        copy.start()
    for copy in copies:
        copy.wait()


def gather_sources(slots, refs, scalars, v_ref):
    half = refs[0].shape[0]
    if scalars:
        rows_ref, *stats = scalars
        scale = 1.0 / first_scalars(*stats, live_entries(rows_ref, v_ref.shape[2]))[2]
    for i, slot in enumerate(slots):
        for which in range(2):
            value = refs[2 * i + which][...]
            if scalars:
                value = (value.astype(F32) * scale).astype(BF16)
            v_ref[slot, half_of(which, half), :] = value


def full_kernel(target, *refs):
    operators, sources, (*scalars, out_ref, v_ref) = refs[:6], refs[6:18], refs[18:]
    gather_sources((0, 1, 2, 3, 4, 5), sources, scalars, v_ref)
    far = place_of(2)
    half = out_ref.shape[0]
    total = None
    for shifts_ref, left_ref, right_ref in (operators[:3], operators[3:]):
        for w in range(left_ref.shape[0]):
            offset = target - shifts_ref[w]
            place = (offset >> 1) + 1
            kind = jnp.where(place == 1, 0, jnp.where(place == far, 4, 2))
            part = jnp.dot(
                left_ref[w, target, half_of(0, half), :],
                v_ref[kind + (offset & 1)],
                preferred_element_type=F32,
            ).astype(BF16)
            term = jnp.dot(part, right_ref[w], preferred_element_type=F32)
            total = term if total is None else total + term
    out_ref[...] = total.astype(BF16)


def add_kernel(a_ref, b_ref, out_ref):
    out_ref[...] = (a_ref[...].astype(F32) + b_ref[...].astype(F32)).astype(BF16)


def image_kernel(product, target, sectors, rows_ref, a_ref, b_ref, *refs):
    out_ref = refs[-2] if product != 1 else refs[-1]
    half, columns = out_ref.shape
    value = a_ref[...].astype(F32) + b_ref[...].astype(F32)
    rows = rows_of(rows_ref, target, sectors)
    if product == 1:
        out_ref[...] = masked(value, my_core() * half, rows).astype(BF16)
        return
    stats_ref = refs[-1]
    basis = [r[...].astype(F32) for r in refs[: product + 1]]
    stats, before = refs[product + 1 : -2], None
    if target:
        *stats, before = stats
    live = live_entries(rows_ref, columns)
    if product == 0:
        scale = 1.0 / jnp.sqrt(inner(stats[0], 0, live))
        value = value * scale
        known, others = [], [basis[0] * scale]
    else:
        norm, alpha, beta = first_scalars(*stats, live)
        scale = 1.0 / beta
        zeroth = basis[0] * (1.0 / norm)
        first = (basis[1] - alpha * zeroth) * scale
        image = (basis[2] - alpha * basis[1]) * scale
        value = (value - (alpha * scale) * basis[2]) * scale
        known, others = [image * image, image * first, image * zeroth], [image, first, zeroth]
    value = masked(value, my_core() * half, rows).astype(BF16)
    out_ref[...] = value
    value = value.astype(F32)
    write_sums(stats_ref, known + [value * v for v in [value] + others], before)


def last_kernel(rows_ref, *refs):
    out_ref, coef_ref = refs[-2:]
    start_stats, image_stats, last_stats = refs[-5:-2]
    sectors, block_rows, columns = out_ref.shape
    live = live_entries(rows_ref, columns)
    norm, alpha0, beta0 = first_scalars(start_stats, image_stats, live)
    one, none = jnp.ones_like(norm), jnp.zeros_like(norm)
    w11, w1q1, w1q0, zz, zw1, zq1, zq0 = (inner(last_stats, k, live) for k in range(7))
    gram = [[one, none, w1q0, zq0], [None, one, w1q1, zq1], [None, None, w11, zw1], [None] * 3 + [zz]]
    q0, q1, w1 = {0: one}, {1: one}, {2: one}
    alpha1 = w1q1
    r1 = plus(one, (one, w1), (-alpha1, q1), (-beta0, q0))
    beta1 = jnp.sqrt(jnp.maximum(form(gram, r1, r1), 0.0))
    q2 = plus(1.0 / beta1, (one, r1))
    w0 = {0: alpha0, 1: beta0}
    w2 = plus(1.0 / beta1, (beta0, {3: one}), (-alpha1, w1), (-beta0, w0))
    alpha2 = form(gram, q2, w2)
    r2 = plus(one, (one, w2), (-alpha2, q2), (-beta1, q1))
    beta2 = jnp.sqrt(jnp.maximum(form(gram, r2, r2), 0.0))
    q3 = plus(1.0 / beta2, (one, r2))
    c1 = q3[1] / beta0
    c2 = q3[2] / beta0
    coefs = [(q3[0] - alpha0 * c1) / norm, c1 - alpha0 * c2, c2, q3[3]]
    for t in range(sectors):
        for which in range(2):
            blocks = [refs[8 * t + 2 * k + which][...].astype(F32) for k in range(4)]
            vector = sum(c * block for c, block in zip(coefs, blocks))
            out_ref[t, half_of(which, block_rows // 2), :] = vector.astype(BF16)
    row = lax.broadcasted_iota(jnp.int32, coef_ref.shape, 0)
    column = lax.broadcasted_iota(jnp.int32, coef_ref.shape, 1)
    value = jnp.zeros(coef_ref.shape, F32)
    for k, (alpha, beta) in enumerate(((alpha0, beta0), (alpha1, beta1), (alpha2, beta2))):
        value = jnp.where((row == 0) & (column == k), alpha, value)
        value = jnp.where((row == 1) & (column == k), beta, value)
    coef_ref[...] = value


def on_device(wavefunction, left_blocks, right_blocks, charge_shifts, sector_rows):
    sectors, block_rows, columns = wavefunction.shape
    half = block_rows // 2
    n_sec, n_op = lax.axis_size("sec"), lax.axis_size("op")
    assert sectors == 2 and n_sec % 2 == 0 and n_op % 4 == 0
    core_pairs = [(i, i ^ 1) for i in range(n_op)]
    pairs = [(i, i ^ 1) for i in range(n_sec)]
    onward = [(i, i + 2) for i in range(0, n_sec - 2, 2)]
    onward += [(i, i - 2) for i in range(3, n_sec, 2)]
    diagonal = [(i, i + 1) for i in range(1, n_sec - 1, 2)]
    diagonal += [(j, i) for i, j in diagonal]

    def across_cores(value):
        return lax.ppermute(value, "op", core_pairs)

    def flipped_sum(stats, bits):
        for bit in bits:
            stats = stats + lax.ppermute(stats, "sec", [(i, i ^ bit) for i in range(n_sec)])
        return stats

    def sum_pairs(stats):
        crossed = [(i, i ^ 1 ^ n_op) for i in range(n_op * n_sec)]
        core = lax.ppermute(stats, "op", core_pairs)
        pair = lax.ppermute(stats, "sec", pairs)
        cross = lax.ppermute(stats, ("sec", "op"), crossed)
        return (stats + cross) + (core + pair)

    bits = [1 << k for k in range(n_sec.bit_length() - 1)]

    half_type = jax.ShapeDtypeStruct((half, columns), BF16)
    stats_type = jax.ShapeDtypeStruct((8, 128), F32)
    v_scratch = pltpu.VMEM((6, block_rows, columns), BF16)

    *halves, sums = call(
        start_kernel, "start", [half_type] * (2 * sectors) + [stats_type], [],
        sector_rows, wavefunction,
    )
    basis = [[(halves[0], halves[1]), (halves[2], halves[3])]]
    pair_0 = lax.ppermute(halves[0], "sec", pairs)
    start_sums = flipped_sum(sums, bits[1:])
    operators = (charge_shifts, left_blocks, right_blocks)
    others = tuple(across_cores(value) for value in operators)
    stats = []
    pair_0 = after(pair_0, start_sums)

    for product in range(3):
        (mine_0, other_0), (mine_1, other_1) = basis[-1]
        if product:
            pair_0 = lax.ppermute(mine_0, "sec", pairs)
        if product:
            pair_0 = after(pair_0, mine_1)
        else:
            mine_1 = after(mine_1, pair_0)
        if product == 2:
            image_sums = flipped_sum(after(image_sums, mine_0), bits[1:2])
            pair_0 = after(pair_0, image_sums)
        pair_1 = lax.ppermute(mine_1, "sec", pairs)
        if product == 0:
            hbm = pl.BlockSpec(memory_space=pltpu.HBM)
            left, right = pl.pallas_call(
                stage_kernel,
                name="stage",
                out_shape=[jax.ShapeDtypeStruct(v.shape, v.dtype) for v in operators[1:]],
                in_specs=[hbm] * 2,
                out_specs=[VMEM] * 2,
                scratch_shapes=[pltpu.SemaphoreType.DMA((2,))],
                compiler_params=pltpu.CompilerParams(vmem_limit_bytes=16 << 20),
                cost_estimate=pl.CostEstimate(flops=0, bytes_accessed=0, transcendentals=0),
            )(after(operators[1], pair_0), operators[2])
            operators = (charge_shifts, left, right) + others
            pair_1 = after(pair_1, left)
        far_0 = lax.ppermute(pair_0, "sec", onward)
        far_1 = lax.ppermute(mine_1, "sec", diagonal)
        if product == 0:
            start_sums = flipped_sum(after(start_sums, pair_0), bits[:1])
            stats.append(start_sums)
            pair_1 = after(pair_1, start_sums)
        elif product == 1:
            image_sums = flipped_sum(sums + across_cores(sums), bits[:1])
            pair_1 = after(pair_1, image_sums)
        else:
            image_sums = flipped_sum(after(image_sums, pair_0), bits[2:])
            stats.append(image_sums)
            pair_1 = after(pair_1, image_sums)
        scalars = (sector_rows, *stats) if product == 2 else ()
        sources = [mine_0, other_0, mine_1, other_1]
        for part in (pair_0, pair_1, far_0, far_1):
            sources += [part, across_cores(part)]
        values = [
            call(
                functools.partial(full_kernel, t), "full", half_type,
                [v_scratch], *operators, *sources, *scalars,
            )
            for t in range(sectors)
        ]
        image = []
        earlier = []
        for t, value in enumerate(values):
            bit = 2
            while 2 * bit < n_op:
                arrived = lax.ppermute(value, "op", [(i, i ^ bit) for i in range(n_op)])
                value = call(add_kernel, "add", half_type, [], value, arrived)
                bit *= 2
            arrived = lax.ppermute(value, "op", [(i, i ^ bit) for i in range(n_op)])
            if t == 0:
                arrived = after(arrived, values[-1])
            out = [half_type] if product == 1 else [half_type, stats_type]
            needed = () if product == 1 else (*[b[t][0] for b in basis], *stats, *earlier)
            mine, *earlier = call(
                functools.partial(image_kernel, product, t, sectors), "image", out, [],
                sector_rows, value, arrived, *needed,
            )
            image.append((mine, across_cores(mine)))
        basis.append(image)
        if earlier:
            sums = earlier[0]
    stats.append(flipped_sum(sum_pairs(sums), bits[1:]))

    flat = [h for t in range(sectors) for b in basis for h in b[t]]
    vector_type = jax.ShapeDtypeStruct(wavefunction.shape, BF16)
    coef_type = jax.ShapeDtypeStruct((2, 3), F32)
    vector, coef = call(
        last_kernel, "last", [vector_type, coef_type], [], sector_rows, *flat, *stats
    )
    return vector, coef


def solution(mesh):
    in_specs = (P("sec", None, None), P("op", "sec", None, None), P("op", None, None), P("op"), P())
    out_specs = (P("sec", None, None), P())
    return jax.shard_map(
        on_device, mesh=mesh, in_specs=in_specs, out_specs=out_specs, check_vma=False
    )
```

```python
import functools

import jax
import jax.numpy as jnp
from jax import lax
from jax.experimental import pallas as pl
from jax.experimental.pallas import tpu as pltpu
from jax.sharding import PartitionSpec as P

F32 = jnp.float32
BF16 = jnp.bfloat16
START_SCALE = 2.0**60
VMEM = pl.BlockSpec(memory_space=pltpu.VMEM)
SMEM = pl.BlockSpec(memory_space=pltpu.SMEM)


def call(kernel, name, out, scratch, *operands):
    return pl.pallas_call(
        kernel,
        name=name,
        out_shape=out,
        in_specs=[SMEM if a.dtype == jnp.int32 else VMEM for a in operands],
        out_specs=jax.tree.map(lambda _: VMEM, out),
        scratch_shapes=scratch,
        compiler_params=pltpu.CompilerParams(vmem_limit_bytes=16 << 20),
        cost_estimate=pl.CostEstimate(flops=0, bytes_accessed=0, transcendentals=0),
    )(*operands)


def after(value, *others):
    return lax.optimization_barrier((value, *others))[0]


def my_core():
    return lax.axis_index("op") % 2


def half_of(which, half):
    core = my_core()
    return pl.ds(pl.multiple_of((core if which == 0 else 1 - core) * half, half), half)


def side_of(which, rows, count):
    side = lax.axis_index("op") // (count // 2)
    return pl.ds(pl.multiple_of((side if which == 0 else 1 - side) * rows, rows), rows)


def rows_of(rows_ref, target, sectors):
    return rows_ref[lax.axis_index("sec") * sectors + target]


def live_entries(rows_ref, columns):
    return sum(rows_ref[i] for i in range(rows_ref.shape[0])).astype(F32) * columns


def masked(value, first, rows):
    return jnp.where(lax.broadcasted_iota(jnp.int32, value.shape, 0) + first < rows, value, 0.0)


def inner(stats_ref, row, live):
    return jnp.sum(stats_ref[row : row + 1, :], axis=1, keepdims=True) / live


def write_sums(stats_ref, values, before=None):
    parts = [jnp.zeros((1, 128), F32)] * 8
    for k, value in enumerate(values):
        folded = sum(value[:, i : i + 128] for i in range(0, value.shape[1], 128))
        parts[k] = jnp.sum(folded, axis=0, keepdims=True)
    rows = jnp.concatenate(parts, axis=0)
    stats_ref[...] = rows if before is None else rows + before[...]


def largest(value):
    return jnp.maximum(jnp.max(jnp.abs(value), keepdims=True), 1e-37)


def scaled_sums(pairs):
    sums, lefts, rights = [], [], []
    for left, right in pairs:
        scales = largest(left), largest(right)
        product = (left * (1.0 / scales[0])) * (right * (1.0 / scales[1]))
        folded = sum(product[:, i : i + 128] for i in range(0, product.shape[1], 128))
        sums.append(jnp.sum(folded, axis=0, keepdims=True))
        lefts.append(jnp.broadcast_to(scales[0], (1, 128)))
        rights.append(jnp.broadcast_to(scales[1], (1, 128)))
    fill = [jnp.zeros((1, 128), F32)] * (8 - len(pairs))
    ones = [jnp.full((1, 128), 1e-37, F32)] * (8 - len(pairs))
    return jnp.concatenate(sums + fill + lefts + ones + rights + ones, axis=0)


def merged(a, b):
    left = jnp.maximum(a[8:16], b[8:16])
    right = jnp.maximum(a[16:], b[16:])
    total = sum(t[:8] * (t[8:16] / left) * (t[16:] / right) for t in (a, b))
    return jnp.concatenate([total, left, right], axis=0)


def merge_kernel(axis, bit, own_ref, arrived_ref, out_ref):
    low = lax.axis_index(axis) & bit == 0
    own, arrived = own_ref[...], arrived_ref[...]
    out_ref[...] = merged(jnp.where(low, own, arrived), jnp.where(low, arrived, own))


def first_scalars(tile, live):
    def row(k):
        return (
            jnp.sum(tile[k : k + 1, :], axis=1, keepdims=True) / live,
            tile[8 + k : 9 + k, 0:1],
            tile[16 + k : 17 + k, 0:1],
        )

    square, scale, _ = row(0)
    norm = scale * jnp.sqrt(square)
    cross, image_scale, start_scale = row(1)
    alpha = cross * (image_scale / norm) * (start_scale / norm)
    image_square, image_scale, _ = row(2)
    unit = image_scale / norm
    rest = image_square - (alpha / unit) * (alpha / unit)
    return norm, alpha, unit * jnp.sqrt(jnp.maximum(rest, 0.0))


def form(gram, a, b):
    return sum(a[i] * b[j] * gram[min(i, j)][max(i, j)] for i in a for j in b)


def plus(scale, *terms):
    out = {}
    for c, vector in terms:
        for i, v in vector.items():
            out[i] = out[i] + c * v if i in out else c * v
    return {i: scale * v for i, v in out.items()}


def start_kernel(rows_ref, x_ref, *refs):
    sectors, block_rows, _ = x_ref.shape
    for t in range(sectors):
        for which in range(2):
            part = half_of(which, block_rows // 2)
            value = masked(
                x_ref[t, part, :].astype(F32), part.start, rows_of(rows_ref, t, sectors)
            )
            refs[2 * t + which][...] = (value * START_SCALE).astype(BF16)


def place_of(k):
    pair = jnp.where(lax.axis_index("sec") % 2 == 0, 2, 0)
    return (1, pair, 2 - pair)[k]


def stage_kernel(left_ref, right_ref, left_out, right_out, sems):
    copies = [
        pltpu.make_async_copy(left_ref, left_out, sems.at[0]),
        pltpu.make_async_copy(right_ref, right_out, sems.at[1]),
    ]
    for copy in copies:
        copy.start()
    for copy in copies:
        copy.wait()


def gather_sources(slots, refs, scalars, v_ref):
    half = refs[0].shape[0]
    if scalars:
        rows_ref, tile_ref = scalars
        norm, _, beta = first_scalars(tile_ref, live_entries(rows_ref, v_ref.shape[2]))
        scale = 1.0 / (norm * beta)
    for i, slot in enumerate(slots):
        for which in range(2):
            value = refs[2 * i + which][...]
            if scalars:
                value = (value.astype(F32) * scale).astype(BF16)
            v_ref[slot, half_of(which, half), :] = value


def full_kernel(target, *refs):
    operators, sources, rest = refs[:6], refs[6:18], refs[18:]
    if len(rest) == 2:
        scalars, outs, v_ref = (), rest[:1], rest[1]
    else:
        *scalars, keep_ref, give_ref, v_ref, total_ref = rest
        outs = keep_ref, give_ref
    gather_sources((0, 1, 2, 3, 4, 5), sources, scalars, v_ref)
    far = place_of(2)
    half = sources[0].shape[0]
    total = None
    for shifts_ref, left_ref, right_ref in (operators[:3], operators[3:]):
        for w in range(left_ref.shape[0]):
            offset = target - shifts_ref[w]
            place = (offset >> 1) + 1
            kind = jnp.where(place == 1, 0, jnp.where(place == far, 4, 2))
            part = jnp.dot(
                left_ref[w, target, half_of(0, half), :],
                v_ref[kind + (offset & 1)],
                preferred_element_type=F32,
            ).astype(BF16)
            term = jnp.dot(part, right_ref[w], preferred_element_type=F32)
            total = term if total is None else total + term
    if len(outs) == 1:
        outs[0][...] = total.astype(BF16)
    else:
        total_ref[...] = total.astype(BF16)
        for which, ref in enumerate(outs):
            ref[...] = total_ref[side_of(which, half // 2, lax.axis_size("op")), :]


def add_kernel(a_ref, b_ref, out_ref):
    out_ref[...] = (a_ref[...].astype(F32) + b_ref[...].astype(F32)).astype(BF16)


def image_kernel(product, target, sectors, rows_ref, a_ref, b_ref, *refs):
    out_ref = refs[-2] if product != 1 else refs[-1]
    half, columns = out_ref.shape
    value = a_ref[...].astype(F32) + b_ref[...].astype(F32)
    rows = rows_of(rows_ref, target, sectors)
    first_row = my_core() * half
    part = pl.ds(0, half)
    if product == 2:
        part = side_of(0, half, lax.axis_size("op"))
        first_row = 2 * first_row + part.start
    value = masked(value, first_row, rows)
    if product == 1:
        out_ref[...] = value.astype(BF16)
        return
    stats_ref = refs[-1]
    basis = [r[part, :].astype(F32) for r in refs[: product + 1]]
    if product == 0:
        value = value.astype(BF16)
        out_ref[...] = value
        value = value.astype(F32)
        tile = scaled_sums([(basis[0], basis[0]), (value, basis[0]), (value, value)])
        stats_ref[...] = merged(refs[1][...], tile) if target else tile
        return
    tile_ref, before = refs[product + 1], refs[product + 2] if target else None
    norm, alpha, beta = first_scalars(tile_ref, live_entries(rows_ref, columns))
    zeroth, image, second = (block * (1.0 / norm) for block in basis)
    scale = 1.0 / beta
    first = (image - alpha * zeroth) * scale
    value = (value - (alpha * scale) * second) * scale
    second = (second - alpha * image) * scale
    value = value.astype(BF16)
    out_ref[...] = value
    value = value.astype(F32)
    known = [second * second, second * first, second * zeroth]
    write_sums(stats_ref, known + [value * v for v in (value, second, first, zeroth)], before)


def last_kernel(rows_ref, *refs):
    out_ref, coef_ref = refs[-2:]
    tile_ref, last_stats = refs[-4:-2]
    sectors, block_rows, columns = out_ref.shape
    live = live_entries(rows_ref, columns)
    norm, alpha0, beta0 = first_scalars(tile_ref, live)
    one, none = jnp.ones_like(norm), jnp.zeros_like(norm)
    w11, w1q1, w1q0, zz, zw1, zq1, zq0 = (inner(last_stats, k, live) for k in range(7))
    gram = [[one, none, w1q0, zq0], [None, one, w1q1, zq1], [None, None, w11, zw1], [None] * 3 + [zz]]
    q0, q1, w1 = {0: one}, {1: one}, {2: one}
    alpha1 = w1q1
    r1 = plus(one, (one, w1), (-alpha1, q1), (-beta0, q0))
    beta1 = jnp.sqrt(jnp.maximum(form(gram, r1, r1), 0.0))
    q2 = plus(1.0 / beta1, (one, r1))
    w0 = {0: alpha0, 1: beta0}
    w2 = plus(1.0 / beta1, (beta0, {3: one}), (-alpha1, w1), (-beta0, w0))
    alpha2 = form(gram, q2, w2)
    r2 = plus(one, (one, w2), (-alpha2, q2), (-beta1, q1))
    beta2 = jnp.sqrt(jnp.maximum(form(gram, r2, r2), 0.0))
    q3 = plus(1.0 / beta2, (one, r2))
    c1 = q3[1] / beta0
    c2 = q3[2] / beta0
    coefs = [(q3[0] - alpha0 * c1) / norm, (c1 - alpha0 * c2) / norm, c2 / norm, q3[3]]
    quarter = block_rows // 4
    for t in range(sectors):
        sector_refs = refs[10 * t : 10 * t + 10]
        for which in range(2):
            start = half_of(which, 2 * quarter).start
            for side in range(2):
                part = side_of(side, quarter, lax.axis_size("op"))
                blocks = [sector_refs[2 * k + which][part, :] for k in range(3)]
                blocks.append(sector_refs[6 + 2 * side + which][...])
                vector = sum(c * block.astype(F32) for c, block in zip(coefs, blocks))
                rows = pl.ds(pl.multiple_of(start + part.start, quarter), quarter)
                out_ref[t, rows, :] = vector.astype(BF16)
    row = lax.broadcasted_iota(jnp.int32, coef_ref.shape, 0)
    column = lax.broadcasted_iota(jnp.int32, coef_ref.shape, 1)
    value = jnp.zeros(coef_ref.shape, F32)
    for k, (alpha, beta) in enumerate(((alpha0, beta0), (alpha1, beta1), (alpha2, beta2))):
        value = jnp.where((row == 0) & (column == k), alpha, value)
        value = jnp.where((row == 1) & (column == k), beta, value)
    coef_ref[...] = value


def on_device(wavefunction, left_blocks, right_blocks, charge_shifts, sector_rows):
    sectors, block_rows, columns = wavefunction.shape
    half = block_rows // 2
    n_sec, n_op = lax.axis_size("sec"), lax.axis_size("op")
    assert sectors == 2 and n_sec % 4 == 0 and n_op % 4 == 0
    core_pairs = [(i, i ^ 1) for i in range(n_op)]
    pairs = [(i, i ^ 1) for i in range(n_sec)]
    onward = [(i, i + 2) for i in range(0, n_sec - 2, 2)]
    onward += [(i, i - 2) for i in range(3, n_sec, 2)]
    diagonal = [(i, i + 1) for i in range(1, n_sec - 1, 2)]
    diagonal += [(j, i) for i, j in diagonal]

    def across_cores(value):
        return lax.ppermute(value, "op", core_pairs)

    def flipped_sum(stats, bits):
        for bit in bits:
            stats = stats + lax.ppermute(stats, "sec", [(i, i ^ bit) for i in range(n_sec)])
        return stats

    def flipped_merge(tile, axis, bits):
        for bit in bits:
            flips = [(i, i ^ bit) for i in range(lax.axis_size(axis))]
            arrived = lax.ppermute(tile, axis, flips)
            tile = call(
                functools.partial(merge_kernel, axis, bit), "merge", tile_type, [], tile, arrived
            )
        return tile

    def sum_four(stats, one, two):
        places = range(n_sec * n_op)
        first, second, both = (
            lax.ppermute(stats, ("sec", "op"), [(i, i ^ mask) for i in places])
            for mask in (one, two, one ^ two)
        )
        return (stats + both) + (first + second)

    bits = [1 << k for k in range(n_sec.bit_length() - 1)]

    last_bit = n_op // 2
    half_type = jax.ShapeDtypeStruct((half, columns), BF16)
    quarter_type = jax.ShapeDtypeStruct((half // 2, columns), BF16)
    stats_type = jax.ShapeDtypeStruct((8, 128), F32)
    tile_type = jax.ShapeDtypeStruct((24, 128), F32)
    v_scratch = pltpu.VMEM((6, block_rows, columns), BF16)

    halves = call(
        start_kernel, "start", [half_type] * (2 * sectors), [], sector_rows, wavefunction
    )
    basis = [[(halves[0], halves[1]), (halves[2], halves[3])]]
    pair_0 = lax.ppermute(halves[0], "sec", pairs)
    operators = (charge_shifts, left_blocks, right_blocks)
    others = tuple(across_cores(value) for value in operators)
    stats = []
    hbm = pl.BlockSpec(memory_space=pltpu.HBM)
    left, right = pl.pallas_call(
        stage_kernel,
        name="stage",
        out_shape=[jax.ShapeDtypeStruct(v.shape, v.dtype) for v in operators[1:]],
        in_specs=[hbm] * 2,
        out_specs=[VMEM] * 2,
        scratch_shapes=[pltpu.SemaphoreType.DMA((2,))],
        compiler_params=pltpu.CompilerParams(vmem_limit_bytes=16 << 20),
        cost_estimate=pl.CostEstimate(flops=0, bytes_accessed=0, transcendentals=0),
    )(operators[1], operators[2])
    operators = (charge_shifts, left, right) + others
    pair_0 = after(pair_0, left)

    for product in range(3):
        (mine_0, other_0), (mine_1, other_1) = basis[-1]
        if product:
            pair_0 = lax.ppermute(mine_0, "sec", pairs)
        if product:
            pair_0 = after(pair_0, mine_1)
        else:
            mine_1 = after(mine_1, pair_0)
        if product == 2:
            tile = flipped_merge(after(tile, mine_0), "sec", bits[1:2])
            pair_0 = after(pair_0, tile)
        pair_1 = lax.ppermute(mine_1, "sec", pairs)
        far_0 = lax.ppermute(pair_0, "sec", onward)
        far_1 = lax.ppermute(mine_1, "sec", diagonal)
        if product == 0:
            pair_1 = after(pair_1, far_0)
        if product == 1:
            tile = flipped_merge(flipped_merge(sums, "op", [1]), "sec", bits[:1])
            pair_1 = after(pair_1, tile)
        elif product == 2:
            tile = flipped_merge(after(tile, pair_0), "sec", bits[2:])
            stats.append(tile)
            pair_1 = after(pair_1, tile)
        scalars = (sector_rows, *stats) if product == 2 else ()
        sources = [mine_0, other_0, mine_1, other_1]
        for part in (pair_0, pair_1, far_0, far_1):
            sources += [part, across_cores(part)]
        out, scratch = [half_type], [v_scratch]
        if product == 2:
            out = [quarter_type] * 2
            scratch.append(pltpu.VMEM((half, columns), BF16))
        values = [
            call(
                functools.partial(full_kernel, t), "full", out, scratch,
                *operators, *sources, *scalars,
            )
            for t in range(sectors)
        ]
        image = []
        earlier = []
        for t, parts in enumerate(values):
            bit = 2
            while bit < last_bit:
                flips = [(i, i ^ bit) for i in range(n_op)]
                parts = [
                    call(add_kernel, "add", jax.ShapeDtypeStruct(part.shape, BF16), [], part, lax.ppermute(part, "op", flips))
                    for part in parts
                ]
                bit *= 2
            flips = [(i, i ^ last_bit) for i in range(n_op)]
            arrived = lax.ppermute(parts[-1], "op", flips)
            if t == 0:
                arrived = after(arrived, values[-1][0])
            out = (half_type, half_type, quarter_type)[product]
            needed = () if product == 1 else (*[b[t][0] for b in basis], *stats, *earlier)
            mine, *earlier = call(
                functools.partial(image_kernel, product, t, sectors), "image",
                [out] if product == 1 else [out, stats_type if product else tile_type], [],
                sector_rows, parts[0], arrived, *needed,
            )
            image.append((mine, across_cores(mine)))
            if product == 2:
                other = lax.ppermute(mine, "op", flips)
                image[-1] += (other, across_cores(other))
        basis.append(image)
        if earlier:
            sums = earlier[0]
    sums = sum_four(sum_four(sums, 1, last_bit), n_op, 2 * n_op)
    stats.append(flipped_sum(sums, bits[2:]))

    flat = [h for t in range(sectors) for b in basis for h in b[t]]
    vector_type = jax.ShapeDtypeStruct(wavefunction.shape, BF16)
    coef_type = jax.ShapeDtypeStruct((2, 3), F32)
    vector, coef = call(
        last_kernel, "last", [vector_type, coef_type], [], sector_rows, *flat, *stats
    )
    return vector, coef


def solution(mesh):
    in_specs = (P("sec", None, None), P("op", "sec", None, None), P("op", None, None), P("op"), P())
    out_specs = (P("sec", None, None), P())
    return jax.shard_map(
        on_device, mesh=mesh, in_specs=in_specs, out_specs=out_specs, check_vma=False
    )
```

```python
import functools

import jax
import jax.numpy as jnp
from jax import lax
from jax.experimental import pallas as pl
from jax.experimental.pallas import tpu as pltpu
from jax.sharding import PartitionSpec as P

F32 = jnp.float32
BF16 = jnp.bfloat16
START_SCALE = 2.0**60
VMEM = pl.BlockSpec(memory_space=pltpu.VMEM)
SMEM = pl.BlockSpec(memory_space=pltpu.SMEM)


def call(kernel, name, out, scratch, *operands):
    return pl.pallas_call(
        kernel,
        name=name,
        out_shape=out,
        in_specs=[SMEM if a.dtype == jnp.int32 else VMEM for a in operands],
        out_specs=jax.tree.map(lambda _: VMEM, out),
        scratch_shapes=scratch,
        compiler_params=pltpu.CompilerParams(vmem_limit_bytes=16 << 20),
        cost_estimate=pl.CostEstimate(flops=0, bytes_accessed=0, transcendentals=0),
    )(*operands)


def after(value, *others):
    return lax.optimization_barrier((value, *others))[0]


def my_core():
    return lax.axis_index("op") % 2


def half_of(which, half):
    core = my_core()
    return pl.ds(pl.multiple_of((core if which == 0 else 1 - core) * half, half), half)


def side_of(which, rows, count):
    side = lax.axis_index("op") // (count // 2)
    return pl.ds(pl.multiple_of((side if which == 0 else 1 - side) * rows, rows), rows)


def rows_of(rows_ref, target, sectors):
    return rows_ref[lax.axis_index("sec") * sectors + target]


def live_entries(rows_ref, columns):
    return sum(rows_ref[i] for i in range(rows_ref.shape[0])).astype(F32) * columns


def masked(value, first, rows):
    return jnp.where(lax.broadcasted_iota(jnp.int32, value.shape, 0) + first < rows, value, 0.0)


def inner(stats_ref, row, live):
    return jnp.sum(stats_ref[row : row + 1, :], axis=1, keepdims=True) / live


def write_sums(stats_ref, values, before=None):
    parts = [jnp.zeros((1, 128), F32)] * 8
    for k, value in enumerate(values):
        folded = sum(value[:, i : i + 128] for i in range(0, value.shape[1], 128))
        parts[k] = jnp.sum(folded, axis=0, keepdims=True)
    rows = jnp.concatenate(parts, axis=0)
    stats_ref[...] = rows if before is None else rows + before[...]


def largest(value):
    return jnp.maximum(jnp.max(jnp.abs(value), keepdims=True), 1e-37)


def scaled_sums(pairs):
    sums, lefts, rights = [], [], []
    for left, right in pairs:
        scales = largest(left), largest(right)
        product = (left * (1.0 / scales[0])) * (right * (1.0 / scales[1]))
        folded = sum(product[:, i : i + 128] for i in range(0, product.shape[1], 128))
        sums.append(jnp.sum(folded, axis=0, keepdims=True))
        lefts.append(jnp.broadcast_to(scales[0], (1, 128)))
        rights.append(jnp.broadcast_to(scales[1], (1, 128)))
    fill = [jnp.zeros((1, 128), F32)] * (8 - len(pairs))
    ones = [jnp.full((1, 128), 1e-37, F32)] * (8 - len(pairs))
    return jnp.concatenate(sums + fill + lefts + ones + rights + ones, axis=0)


def merged(a, b):
    left = jnp.maximum(a[8:16], b[8:16])
    right = jnp.maximum(a[16:], b[16:])
    total = sum(t[:8] * (t[8:16] / left) * (t[16:] / right) for t in (a, b))
    return jnp.concatenate([total, left, right], axis=0)


def merge_kernel(axis, bit, own_ref, arrived_ref, out_ref):
    low = lax.axis_index(axis) & bit == 0
    own, arrived = own_ref[...], arrived_ref[...]
    out_ref[...] = merged(jnp.where(low, own, arrived), jnp.where(low, arrived, own))


def first_scalars(tile, live):
    def row(k):
        return (
            jnp.sum(tile[k : k + 1, :], axis=1, keepdims=True) / live,
            tile[8 + k : 9 + k, 0:1],
            tile[16 + k : 17 + k, 0:1],
        )

    square, scale, _ = row(0)
    norm = scale * jnp.sqrt(square)
    cross, image_scale, start_scale = row(1)
    alpha = cross * (image_scale / norm) * (start_scale / norm)
    image_square, image_scale, _ = row(2)
    unit = image_scale / norm
    rest = image_square - (alpha / unit) * (alpha / unit)
    return norm, alpha, unit * jnp.sqrt(jnp.maximum(rest, 0.0))


def form(gram, a, b):
    return sum(a[i] * b[j] * gram[min(i, j)][max(i, j)] for i in a for j in b)


def plus(scale, *terms):
    out = {}
    for c, vector in terms:
        for i, v in vector.items():
            out[i] = out[i] + c * v if i in out else c * v
    return {i: scale * v for i, v in out.items()}


def start_kernel(rows_ref, x_ref, *refs):
    sectors, block_rows, _ = x_ref.shape
    for t in range(sectors):
        for which in range(2):
            part = half_of(which, block_rows // 2)
            value = masked(
                x_ref[t, part, :].astype(F32), part.start, rows_of(rows_ref, t, sectors)
            )
            refs[2 * t + which][...] = (value * START_SCALE).astype(BF16)


def place_of(k):
    pair = jnp.where(lax.axis_index("sec") % 2 == 0, 2, 0)
    return (1, pair, 2 - pair)[k]


def stage_kernel(left_ref, right_ref, left_out, right_out, sems):
    copies = [
        pltpu.make_async_copy(left_ref, left_out, sems.at[0]),
        pltpu.make_async_copy(right_ref, right_out, sems.at[1]),
    ]
    for copy in copies:
        copy.start()
    for copy in copies:
        copy.wait()


def gather_sources(slots, refs, scalars, v_ref):
    half = refs[0].shape[0]
    if scalars:
        rows_ref, tile_ref = scalars
        norm, _, beta = first_scalars(tile_ref, live_entries(rows_ref, v_ref.shape[2]))
        scale = 1.0 / (norm * beta)
    for i, slot in enumerate(slots):
        for which in range(2):
            value = refs[2 * i + which][...]
            if scalars:
                value = (value.astype(F32) * scale).astype(BF16)
            v_ref[slot, half_of(which, half), :] = value


def full_kernel(target, *refs):
    operators, sources, rest = refs[:6], refs[6:18], refs[18:]
    if len(rest) == 2:
        scalars, outs, v_ref = (), rest[:1], rest[1]
    else:
        *scalars, keep_ref, give_ref, v_ref, total_ref = rest
        outs = keep_ref, give_ref
    gather_sources((0, 1, 2, 3, 4, 5), sources, scalars, v_ref)
    far = place_of(2)
    half = sources[0].shape[0]
    total = None
    for shifts_ref, left_ref, right_ref in (operators[:3], operators[3:]):
        for w in range(left_ref.shape[0]):
            offset = target - shifts_ref[w]
            place = (offset >> 1) + 1
            kind = jnp.where(place == 1, 0, jnp.where(place == far, 4, 2))
            part = jnp.dot(
                left_ref[w, target, half_of(0, half), :],
                v_ref[kind + (offset & 1)],
                preferred_element_type=F32,
            ).astype(BF16)
            term = jnp.dot(part, right_ref[w], preferred_element_type=F32)
            total = term if total is None else total + term
    if len(outs) == 1:
        outs[0][...] = total.astype(BF16)
    else:
        total_ref[...] = total.astype(BF16)
        for which, ref in enumerate(outs):
            ref[...] = total_ref[side_of(which, half // 2, lax.axis_size("op")), :]


def add_kernel(a_ref, b_ref, out_ref):
    out_ref[...] = (a_ref[...].astype(F32) + b_ref[...].astype(F32)).astype(BF16)


def image_kernel(product, target, sectors, rows_ref, a_ref, b_ref, *refs):
    out_ref = refs[-2] if product != 1 else refs[-1]
    half, columns = out_ref.shape
    value = a_ref[...].astype(F32) + b_ref[...].astype(F32)
    rows = rows_of(rows_ref, target, sectors)
    first_row = my_core() * half
    part = pl.ds(0, half)
    if product == 2:
        part = side_of(0, half, lax.axis_size("op"))
        first_row = 2 * first_row + part.start
    value = masked(value, first_row, rows)
    if product == 1:
        out_ref[...] = value.astype(BF16)
        return
    stats_ref = refs[-1]
    basis = [r[part, :].astype(F32) for r in refs[: product + 1]]
    if product == 0:
        value = value.astype(BF16)
        out_ref[...] = value
        value = value.astype(F32)
        tile = scaled_sums([(basis[0], basis[0]), (value, basis[0]), (value, value)])
        stats_ref[...] = merged(refs[1][...], tile) if target else tile
        return
    tile_ref, before = refs[product + 1], refs[product + 2] if target else None
    norm, alpha, beta = first_scalars(tile_ref, live_entries(rows_ref, columns))
    zeroth, image, second = (block * (1.0 / norm) for block in basis)
    scale = 1.0 / beta
    first = (image - alpha * zeroth) * scale
    value = (value - (alpha * scale) * second) * scale
    second = (second - alpha * image) * scale
    value = value.astype(BF16)
    out_ref[...] = value
    value = value.astype(F32)
    known = [second * second, second * first, second * zeroth]
    write_sums(stats_ref, known + [value * v for v in (value, second, first, zeroth)], before)


def last_kernel(rows_ref, *refs):
    out_ref, coef_ref = refs[-2:]
    tile_ref, last_stats = refs[-4:-2]
    sectors, block_rows, columns = out_ref.shape
    live = live_entries(rows_ref, columns)
    norm, alpha0, beta0 = first_scalars(tile_ref, live)
    one, none = jnp.ones_like(norm), jnp.zeros_like(norm)
    w11, w1q1, w1q0, zz, zw1, zq1, zq0 = (inner(last_stats, k, live) for k in range(7))
    gram = [[one, none, w1q0, zq0], [None, one, w1q1, zq1], [None, None, w11, zw1], [None] * 3 + [zz]]
    q0, q1, w1 = {0: one}, {1: one}, {2: one}
    alpha1 = w1q1
    r1 = plus(one, (one, w1), (-alpha1, q1), (-beta0, q0))
    beta1 = jnp.sqrt(jnp.maximum(form(gram, r1, r1), 0.0))
    q2 = plus(1.0 / beta1, (one, r1))
    w0 = {0: alpha0, 1: beta0}
    w2 = plus(1.0 / beta1, (beta0, {3: one}), (-alpha1, w1), (-beta0, w0))
    alpha2 = form(gram, q2, w2)
    r2 = plus(one, (one, w2), (-alpha2, q2), (-beta1, q1))
    beta2 = jnp.sqrt(jnp.maximum(form(gram, r2, r2), 0.0))
    q3 = plus(1.0 / beta2, (one, r2))
    c1 = q3[1] / beta0
    c2 = q3[2] / beta0
    coefs = [(q3[0] - alpha0 * c1) / norm, (c1 - alpha0 * c2) / norm, c2 / norm, q3[3]]
    quarter = block_rows // 4
    chunk = 32
    for t in range(sectors):
        sector_refs = refs[10 * t : 10 * t + 10]
        for which in range(2):
            start = half_of(which, 2 * quarter).start
            for side in range(2):
                part = side_of(side, quarter, lax.axis_size("op"))
                for r in range(0, quarter, chunk):
                    here = pl.ds(pl.multiple_of(part.start + r, chunk), chunk)
                    blocks = [sector_refs[2 * k + which][here, :] for k in range(3)]
                    blocks.append(sector_refs[6 + 2 * side + which][r : r + chunk, :])
                    vector = sum(c * block.astype(F32) for c, block in zip(coefs, blocks))
                    rows = pl.ds(pl.multiple_of(start + part.start + r, chunk), chunk)
                    out_ref[t, rows, :] = vector.astype(BF16)
    row = lax.broadcasted_iota(jnp.int32, coef_ref.shape, 0)
    column = lax.broadcasted_iota(jnp.int32, coef_ref.shape, 1)
    value = jnp.zeros(coef_ref.shape, F32)
    for k, (alpha, beta) in enumerate(((alpha0, beta0), (alpha1, beta1), (alpha2, beta2))):
        value = jnp.where((row == 0) & (column == k), alpha, value)
        value = jnp.where((row == 1) & (column == k), beta, value)
    coef_ref[...] = value


def on_device(wavefunction, left_blocks, right_blocks, charge_shifts, sector_rows):
    sectors, block_rows, columns = wavefunction.shape
    half = block_rows // 2
    n_sec, n_op = lax.axis_size("sec"), lax.axis_size("op")
    assert sectors == 2 and n_sec % 4 == 0 and n_op % 4 == 0
    core_pairs = [(i, i ^ 1) for i in range(n_op)]
    pairs = [(i, i ^ 1) for i in range(n_sec)]
    onward = [(i, i + 2) for i in range(0, n_sec - 2, 2)]
    onward += [(i, i - 2) for i in range(3, n_sec, 2)]
    diagonal = [(i, i + 1) for i in range(1, n_sec - 1, 2)]
    diagonal += [(j, i) for i, j in diagonal]

    def across_cores(value):
        return lax.ppermute(value, "op", core_pairs)

    def flipped_sum(stats, bits):
        for bit in bits:
            stats = stats + lax.ppermute(stats, "sec", [(i, i ^ bit) for i in range(n_sec)])
        return stats

    def flipped_merge(tile, axis, bits):
        for bit in bits:
            flips = [(i, i ^ bit) for i in range(lax.axis_size(axis))]
            arrived = lax.ppermute(tile, axis, flips)
            tile = call(
                functools.partial(merge_kernel, axis, bit), "merge", tile_type, [], tile, arrived
            )
        return tile

    def sum_four(stats, one, two):
        places = range(n_sec * n_op)
        first, second, both = (
            lax.ppermute(stats, ("sec", "op"), [(i, i ^ mask) for i in places])
            for mask in (one, two, one ^ two)
        )
        return (stats + both) + (first + second)

    bits = [1 << k for k in range(n_sec.bit_length() - 1)]

    last_bit = n_op // 2
    half_type = jax.ShapeDtypeStruct((half, columns), BF16)
    quarter_type = jax.ShapeDtypeStruct((half // 2, columns), BF16)
    stats_type = jax.ShapeDtypeStruct((8, 128), F32)
    tile_type = jax.ShapeDtypeStruct((24, 128), F32)
    v_scratch = pltpu.VMEM((6, block_rows, columns), BF16)

    halves = call(
        start_kernel, "start", [half_type] * (2 * sectors), [], sector_rows, wavefunction
    )
    basis = [[(halves[0], halves[1]), (halves[2], halves[3])]]
    pair_0 = lax.ppermute(halves[0], "sec", pairs)
    operators = (charge_shifts, left_blocks, right_blocks)
    others = tuple(across_cores(value) for value in operators)
    stats = []
    hbm = pl.BlockSpec(memory_space=pltpu.HBM)
    left, right = pl.pallas_call(
        stage_kernel,
        name="stage",
        out_shape=[jax.ShapeDtypeStruct(v.shape, v.dtype) for v in operators[1:]],
        in_specs=[hbm] * 2,
        out_specs=[VMEM] * 2,
        scratch_shapes=[pltpu.SemaphoreType.DMA((2,))],
        compiler_params=pltpu.CompilerParams(vmem_limit_bytes=16 << 20),
        cost_estimate=pl.CostEstimate(flops=0, bytes_accessed=0, transcendentals=0),
    )(operators[1], operators[2])
    operators = (charge_shifts, left, right) + others
    pair_0 = after(pair_0, left)

    for product in range(3):
        (mine_0, other_0), (mine_1, other_1) = basis[-1]
        if product:
            pair_0 = lax.ppermute(mine_0, "sec", pairs)
        if product:
            pair_0 = after(pair_0, mine_1)
        else:
            mine_1 = after(mine_1, pair_0)
        if product == 2:
            tile = flipped_merge(after(tile, mine_0), "sec", bits[1:2])
            pair_0 = after(pair_0, tile)
        pair_1 = lax.ppermute(mine_1, "sec", pairs)
        far_0 = lax.ppermute(pair_0, "sec", onward)
        far_1 = lax.ppermute(mine_1, "sec", diagonal)
        pair_1 = after(pair_1, far_0)
        if product == 1:
            tile = flipped_merge(flipped_merge(sums, "op", [1]), "sec", bits[:1])
            pair_1 = after(pair_1, tile)
        elif product == 2:
            tile = flipped_merge(after(tile, pair_0), "sec", bits[2:])
            stats.append(tile)
            pair_1 = after(pair_1, tile)
        scalars = (sector_rows, *stats) if product == 2 else ()
        sources = [mine_0, other_0, mine_1, other_1]
        for part in (pair_0, pair_1, far_0, far_1):
            sources += [part, across_cores(part)]
        out, scratch = [half_type], [v_scratch]
        if product == 2:
            out = [quarter_type] * 2
            scratch.append(pltpu.VMEM((half, columns), BF16))
        values = [
            call(
                functools.partial(full_kernel, t), "full", out, scratch,
                *operators, *sources, *scalars,
            )
            for t in range(sectors)
        ]
        image = []
        earlier = []
        for t, parts in enumerate(values):
            bit = 2
            while bit < last_bit:
                flips = [(i, i ^ bit) for i in range(n_op)]
                parts = [
                    call(add_kernel, "add", jax.ShapeDtypeStruct(part.shape, BF16), [], part, lax.ppermute(part, "op", flips))
                    for part in parts
                ]
                bit *= 2
            flips = [(i, i ^ last_bit) for i in range(n_op)]
            arrived = lax.ppermute(parts[-1], "op", flips)
            if t == 0:
                arrived = after(arrived, values[-1][0])
            out = (half_type, half_type, quarter_type)[product]
            needed = () if product == 1 else (*[b[t][0] for b in basis], *stats, *earlier)
            mine, *earlier = call(
                functools.partial(image_kernel, product, t, sectors), "image",
                [out] if product == 1 else [out, stats_type if product else tile_type], [],
                sector_rows, parts[0], arrived, *needed,
            )
            image.append((mine, across_cores(mine)))
            if product == 2:
                other = lax.ppermute(mine, "op", flips)
                image[-1] += (other, across_cores(other))
        basis.append(image)
        if earlier:
            sums = earlier[0]
    sums = sum_four(sum_four(sums, 1, last_bit), n_op, 2 * n_op)
    stats.append(flipped_sum(sums, bits[2:]))

    flat = [h for t in range(sectors) for b in basis for h in b[t]]
    vector_type = jax.ShapeDtypeStruct(wavefunction.shape, BF16)
    coef_type = jax.ShapeDtypeStruct((2, 3), F32)
    vector, coef = call(
        last_kernel, "last", [vector_type, coef_type], [], sector_rows, *flat, *stats
    )
    return vector, coef


def solution(mesh):
    in_specs = (P("sec", None, None), P("op", "sec", None, None), P("op", None, None), P("op"), P())
    out_specs = (P("sec", None, None), P())
    return jax.shard_map(
        on_device, mesh=mesh, in_specs=in_specs, out_specs=out_specs, check_vma=False
    )
```

```python
import functools

import jax
import jax.numpy as jnp
from jax import lax
from jax.experimental import pallas as pl
from jax.experimental.pallas import tpu as pltpu
from jax.sharding import PartitionSpec as P

F32 = jnp.float32
BF16 = jnp.bfloat16
START_SCALE = 2.0**60
VMEM = pl.BlockSpec(memory_space=pltpu.VMEM)
SMEM = pl.BlockSpec(memory_space=pltpu.SMEM)


def call(kernel, name, out, scratch, *operands):
    return pl.pallas_call(
        kernel,
        name=name,
        out_shape=out,
        in_specs=[SMEM if a.dtype == jnp.int32 else VMEM for a in operands],
        out_specs=jax.tree.map(lambda _: VMEM, out),
        scratch_shapes=scratch,
        compiler_params=pltpu.CompilerParams(vmem_limit_bytes=16 << 20),
        cost_estimate=pl.CostEstimate(flops=0, bytes_accessed=0, transcendentals=0),
    )(*operands)


def after(value, *others):
    return lax.optimization_barrier((value, *others))[0]


def my_core():
    return lax.axis_index("op") % 2


def half_of(which, half):
    core = my_core()
    return pl.ds(pl.multiple_of((core if which == 0 else 1 - core) * half, half), half)


def side_of(which, rows, count):
    side = lax.axis_index("op") // (count // 2)
    return pl.ds(pl.multiple_of((side if which == 0 else 1 - side) * rows, rows), rows)


def rows_of(rows_ref, target, sectors):
    return rows_ref[lax.axis_index("sec") * sectors + target]


def live_entries(rows_ref, columns):
    return sum(rows_ref[i] for i in range(rows_ref.shape[0])).astype(F32) * columns


def masked(value, first, rows):
    return jnp.where(lax.broadcasted_iota(jnp.int32, value.shape, 0) + first < rows, value, 0.0)


def inner(stats_ref, row, live):
    return jnp.sum(stats_ref[row : row + 1, :], axis=1, keepdims=True) / live


def write_sums(stats_ref, values, before=None):
    parts = [jnp.zeros((1, 128), F32)] * 8
    for k, value in enumerate(values):
        folded = sum(value[:, i : i + 128] for i in range(0, value.shape[1], 128))
        parts[k] = jnp.sum(folded, axis=0, keepdims=True)
    rows = jnp.concatenate(parts, axis=0)
    stats_ref[...] = rows if before is None else rows + before[...]


def largest(value):
    return jnp.maximum(jnp.max(jnp.abs(value), keepdims=True), 1e-37)


def scaled_sums(pairs):
    sums, lefts, rights = [], [], []
    for left, right in pairs:
        scales = largest(left), largest(right)
        product = (left * (1.0 / scales[0])) * (right * (1.0 / scales[1]))
        folded = sum(product[:, i : i + 128] for i in range(0, product.shape[1], 128))
        sums.append(jnp.sum(folded, axis=0, keepdims=True))
        lefts.append(jnp.broadcast_to(scales[0], (1, 128)))
        rights.append(jnp.broadcast_to(scales[1], (1, 128)))
    fill = [jnp.zeros((1, 128), F32)] * (8 - len(pairs))
    ones = [jnp.full((1, 128), 1e-37, F32)] * (8 - len(pairs))
    return jnp.concatenate(sums + fill + lefts + ones + rights + ones, axis=0)


def merged(a, b):
    left = jnp.maximum(a[8:16], b[8:16])
    right = jnp.maximum(a[16:], b[16:])
    total = sum(t[:8] * (t[8:16] / left) * (t[16:] / right) for t in (a, b))
    return jnp.concatenate([total, left, right], axis=0)


def merge_kernel(axis, bit, own_ref, arrived_ref, out_ref):
    low = lax.axis_index(axis) & bit == 0
    own, arrived = own_ref[...], arrived_ref[...]
    out_ref[...] = merged(jnp.where(low, own, arrived), jnp.where(low, arrived, own))


def first_scalars(tile, live):
    def row(k):
        return (
            jnp.sum(tile[k : k + 1, :], axis=1, keepdims=True) / live,
            tile[8 + k : 9 + k, 0:1],
            tile[16 + k : 17 + k, 0:1],
        )

    square, scale, _ = row(0)
    norm = scale * jnp.sqrt(square)
    cross, image_scale, start_scale = row(1)
    alpha = cross * (image_scale / norm) * (start_scale / norm)
    image_square, image_scale, _ = row(2)
    unit = image_scale / norm
    rest = image_square - (alpha / unit) * (alpha / unit)
    return norm, alpha, unit * jnp.sqrt(jnp.maximum(rest, 0.0))


def input_scale(norm, beta):
    return (1.0 / (norm * beta)).astype(BF16)


def form(gram, a, b):
    return sum(a[i] * b[j] * gram[min(i, j)][max(i, j)] for i in a for j in b)


def plus(scale, *terms):
    out = {}
    for c, vector in terms:
        for i, v in vector.items():
            out[i] = out[i] + c * v if i in out else c * v
    return {i: scale * v for i, v in out.items()}


def start_kernel(rows_ref, x_ref, *refs):
    sectors, block_rows, _ = x_ref.shape
    for t in range(sectors):
        for which in range(2):
            part = half_of(which, block_rows // 2)
            value = masked(
                x_ref[t, part, :].astype(F32), part.start, rows_of(rows_ref, t, sectors)
            )
            refs[2 * t + which][...] = (value * START_SCALE).astype(BF16)


def place_of(k):
    pair = jnp.where(lax.axis_index("sec") % 2 == 0, 2, 0)
    return (1, pair, 2 - pair)[k]


def stage_kernel(left_ref, right_ref, left_out, right_out, sems):
    copies = [
        pltpu.make_async_copy(left_ref, left_out, sems.at[0]),
        pltpu.make_async_copy(right_ref, right_out, sems.at[1]),
    ]
    for copy in copies:
        copy.start()
    for copy in copies:
        copy.wait()


def gather_sources(slots, refs, scalars, v_ref):
    half = refs[0].shape[0]
    if scalars:
        rows_ref, tile_ref = scalars
        norm, _, beta = first_scalars(tile_ref, live_entries(rows_ref, v_ref.shape[2]))
        scale = input_scale(norm, beta)
    for i, slot in enumerate(slots):
        for which in range(2):
            value = refs[2 * i + which][...]
            if scalars:
                value = value * scale
            v_ref[slot, half_of(which, half), :] = value


def full_kernel(target, *refs):
    operators, sources, rest = refs[:6], refs[6:18], refs[18:]
    if len(rest) == 2:
        scalars, outs, v_ref = (), rest[:1], rest[1]
    else:
        *scalars, keep_ref, give_ref, v_ref, total_ref = rest
        outs = keep_ref, give_ref
    gather_sources((0, 1, 2, 3, 4, 5), sources, scalars, v_ref)
    far = place_of(2)
    half = sources[0].shape[0]
    total = None
    for shifts_ref, left_ref, right_ref in (operators[:3], operators[3:]):
        for w in range(left_ref.shape[0]):
            offset = target - shifts_ref[w]
            place = (offset >> 1) + 1
            kind = jnp.where(place == 1, 0, jnp.where(place == far, 4, 2))
            part = jnp.dot(
                left_ref[w, target, half_of(0, half), :],
                v_ref[kind + (offset & 1)],
                preferred_element_type=F32,
            ).astype(BF16)
            term = jnp.dot(part, right_ref[w], preferred_element_type=F32)
            total = term if total is None else total + term
    if len(outs) == 1:
        outs[0][...] = total.astype(BF16)
    else:
        total_ref[...] = total.astype(BF16)
        for which, ref in enumerate(outs):
            ref[...] = total_ref[side_of(which, half // 2, lax.axis_size("op")), :]


def add_kernel(a_ref, b_ref, out_ref):
    out_ref[...] = (a_ref[...].astype(F32) + b_ref[...].astype(F32)).astype(BF16)


def image_kernel(product, target, sectors, rows_ref, a_ref, b_ref, *refs):
    out_ref = refs[-2] if product != 1 else refs[-1]
    half, columns = out_ref.shape
    value = a_ref[...].astype(F32) + b_ref[...].astype(F32)
    rows = rows_of(rows_ref, target, sectors)
    first_row = my_core() * half
    part = pl.ds(0, half)
    if product == 2:
        part = side_of(0, half, lax.axis_size("op"))
        first_row = 2 * first_row + part.start
    value = masked(value, first_row, rows)
    if product == 1:
        out_ref[...] = value.astype(BF16)
        return
    stats_ref = refs[-1]
    basis = [r[part, :].astype(F32) for r in refs[: product + 1]]
    if product == 0:
        value = value.astype(BF16)
        out_ref[...] = value
        value = value.astype(F32)
        tile = scaled_sums([(basis[0], basis[0]), (value, basis[0]), (value, value)])
        stats_ref[...] = merged(refs[1][...], tile) if target else tile
        return
    tile_ref, before = refs[product + 1], refs[product + 2] if target else None
    norm, alpha, beta = first_scalars(tile_ref, live_entries(rows_ref, columns))
    zeroth, image, second = (block * (1.0 / norm) for block in basis)
    scale = 1.0 / beta
    first = (image - alpha * zeroth) * scale
    value = value * (scale / (input_scale(norm, beta).astype(F32) * norm))
    value = (value - (alpha * scale) * second) * scale
    second = (second - alpha * image) * scale
    value = value.astype(BF16)
    out_ref[...] = value
    value = value.astype(F32)
    known = [second * second, second * first, second * zeroth]
    write_sums(stats_ref, known + [value * v for v in (value, second, first, zeroth)], before)


def last_kernel(rows_ref, *refs):
    out_ref, coef_ref = refs[-2:]
    tile_ref, last_stats = refs[-4:-2]
    sectors, block_rows, columns = out_ref.shape
    live = live_entries(rows_ref, columns)
    norm, alpha0, beta0 = first_scalars(tile_ref, live)
    one, none = jnp.ones_like(norm), jnp.zeros_like(norm)
    w11, w1q1, w1q0, zz, zw1, zq1, zq0 = (inner(last_stats, k, live) for k in range(7))
    gram = [[one, none, w1q0, zq0], [None, one, w1q1, zq1], [None, None, w11, zw1], [None] * 3 + [zz]]
    q0, q1, w1 = {0: one}, {1: one}, {2: one}
    alpha1 = w1q1
    r1 = plus(one, (one, w1), (-alpha1, q1), (-beta0, q0))
    beta1 = jnp.sqrt(jnp.maximum(form(gram, r1, r1), 0.0))
    q2 = plus(1.0 / beta1, (one, r1))
    w0 = {0: alpha0, 1: beta0}
    w2 = plus(1.0 / beta1, (beta0, {3: one}), (-alpha1, w1), (-beta0, w0))
    alpha2 = form(gram, q2, w2)
    r2 = plus(one, (one, w2), (-alpha2, q2), (-beta1, q1))
    beta2 = jnp.sqrt(jnp.maximum(form(gram, r2, r2), 0.0))
    q3 = plus(1.0 / beta2, (one, r2))
    c1 = q3[1] / beta0
    c2 = q3[2] / beta0
    coefs = [(q3[0] - alpha0 * c1) / norm, (c1 - alpha0 * c2) / norm, c2 / norm, q3[3]]
    quarter = block_rows // 4
    chunk = 32
    for t in range(sectors):
        sector_refs = refs[10 * t : 10 * t + 10]
        for which in range(2):
            start = half_of(which, 2 * quarter).start
            for side in range(2):
                part = side_of(side, quarter, lax.axis_size("op"))
                for r in range(0, quarter, chunk):
                    here = pl.ds(pl.multiple_of(part.start + r, chunk), chunk)
                    blocks = [sector_refs[2 * k + which][here, :] for k in range(3)]
                    blocks.append(sector_refs[6 + 2 * side + which][r : r + chunk, :])
                    vector = sum(c * block.astype(F32) for c, block in zip(coefs, blocks))
                    rows = pl.ds(pl.multiple_of(start + part.start + r, chunk), chunk)
                    out_ref[t, rows, :] = vector.astype(BF16)
    row = lax.broadcasted_iota(jnp.int32, coef_ref.shape, 0)
    column = lax.broadcasted_iota(jnp.int32, coef_ref.shape, 1)
    value = jnp.zeros(coef_ref.shape, F32)
    for k, (alpha, beta) in enumerate(((alpha0, beta0), (alpha1, beta1), (alpha2, beta2))):
        value = jnp.where((row == 0) & (column == k), alpha, value)
        value = jnp.where((row == 1) & (column == k), beta, value)
    coef_ref[...] = value


def on_device(wavefunction, left_blocks, right_blocks, charge_shifts, sector_rows):
    sectors, block_rows, columns = wavefunction.shape
    half = block_rows // 2
    n_sec, n_op = lax.axis_size("sec"), lax.axis_size("op")
    assert sectors == 2 and n_sec % 4 == 0 and n_op % 4 == 0
    core_pairs = [(i, i ^ 1) for i in range(n_op)]
    pairs = [(i, i ^ 1) for i in range(n_sec)]
    onward = [(i, i + 2) for i in range(0, n_sec - 2, 2)]
    onward += [(i, i - 2) for i in range(3, n_sec, 2)]
    diagonal = [(i, i + 1) for i in range(1, n_sec - 1, 2)]
    diagonal += [(j, i) for i, j in diagonal]

    def across_cores(value):
        return lax.ppermute(value, "op", core_pairs)

    def flipped_sum(stats, bits):
        for bit in bits:
            stats = stats + lax.ppermute(stats, "sec", [(i, i ^ bit) for i in range(n_sec)])
        return stats

    def flipped_merge(tile, axis, bits):
        for bit in bits:
            flips = [(i, i ^ bit) for i in range(lax.axis_size(axis))]
            arrived = lax.ppermute(tile, axis, flips)
            tile = call(
                functools.partial(merge_kernel, axis, bit), "merge", tile_type, [], tile, arrived
            )
        return tile

    def sum_four(stats, one, two):
        places = range(n_sec * n_op)
        first, second, both = (
            lax.ppermute(stats, ("sec", "op"), [(i, i ^ mask) for i in places])
            for mask in (one, two, one ^ two)
        )
        return (stats + both) + (first + second)

    bits = [1 << k for k in range(n_sec.bit_length() - 1)]

    last_bit = n_op // 2
    half_type = jax.ShapeDtypeStruct((half, columns), BF16)
    quarter_type = jax.ShapeDtypeStruct((half // 2, columns), BF16)
    stats_type = jax.ShapeDtypeStruct((8, 128), F32)
    tile_type = jax.ShapeDtypeStruct((24, 128), F32)
    v_scratch = pltpu.VMEM((6, block_rows, columns), BF16)

    halves = call(
        start_kernel, "start", [half_type] * (2 * sectors), [], sector_rows, wavefunction
    )
    basis = [[(halves[0], halves[1]), (halves[2], halves[3])]]
    pair_0 = lax.ppermute(halves[0], "sec", pairs)
    operators = (charge_shifts, left_blocks, right_blocks)
    others = tuple(across_cores(value) for value in operators)
    stats = []
    hbm = pl.BlockSpec(memory_space=pltpu.HBM)
    left, right = pl.pallas_call(
        stage_kernel,
        name="stage",
        out_shape=[jax.ShapeDtypeStruct(v.shape, v.dtype) for v in operators[1:]],
        in_specs=[hbm] * 2,
        out_specs=[VMEM] * 2,
        scratch_shapes=[pltpu.SemaphoreType.DMA((2,))],
        compiler_params=pltpu.CompilerParams(vmem_limit_bytes=16 << 20),
        cost_estimate=pl.CostEstimate(flops=0, bytes_accessed=0, transcendentals=0),
    )(operators[1], operators[2])
    operators = (charge_shifts, left, right) + others
    pair_0 = after(pair_0, left)

    for product in range(3):
        (mine_0, other_0), (mine_1, other_1) = basis[-1]
        if product:
            pair_0 = lax.ppermute(mine_0, "sec", pairs)
        if product:
            pair_0 = after(pair_0, mine_1)
        else:
            mine_1 = after(mine_1, pair_0)
        if product == 2:
            tile = flipped_merge(after(tile, mine_0), "sec", bits[1:2])
            pair_0 = after(pair_0, tile)
        pair_1 = lax.ppermute(mine_1, "sec", pairs)
        far_0 = lax.ppermute(pair_0, "sec", onward)
        far_1 = lax.ppermute(mine_1, "sec", diagonal)
        pair_1 = after(pair_1, far_0)
        if product == 1:
            tile = flipped_merge(flipped_merge(sums, "op", [1]), "sec", bits[:1])
            pair_1 = after(pair_1, tile)
        elif product == 2:
            tile = flipped_merge(after(tile, pair_0), "sec", bits[2:])
            stats.append(tile)
            pair_1 = after(pair_1, tile)
        scalars = (sector_rows, *stats) if product == 2 else ()
        sources = [mine_0, other_0, mine_1, other_1]
        for part in (pair_0, pair_1, far_0, far_1):
            sources += [part, across_cores(part)]
        out, scratch = [half_type], [v_scratch]
        if product == 2:
            out = [quarter_type] * 2
            scratch.append(pltpu.VMEM((half, columns), BF16))
        values = [
            call(
                functools.partial(full_kernel, t), "full", out, scratch,
                *operators, *sources, *scalars,
            )
            for t in range(sectors)
        ]
        image = []
        earlier = []
        for t, parts in enumerate(values):
            bit = 2
            while bit < last_bit:
                flips = [(i, i ^ bit) for i in range(n_op)]
                parts = [
                    call(add_kernel, "add", jax.ShapeDtypeStruct(part.shape, BF16), [], part, lax.ppermute(part, "op", flips))
                    for part in parts
                ]
                bit *= 2
            flips = [(i, i ^ last_bit) for i in range(n_op)]
            arrived = lax.ppermute(parts[-1], "op", flips)
            if t == 0:
                arrived = after(arrived, values[-1][0])
            out = (half_type, half_type, quarter_type)[product]
            needed = () if product == 1 else (*[b[t][0] for b in basis], *stats, *earlier)
            mine, *earlier = call(
                functools.partial(image_kernel, product, t, sectors), "image",
                [out] if product == 1 else [out, stats_type if product else tile_type], [],
                sector_rows, parts[0], arrived, *needed,
            )
            image.append((mine, across_cores(mine)))
            if product == 2:
                other = lax.ppermute(mine, "op", flips)
                image[-1] += (other, across_cores(other))
        basis.append(image)
        if earlier:
            sums = earlier[0]
    sums = sum_four(sum_four(sums, 1, last_bit), n_op, 2 * n_op)
    stats.append(flipped_sum(sums, bits[2:]))

    flat = [h for t in range(sectors) for b in basis for h in b[t]]
    vector_type = jax.ShapeDtypeStruct(wavefunction.shape, BF16)
    coef_type = jax.ShapeDtypeStruct((2, 3), F32)
    vector, coef = call(
        last_kernel, "last", [vector_type, coef_type], [], sector_rows, *flat, *stats
    )
    return vector, coef


def solution(mesh):
    in_specs = (P("sec", None, None), P("op", "sec", None, None), P("op", None, None), P("op"), P())
    out_specs = (P("sec", None, None), P())
    return jax.shard_map(
        on_device, mesh=mesh, in_specs=in_specs, out_specs=out_specs, check_vma=False
    )
```

```python
import functools

import jax
import jax.numpy as jnp
from jax import lax
from jax.experimental import pallas as pl
from jax.experimental.pallas import tpu as pltpu
from jax.sharding import PartitionSpec as P

F32 = jnp.float32
BF16 = jnp.bfloat16
START_SCALE = 2.0**60
VMEM = pl.BlockSpec(memory_space=pltpu.VMEM)
SMEM = pl.BlockSpec(memory_space=pltpu.SMEM)


def call(kernel, name, out, scratch, *operands):
    return pl.pallas_call(
        kernel,
        name=name,
        out_shape=out,
        in_specs=[SMEM if a.dtype == jnp.int32 else VMEM for a in operands],
        out_specs=jax.tree.map(lambda _: VMEM, out),
        scratch_shapes=scratch,
        compiler_params=pltpu.CompilerParams(vmem_limit_bytes=16 << 20),
        cost_estimate=pl.CostEstimate(flops=0, bytes_accessed=0, transcendentals=0),
    )(*operands)


def after(value, *others):
    return lax.optimization_barrier((value, *others))[0]


def my_core():
    return lax.axis_index("op") % 2


def half_of(which, half):
    core = my_core()
    return pl.ds(pl.multiple_of((core if which == 0 else 1 - core) * half, half), half)


def side_of(which, rows, count):
    side = lax.axis_index("op") // (count // 2)
    return pl.ds(pl.multiple_of((side if which == 0 else 1 - side) * rows, rows), rows)


def rows_of(rows_ref, target, sectors):
    return rows_ref[lax.axis_index("sec") * sectors + target]


def live_entries(rows_ref, columns):
    return sum(rows_ref[i] for i in range(rows_ref.shape[0])).astype(F32) * columns


def masked(value, first, rows):
    return jnp.where(lax.broadcasted_iota(jnp.int32, value.shape, 0) + first < rows, value, 0.0)


def inner(stats_ref, row, live):
    return jnp.sum(stats_ref[row : row + 1, :], axis=1, keepdims=True) / live


def write_sums(stats_ref, values, before=None):
    parts = [jnp.zeros((1, 128), F32)] * 8
    for k, value in enumerate(values):
        folded = sum(value[:, i : i + 128] for i in range(0, value.shape[1], 128))
        parts[k] = jnp.sum(folded, axis=0, keepdims=True)
    rows = jnp.concatenate(parts, axis=0)
    stats_ref[...] = rows if before is None else rows + before[...]


def largest(value):
    return jnp.maximum(jnp.max(jnp.abs(value), keepdims=True), 1e-37)


def scaled_sums(pairs):
    sums, lefts, rights = [], [], []
    for left, right in pairs:
        scales = largest(left), largest(right)
        product = (left * (1.0 / scales[0])) * (right * (1.0 / scales[1]))
        folded = sum(product[:, i : i + 128] for i in range(0, product.shape[1], 128))
        sums.append(jnp.sum(folded, axis=0, keepdims=True))
        lefts.append(jnp.broadcast_to(scales[0], (1, 128)))
        rights.append(jnp.broadcast_to(scales[1], (1, 128)))
    fill = [jnp.zeros((1, 128), F32)] * (8 - len(pairs))
    ones = [jnp.full((1, 128), 1e-37, F32)] * (8 - len(pairs))
    return jnp.concatenate(sums + fill + lefts + ones + rights + ones, axis=0)


def merged(a, b):
    left = jnp.maximum(a[8:16], b[8:16])
    right = jnp.maximum(a[16:], b[16:])
    total = sum(t[:8] * (t[8:16] / left) * (t[16:] / right) for t in (a, b))
    return jnp.concatenate([total, left, right], axis=0)


def merge_kernel(axis, bit, own_ref, arrived_ref, out_ref):
    low = lax.axis_index(axis) & bit == 0
    own, arrived = own_ref[...], arrived_ref[...]
    out_ref[...] = merged(jnp.where(low, own, arrived), jnp.where(low, arrived, own))


def first_scalars(tile, live):
    def row(k):
        return (
            jnp.sum(tile[k : k + 1, :], axis=1, keepdims=True) / live,
            tile[8 + k : 9 + k, 0:1],
            tile[16 + k : 17 + k, 0:1],
        )

    square, scale, _ = row(0)
    norm = scale * jnp.sqrt(square)
    cross, image_scale, start_scale = row(1)
    alpha = cross * (image_scale / norm) * (start_scale / norm)
    image_square, image_scale, _ = row(2)
    unit = image_scale / norm
    rest = image_square - (alpha / unit) * (alpha / unit)
    return norm, alpha, unit * jnp.sqrt(jnp.maximum(rest, 0.0))


def input_scale(norm, beta):
    return (1.0 / (norm * beta)).astype(BF16)


def form(gram, a, b):
    return sum(a[i] * b[j] * gram[min(i, j)][max(i, j)] for i in a for j in b)


def plus(scale, *terms):
    out = {}
    for c, vector in terms:
        for i, v in vector.items():
            out[i] = out[i] + c * v if i in out else c * v
    return {i: scale * v for i, v in out.items()}


def start_kernel(rows_ref, x_ref, *refs):
    sectors, block_rows, _ = x_ref.shape
    for t in range(sectors):
        for which in range(2):
            part = half_of(which, block_rows // 2)
            value = masked(
                x_ref[t, part, :].astype(F32), part.start, rows_of(rows_ref, t, sectors)
            )
            refs[2 * t + which][...] = (value * START_SCALE).astype(BF16)


def place_of(k):
    pair = jnp.where(lax.axis_index("sec") % 2 == 0, 2, 0)
    return (1, pair, 2 - pair)[k]


def stage_kernel(left_ref, right_ref, left_out, right_out, sems):
    copies = [
        pltpu.make_async_copy(left_ref, left_out, sems.at[0]),
        pltpu.make_async_copy(right_ref, right_out, sems.at[1]),
    ]
    for copy in copies:
        copy.start()
    for copy in copies:
        copy.wait()


def gather_sources(slots, refs, scalars, v_ref):
    half = refs[0].shape[0]
    if scalars:
        rows_ref, tile_ref = scalars
        norm, _, beta = first_scalars(tile_ref, live_entries(rows_ref, v_ref.shape[2]))
        scale = input_scale(norm, beta)
    for i, slot in enumerate(slots):
        for which in range(2):
            value = refs[2 * i + which][...]
            if scalars:
                value = value * scale
            v_ref[slot, half_of(which, half), :] = value


def full_kernel(target, *refs):
    operators, sources, rest = refs[:6], refs[6:18], refs[18:]
    if len(rest) == 2:
        scalars, outs, v_ref = (), rest[:1], rest[1]
    else:
        *scalars, keep_ref, give_ref, v_ref, total_ref = rest
        outs = keep_ref, give_ref
    gather_sources((0, 1, 2, 3, 4, 5), sources, scalars, v_ref)
    far = place_of(2)
    half = sources[0].shape[0]
    total = None
    for shifts_ref, left_ref, right_ref in (operators[:3], operators[3:]):
        for w in range(left_ref.shape[0]):
            offset = target - shifts_ref[w]
            place = (offset >> 1) + 1
            kind = jnp.where(place == 1, 0, jnp.where(place == far, 4, 2))
            part = jnp.dot(
                left_ref[w, target, half_of(0, half), :],
                v_ref[kind + (offset & 1)],
                preferred_element_type=F32,
            ).astype(BF16)
            term = jnp.dot(part, right_ref[w], preferred_element_type=F32)
            total = term if total is None else total + term
    if len(outs) == 1:
        outs[0][...] = total.astype(BF16)
    else:
        total_ref[...] = total.astype(BF16)
        for which, ref in enumerate(outs):
            ref[...] = total_ref[side_of(which, half // 2, lax.axis_size("op")), :]


def add_kernel(a_ref, b_ref, out_ref):
    out_ref[...] = (a_ref[...].astype(F32) + b_ref[...].astype(F32)).astype(BF16)


def image_kernel(product, target, sectors, rows_ref, a_ref, b_ref, *refs):
    out_ref = refs[-2] if product == 2 else refs[-1]
    half, columns = out_ref.shape
    value = a_ref[...].astype(F32) + b_ref[...].astype(F32)
    rows = rows_of(rows_ref, target, sectors)
    first_row = my_core() * half
    part = pl.ds(0, half)
    if product == 2:
        part = side_of(0, half, lax.axis_size("op"))
        first_row = 2 * first_row + part.start
    value = masked(value, first_row, rows)
    if product < 2:
        out_ref[...] = value.astype(BF16)
        return
    stats_ref = refs[-1]
    basis = [r[part, :].astype(F32) for r in refs[: product + 1]]
    tile_ref, before = refs[product + 1], refs[product + 2] if target else None
    norm, alpha, beta = first_scalars(tile_ref, live_entries(rows_ref, columns))
    zeroth, image, second = (block * (1.0 / norm) for block in basis)
    scale = 1.0 / beta
    first = (image - alpha * zeroth) * scale
    value = value * (scale / (input_scale(norm, beta).astype(F32) * norm))
    value = (value - (alpha * scale) * second) * scale
    second = (second - alpha * image) * scale
    value = value.astype(BF16)
    out_ref[...] = value
    value = value.astype(F32)
    known = [second * second, second * first, second * zeroth]
    write_sums(stats_ref, known + [value * v for v in (value, second, first, zeroth)], before)


def tile_kernel(*refs):
    *blocks, tile_ref = refs
    tile = None
    for start_ref, image_ref in zip(blocks[::2], blocks[1::2]):
        start, image = start_ref[...].astype(F32), image_ref[...].astype(F32)
        part = scaled_sums([(start, start), (image, start), (image, image)])
        tile = part if tile is None else merged(tile, part)
    tile_ref[...] = tile


def last_kernel(rows_ref, *refs):
    out_ref, coef_ref = refs[-2:]
    tile_ref, last_stats = refs[-4:-2]
    sectors, block_rows, columns = out_ref.shape
    live = live_entries(rows_ref, columns)
    norm, alpha0, beta0 = first_scalars(tile_ref, live)
    one, none = jnp.ones_like(norm), jnp.zeros_like(norm)
    w11, w1q1, w1q0, zz, zw1, zq1, zq0 = (inner(last_stats, k, live) for k in range(7))
    gram = [[one, none, w1q0, zq0], [None, one, w1q1, zq1], [None, None, w11, zw1], [None] * 3 + [zz]]
    q0, q1, w1 = {0: one}, {1: one}, {2: one}
    alpha1 = w1q1
    r1 = plus(one, (one, w1), (-alpha1, q1), (-beta0, q0))
    beta1 = jnp.sqrt(jnp.maximum(form(gram, r1, r1), 0.0))
    q2 = plus(1.0 / beta1, (one, r1))
    w0 = {0: alpha0, 1: beta0}
    w2 = plus(1.0 / beta1, (beta0, {3: one}), (-alpha1, w1), (-beta0, w0))
    alpha2 = form(gram, q2, w2)
    r2 = plus(one, (one, w2), (-alpha2, q2), (-beta1, q1))
    beta2 = jnp.sqrt(jnp.maximum(form(gram, r2, r2), 0.0))
    q3 = plus(1.0 / beta2, (one, r2))
    c1 = q3[1] / beta0
    c2 = q3[2] / beta0
    coefs = [(q3[0] - alpha0 * c1) / norm, (c1 - alpha0 * c2) / norm, c2 / norm, q3[3]]
    quarter = block_rows // 4
    chunk = 32
    for t in range(sectors):
        sector_refs = refs[10 * t : 10 * t + 10]
        for which in range(2):
            start = half_of(which, 2 * quarter).start
            for side in range(2):
                part = side_of(side, quarter, lax.axis_size("op"))
                for r in range(0, quarter, chunk):
                    here = pl.ds(pl.multiple_of(part.start + r, chunk), chunk)
                    blocks = [sector_refs[2 * k + which][here, :] for k in range(3)]
                    blocks.append(sector_refs[6 + 2 * side + which][r : r + chunk, :])
                    vector = sum(c * block.astype(F32) for c, block in zip(coefs, blocks))
                    rows = pl.ds(pl.multiple_of(start + part.start + r, chunk), chunk)
                    out_ref[t, rows, :] = vector.astype(BF16)
    row = lax.broadcasted_iota(jnp.int32, coef_ref.shape, 0)
    column = lax.broadcasted_iota(jnp.int32, coef_ref.shape, 1)
    value = jnp.zeros(coef_ref.shape, F32)
    for k, (alpha, beta) in enumerate(((alpha0, beta0), (alpha1, beta1), (alpha2, beta2))):
        value = jnp.where((row == 0) & (column == k), alpha, value)
        value = jnp.where((row == 1) & (column == k), beta, value)
    coef_ref[...] = value


def on_device(wavefunction, left_blocks, right_blocks, charge_shifts, sector_rows):
    sectors, block_rows, columns = wavefunction.shape
    half = block_rows // 2
    n_sec, n_op = lax.axis_size("sec"), lax.axis_size("op")
    assert sectors == 2 and n_sec % 4 == 0 and n_op % 4 == 0
    core_pairs = [(i, i ^ 1) for i in range(n_op)]
    pairs = [(i, i ^ 1) for i in range(n_sec)]
    onward = [(i, i + 2) for i in range(0, n_sec - 2, 2)]
    onward += [(i, i - 2) for i in range(3, n_sec, 2)]
    diagonal = [(i, i + 1) for i in range(1, n_sec - 1, 2)]
    diagonal += [(j, i) for i, j in diagonal]

    def across_cores(value):
        return lax.ppermute(value, "op", core_pairs)

    def flipped_sum(stats, bits):
        for bit in bits:
            stats = stats + lax.ppermute(stats, "sec", [(i, i ^ bit) for i in range(n_sec)])
        return stats

    def flipped_merge(tile, axis, bits):
        for bit in bits:
            flips = [(i, i ^ bit) for i in range(lax.axis_size(axis))]
            arrived = lax.ppermute(tile, axis, flips)
            tile = call(
                functools.partial(merge_kernel, axis, bit), "merge", tile_type, [], tile, arrived
            )
        return tile

    def sum_four(stats, one, two):
        places = range(n_sec * n_op)
        first, second, both = (
            lax.ppermute(stats, ("sec", "op"), [(i, i ^ mask) for i in places])
            for mask in (one, two, one ^ two)
        )
        return (stats + both) + (first + second)

    bits = [1 << k for k in range(n_sec.bit_length() - 1)]

    last_bit = n_op // 2
    half_type = jax.ShapeDtypeStruct((half, columns), BF16)
    quarter_type = jax.ShapeDtypeStruct((half // 2, columns), BF16)
    stats_type = jax.ShapeDtypeStruct((8, 128), F32)
    tile_type = jax.ShapeDtypeStruct((24, 128), F32)
    v_scratch = pltpu.VMEM((6, block_rows, columns), BF16)

    halves = call(
        start_kernel, "start", [half_type] * (2 * sectors), [], sector_rows, wavefunction
    )
    basis = [[(halves[0], halves[1]), (halves[2], halves[3])]]
    pair_0 = lax.ppermute(halves[0], "sec", pairs)
    operators = (charge_shifts, left_blocks, right_blocks)
    others = tuple(across_cores(value) for value in operators)
    stats = []
    hbm = pl.BlockSpec(memory_space=pltpu.HBM)
    left, right = pl.pallas_call(
        stage_kernel,
        name="stage",
        out_shape=[jax.ShapeDtypeStruct(v.shape, v.dtype) for v in operators[1:]],
        in_specs=[hbm] * 2,
        out_specs=[VMEM] * 2,
        scratch_shapes=[pltpu.SemaphoreType.DMA((2,))],
        compiler_params=pltpu.CompilerParams(vmem_limit_bytes=16 << 20),
        cost_estimate=pl.CostEstimate(flops=0, bytes_accessed=0, transcendentals=0),
    )(operators[1], operators[2])
    operators = (charge_shifts, left, right) + others
    pair_0 = after(pair_0, left)

    for product in range(3):
        (mine_0, other_0), (mine_1, other_1) = basis[-1]
        if product:
            pair_0 = lax.ppermute(mine_0, "sec", pairs)
        if product:
            pair_0 = after(pair_0, mine_1)
        else:
            mine_1 = after(mine_1, pair_0)
        if product == 2:
            tile = flipped_merge(after(tile, mine_0), "sec", bits[1:2])
            pair_0 = after(pair_0, tile)
        pair_1 = lax.ppermute(mine_1, "sec", pairs)
        far_0 = lax.ppermute(pair_0, "sec", onward)
        far_1 = lax.ppermute(mine_1, "sec", diagonal)
        pair_1 = after(pair_1, far_0)
        if product == 1:
            blocks = [b[t][0] for t in range(sectors) for b in basis]
            blocks[0] = after(blocks[0], pair_0)
            sums = call(tile_kernel, "tile", tile_type, [], *blocks)
            tile = flipped_merge(flipped_merge(sums, "op", [1]), "sec", bits[:1])
            pair_1 = after(pair_1, tile)
        elif product == 2:
            tile = flipped_merge(after(tile, pair_0), "sec", bits[2:])
            stats.append(tile)
            pair_1 = after(pair_1, tile)
        scalars = (sector_rows, *stats) if product == 2 else ()
        sources = [mine_0, other_0, mine_1, other_1]
        for part in (pair_0, pair_1, far_0, far_1):
            sources += [part, across_cores(part)]
        out, scratch = [half_type], [v_scratch]
        if product == 2:
            out = [quarter_type] * 2
            scratch.append(pltpu.VMEM((half, columns), BF16))
        values = [
            call(
                functools.partial(full_kernel, t), "full", out, scratch,
                *operators, *sources, *scalars,
            )
            for t in range(sectors)
        ]
        image = []
        earlier = []
        for t, parts in enumerate(values):
            bit = 2
            while bit < last_bit:
                flips = [(i, i ^ bit) for i in range(n_op)]
                parts = [
                    call(add_kernel, "add", jax.ShapeDtypeStruct(part.shape, BF16), [], part, lax.ppermute(part, "op", flips))
                    for part in parts
                ]
                bit *= 2
            flips = [(i, i ^ last_bit) for i in range(n_op)]
            arrived = lax.ppermute(parts[-1], "op", flips)
            if t == 0:
                arrived = after(arrived, values[-1][0])
            out = (half_type, half_type, quarter_type)[product]
            needed = () if product < 2 else (*[b[t][0] for b in basis], *stats, *earlier)
            mine, *earlier = call(
                functools.partial(image_kernel, product, t, sectors), "image",
                [out] if product < 2 else [out, stats_type], [],
                sector_rows, parts[0], arrived, *needed,
            )
            image.append((mine, across_cores(mine)))
            if product == 2:
                other = lax.ppermute(mine, "op", flips)
                image[-1] += (other, across_cores(other))
        basis.append(image)
        if earlier:
            sums = earlier[0]
    sums = sum_four(sum_four(sums, 1, last_bit), n_op, 2 * n_op)
    stats.append(flipped_sum(sums, bits[2:]))

    flat = [h for t in range(sectors) for b in basis for h in b[t]]
    vector_type = jax.ShapeDtypeStruct(wavefunction.shape, BF16)
    coef_type = jax.ShapeDtypeStruct((2, 3), F32)
    vector, coef = call(
        last_kernel, "last", [vector_type, coef_type], [], sector_rows, *flat, *stats
    )
    return vector, coef


def solution(mesh):
    in_specs = (P("sec", None, None), P("op", "sec", None, None), P("op", None, None), P("op"), P())
    out_specs = (P("sec", None, None), P())
    return jax.shard_map(
        on_device, mesh=mesh, in_specs=in_specs, out_specs=out_specs, check_vma=False
    )
```

```python
import functools

import jax
import jax.numpy as jnp
from jax import lax
from jax.experimental import pallas as pl
from jax.experimental.pallas import tpu as pltpu
from jax.sharding import PartitionSpec as P

F32 = jnp.float32
BF16 = jnp.bfloat16
START_SCALE = 2.0**60
VMEM = pl.BlockSpec(memory_space=pltpu.VMEM)
SMEM = pl.BlockSpec(memory_space=pltpu.SMEM)


def call(kernel, name, out, scratch, *operands):
    return pl.pallas_call(
        kernel,
        name=name,
        out_shape=out,
        in_specs=[SMEM if a.dtype == jnp.int32 else VMEM for a in operands],
        out_specs=jax.tree.map(lambda _: VMEM, out),
        scratch_shapes=scratch,
        compiler_params=pltpu.CompilerParams(vmem_limit_bytes=16 << 20),
        cost_estimate=pl.CostEstimate(flops=0, bytes_accessed=0, transcendentals=0),
    )(*operands)


def after(value, *others):
    return lax.optimization_barrier((value, *others))[0]


def my_core():
    return lax.axis_index("op") % 2


def half_of(which, half):
    core = my_core()
    return pl.ds(pl.multiple_of((core if which == 0 else 1 - core) * half, half), half)


def side_of(which, rows, count):
    side = lax.axis_index("op") // (count // 2)
    return pl.ds(pl.multiple_of((side if which == 0 else 1 - side) * rows, rows), rows)


def rows_of(rows_ref, target, sectors):
    return rows_ref[lax.axis_index("sec") * sectors + target]


def live_entries(rows_ref, columns):
    return sum(rows_ref[i] for i in range(rows_ref.shape[0])).astype(F32) * columns


def masked(value, first, rows):
    return jnp.where(lax.broadcasted_iota(jnp.int32, value.shape, 0) + first < rows, value, 0.0)


def inner(stats_ref, row, live):
    return jnp.sum(stats_ref[row : row + 1, :], axis=1, keepdims=True) / live


def write_sums(stats_ref, values, before=None):
    parts = [jnp.zeros((1, 128), F32)] * 8
    for k, value in enumerate(values):
        folded = sum(value[:, i : i + 128] for i in range(0, value.shape[1], 128))
        parts[k] = jnp.sum(folded, axis=0, keepdims=True)
    rows = jnp.concatenate(parts, axis=0)
    stats_ref[...] = rows if before is None else rows + before[...]


def largest(value):
    return jnp.maximum(jnp.max(jnp.abs(value), keepdims=True), 1e-37)


def scaled_sums(pairs):
    sums, lefts, rights = [], [], []
    for left, right in pairs:
        scales = largest(left), largest(right)
        product = (left * (1.0 / scales[0])) * (right * (1.0 / scales[1]))
        folded = sum(product[:, i : i + 128] for i in range(0, product.shape[1], 128))
        sums.append(jnp.sum(folded, axis=0, keepdims=True))
        lefts.append(jnp.broadcast_to(scales[0], (1, 128)))
        rights.append(jnp.broadcast_to(scales[1], (1, 128)))
    fill = [jnp.zeros((1, 128), F32)] * (8 - len(pairs))
    ones = [jnp.full((1, 128), 1e-37, F32)] * (8 - len(pairs))
    return jnp.concatenate(sums + fill + lefts + ones + rights + ones, axis=0)


def merged(a, b):
    left = jnp.maximum(a[8:16], b[8:16])
    right = jnp.maximum(a[16:], b[16:])
    total = sum(t[:8] * (t[8:16] / left) * (t[16:] / right) for t in (a, b))
    return jnp.concatenate([total, left, right], axis=0)


def merge_kernel(axis, bit, own_ref, arrived_ref, out_ref):
    low = lax.axis_index(axis) & bit == 0
    own, arrived = own_ref[...], arrived_ref[...]
    out_ref[...] = merged(jnp.where(low, own, arrived), jnp.where(low, arrived, own))


def first_scalars(tile, live):
    def row(k):
        return (
            jnp.sum(tile[k : k + 1, :], axis=1, keepdims=True) / live,
            tile[8 + k : 9 + k, 0:1],
            tile[16 + k : 17 + k, 0:1],
        )

    square, scale, _ = row(0)
    norm = scale * jnp.sqrt(square)
    cross, image_scale, start_scale = row(1)
    alpha = cross * (image_scale / norm) * (start_scale / norm)
    image_square, image_scale, _ = row(2)
    unit = image_scale / norm
    rest = image_square - (alpha / unit) * (alpha / unit)
    return norm, alpha, unit * jnp.sqrt(jnp.maximum(rest, 0.0))


def input_scale(norm, beta):
    return (1.0 / (norm * beta)).astype(BF16)


def form(gram, a, b):
    return sum(a[i] * b[j] * gram[min(i, j)][max(i, j)] for i in a for j in b)


def plus(scale, *terms):
    out = {}
    for c, vector in terms:
        for i, v in vector.items():
            out[i] = out[i] + c * v if i in out else c * v
    return {i: scale * v for i, v in out.items()}


def start_kernel(rows_ref, x_ref, *refs):
    sectors, block_rows, _ = x_ref.shape
    for t in range(sectors):
        for which in range(2):
            part = half_of(which, block_rows // 2)
            value = masked(
                x_ref[t, part, :].astype(F32), part.start, rows_of(rows_ref, t, sectors)
            )
            refs[2 * t + which][...] = (value * START_SCALE).astype(BF16)


def place_of(k):
    pair = jnp.where(lax.axis_index("sec") % 2 == 0, 2, 0)
    return (1, pair, 2 - pair)[k]


def stage_kernel(left_ref, right_ref, left_out, right_out, sems):
    copies = [
        pltpu.make_async_copy(left_ref, left_out, sems.at[0]),
        pltpu.make_async_copy(right_ref, right_out, sems.at[1]),
    ]
    for copy in copies:
        copy.start()
    for copy in copies:
        copy.wait()


def gather_sources(slots, refs, scalars, v_ref):
    half = refs[0].shape[0]
    if scalars:
        rows_ref, tile_ref = scalars
        norm, _, beta = first_scalars(tile_ref, live_entries(rows_ref, v_ref.shape[2]))
        scale = input_scale(norm, beta)
    for i, slot in enumerate(slots):
        for which in range(2):
            value = refs[2 * i + which][...]
            if scalars:
                value = value * scale
            v_ref[slot, half_of(which, half), :] = value


def full_kernel(target, *refs):
    operators, sources, rest = refs[:6], refs[6:18], refs[18:]
    if len(rest) == 2:
        scalars, outs, v_ref = (), rest[:1], rest[1]
    else:
        *scalars, keep_ref, give_ref, v_ref, total_ref = rest
        outs = keep_ref, give_ref
    gather_sources((0, 1, 2, 3, 4, 5), sources, scalars, v_ref)
    far = place_of(2)
    half = sources[0].shape[0]
    total = None
    for shifts_ref, left_ref, right_ref in (operators[:3], operators[3:]):
        for w in range(left_ref.shape[0]):
            offset = target - shifts_ref[w]
            place = (offset >> 1) + 1
            kind = jnp.where(place == 1, 0, jnp.where(place == far, 4, 2))
            part = jnp.dot(
                left_ref[w, target, half_of(0, half), :],
                v_ref[kind + (offset & 1)],
                preferred_element_type=F32,
            ).astype(BF16)
            term = jnp.dot(part, right_ref[w], preferred_element_type=F32)
            total = term if total is None else total + term
    if len(outs) == 1:
        outs[0][...] = total.astype(BF16)
    else:
        total_ref[...] = total.astype(BF16)
        for which, ref in enumerate(outs):
            ref[...] = total_ref[side_of(which, half // 2, lax.axis_size("op")), :]


def add_kernel(a_ref, b_ref, out_ref):
    out_ref[...] = (a_ref[...].astype(F32) + b_ref[...].astype(F32)).astype(BF16)


def image_kernel(product, target, sectors, rows_ref, a_ref, b_ref, *refs):
    out_ref = refs[-2] if product == 2 else refs[-1]
    half, columns = out_ref.shape
    value = a_ref[...].astype(F32) + b_ref[...].astype(F32)
    rows = rows_of(rows_ref, target, sectors)
    first_row = my_core() * half
    part = pl.ds(0, half)
    if product == 2:
        part = side_of(0, half, lax.axis_size("op"))
        first_row = 2 * first_row + part.start
    value = masked(value, first_row, rows)
    if product < 2:
        out_ref[...] = value.astype(BF16)
        return
    stats_ref = refs[-1]
    basis = [r[part, :].astype(F32) for r in refs[: product + 1]]
    tile_ref, before = refs[product + 1], refs[product + 2] if target else None
    norm, alpha, beta = first_scalars(tile_ref, live_entries(rows_ref, columns))
    zeroth, image, second = (block * (1.0 / norm) for block in basis)
    scale = 1.0 / beta
    first = (image - alpha * zeroth) * scale
    value = value * (scale / (input_scale(norm, beta).astype(F32) * norm))
    value = (value - (alpha * scale) * second) * scale
    second = (second - alpha * image) * scale
    value = value.astype(BF16)
    out_ref[...] = value
    value = value.astype(F32)
    known = [second * second, second * first, second * zeroth]
    write_sums(stats_ref, known + [value * v for v in (value, second, first, zeroth)], before)


def tile_kernel(*refs):
    *blocks, tile_ref = refs
    tile = None
    for start_ref, image_ref in zip(blocks[::2], blocks[1::2]):
        start, image = start_ref[...].astype(F32), image_ref[...].astype(F32)
        part = scaled_sums([(start, start), (image, start), (image, image)])
        tile = part if tile is None else merged(tile, part)
    tile_ref[...] = tile


def last_kernel(rows_ref, *refs):
    out_ref, coef_ref = refs[-2:]
    tile_ref, last_stats = refs[-4:-2]
    sectors, block_rows, columns = out_ref.shape
    live = live_entries(rows_ref, columns)
    norm, alpha0, beta0 = first_scalars(tile_ref, live)
    one, none = jnp.ones_like(norm), jnp.zeros_like(norm)
    w11, w1q1, w1q0, zz, zw1, zq1, zq0 = (inner(last_stats, k, live) for k in range(7))
    gram = [[one, none, w1q0, zq0], [None, one, w1q1, zq1], [None, None, w11, zw1], [None] * 3 + [zz]]
    q0, q1, w1 = {0: one}, {1: one}, {2: one}
    alpha1 = w1q1
    r1 = plus(one, (one, w1), (-alpha1, q1), (-beta0, q0))
    beta1 = jnp.sqrt(jnp.maximum(form(gram, r1, r1), 0.0))
    q2 = plus(1.0 / beta1, (one, r1))
    w0 = {0: alpha0, 1: beta0}
    w2 = plus(1.0 / beta1, (beta0, {3: one}), (-alpha1, w1), (-beta0, w0))
    alpha2 = form(gram, q2, w2)
    r2 = plus(one, (one, w2), (-alpha2, q2), (-beta1, q1))
    beta2 = jnp.sqrt(jnp.maximum(form(gram, r2, r2), 0.0))
    q3 = plus(1.0 / beta2, (one, r2))
    c1 = q3[1] / beta0
    c2 = q3[2] / beta0
    coefs = [(q3[0] - alpha0 * c1) / norm, (c1 - alpha0 * c2) / norm, c2 / norm, q3[3]]
    quarter = block_rows // 4
    chunk = 16
    for t in range(sectors):
        sector_refs = refs[10 * t : 10 * t + 10]
        for which in range(2):
            start = half_of(which, 2 * quarter).start
            for side in range(2):
                part = side_of(side, quarter, lax.axis_size("op"))
                for r in range(0, quarter, chunk):
                    here = pl.ds(pl.multiple_of(part.start + r, chunk), chunk)
                    blocks = [sector_refs[2 * k + which][here, :] for k in range(3)]
                    blocks.append(sector_refs[6 + 2 * side + which][r : r + chunk, :])
                    vector = sum(c * block.astype(F32) for c, block in zip(coefs, blocks))
                    rows = pl.ds(pl.multiple_of(start + part.start + r, chunk), chunk)
                    out_ref[t, rows, :] = vector.astype(BF16)
    row = lax.broadcasted_iota(jnp.int32, coef_ref.shape, 0)
    column = lax.broadcasted_iota(jnp.int32, coef_ref.shape, 1)
    value = jnp.zeros(coef_ref.shape, F32)
    for k, (alpha, beta) in enumerate(((alpha0, beta0), (alpha1, beta1), (alpha2, beta2))):
        value = jnp.where((row == 0) & (column == k), alpha, value)
        value = jnp.where((row == 1) & (column == k), beta, value)
    coef_ref[...] = value


def on_device(wavefunction, left_blocks, right_blocks, charge_shifts, sector_rows):
    sectors, block_rows, columns = wavefunction.shape
    half = block_rows // 2
    n_sec, n_op = lax.axis_size("sec"), lax.axis_size("op")
    assert sectors == 2 and n_sec % 4 == 0 and n_op % 4 == 0
    core_pairs = [(i, i ^ 1) for i in range(n_op)]
    pairs = [(i, i ^ 1) for i in range(n_sec)]
    onward = [(i, i + 2) for i in range(0, n_sec - 2, 2)]
    onward += [(i, i - 2) for i in range(3, n_sec, 2)]
    diagonal = [(i, i + 1) for i in range(1, n_sec - 1, 2)]
    diagonal += [(j, i) for i, j in diagonal]

    def across_cores(value):
        return lax.ppermute(value, "op", core_pairs)

    def flipped_sum(stats, bits):
        for bit in bits:
            stats = stats + lax.ppermute(stats, "sec", [(i, i ^ bit) for i in range(n_sec)])
        return stats

    def flipped_merge(tile, axis, bits):
        for bit in bits:
            flips = [(i, i ^ bit) for i in range(lax.axis_size(axis))]
            arrived = lax.ppermute(tile, axis, flips)
            tile = call(
                functools.partial(merge_kernel, axis, bit), "merge", tile_type, [], tile, arrived
            )
        return tile

    def sum_four(stats, one, two):
        places = range(n_sec * n_op)
        first, second, both = (
            lax.ppermute(stats, ("sec", "op"), [(i, i ^ mask) for i in places])
            for mask in (one, two, one ^ two)
        )
        return (stats + both) + (first + second)

    bits = [1 << k for k in range(n_sec.bit_length() - 1)]

    last_bit = n_op // 2
    half_type = jax.ShapeDtypeStruct((half, columns), BF16)
    quarter_type = jax.ShapeDtypeStruct((half // 2, columns), BF16)
    stats_type = jax.ShapeDtypeStruct((8, 128), F32)
    tile_type = jax.ShapeDtypeStruct((24, 128), F32)
    v_scratch = pltpu.VMEM((6, block_rows, columns), BF16)

    halves = call(
        start_kernel, "start", [half_type] * (2 * sectors), [], sector_rows, wavefunction
    )
    basis = [[(halves[0], halves[1]), (halves[2], halves[3])]]
    pair_0 = lax.ppermute(halves[0], "sec", pairs)
    operators = (charge_shifts, left_blocks, right_blocks)
    others = tuple(across_cores(value) for value in operators)
    stats = []
    hbm = pl.BlockSpec(memory_space=pltpu.HBM)
    left, right = pl.pallas_call(
        stage_kernel,
        name="stage",
        out_shape=[jax.ShapeDtypeStruct(v.shape, v.dtype) for v in operators[1:]],
        in_specs=[hbm] * 2,
        out_specs=[VMEM] * 2,
        scratch_shapes=[pltpu.SemaphoreType.DMA((2,))],
        compiler_params=pltpu.CompilerParams(vmem_limit_bytes=16 << 20),
        cost_estimate=pl.CostEstimate(flops=0, bytes_accessed=0, transcendentals=0),
    )(operators[1], operators[2])
    operators = (charge_shifts, left, right) + others
    pair_0 = after(pair_0, left)

    for product in range(3):
        (mine_0, other_0), (mine_1, other_1) = basis[-1]
        if product:
            pair_0 = lax.ppermute(mine_0, "sec", pairs)
        if product:
            pair_0 = after(pair_0, mine_1)
        else:
            mine_1 = after(mine_1, pair_0)
        if product == 2:
            tile = flipped_merge(after(tile, mine_0), "sec", bits[1:2])
            pair_0 = after(pair_0, tile)
        pair_1 = lax.ppermute(mine_1, "sec", pairs)
        far_0 = lax.ppermute(pair_0, "sec", onward)
        far_1 = lax.ppermute(mine_1, "sec", diagonal)
        pair_1 = after(pair_1, far_0)
        if product == 1:
            blocks = [b[t][0] for t in range(sectors) for b in basis]
            blocks[0] = after(blocks[0], pair_0)
            sums = call(tile_kernel, "tile", tile_type, [], *blocks)
            tile = flipped_merge(flipped_merge(sums, "op", [1]), "sec", bits[:1])
            pair_1 = after(pair_1, tile)
        elif product == 2:
            tile = flipped_merge(after(tile, pair_0), "sec", bits[2:])
            stats.append(tile)
            pair_1 = after(pair_1, tile)
        scalars = (sector_rows, *stats) if product == 2 else ()
        sources = [mine_0, other_0, mine_1, other_1]
        for part in (pair_0, pair_1, far_0, far_1):
            sources += [part, across_cores(part)]
        out, scratch = [half_type], [v_scratch]
        if product == 2:
            out = [quarter_type] * 2
            scratch.append(pltpu.VMEM((half, columns), BF16))
        values = [
            call(
                functools.partial(full_kernel, t), "full", out, scratch,
                *operators, *sources, *scalars,
            )
            for t in range(sectors)
        ]
        image = []
        earlier = []
        for t, parts in enumerate(values):
            bit = 2
            while bit < last_bit:
                flips = [(i, i ^ bit) for i in range(n_op)]
                parts = [
                    call(add_kernel, "add", jax.ShapeDtypeStruct(part.shape, BF16), [], part, lax.ppermute(part, "op", flips))
                    for part in parts
                ]
                bit *= 2
            flips = [(i, i ^ last_bit) for i in range(n_op)]
            arrived = lax.ppermute(parts[-1], "op", flips)
            if t == 0:
                arrived = after(arrived, values[-1][0])
            out = (half_type, half_type, quarter_type)[product]
            needed = () if product < 2 else (*[b[t][0] for b in basis], *stats, *earlier)
            mine, *earlier = call(
                functools.partial(image_kernel, product, t, sectors), "image",
                [out] if product < 2 else [out, stats_type], [],
                sector_rows, parts[0], arrived, *needed,
            )
            image.append((mine, across_cores(mine)))
            if product == 2:
                other = lax.ppermute(mine, "op", flips)
                image[-1] += (other, across_cores(other))
        basis.append(image)
        if earlier:
            sums = earlier[0]
    sums = sum_four(sum_four(sums, 1, last_bit), n_op, 2 * n_op)
    stats.append(flipped_sum(sums, bits[2:]))

    flat = [h for t in range(sectors) for b in basis for h in b[t]]
    vector_type = jax.ShapeDtypeStruct(wavefunction.shape, BF16)
    coef_type = jax.ShapeDtypeStruct((2, 3), F32)
    vector, coef = call(
        last_kernel, "last", [vector_type, coef_type], [], sector_rows, *flat, *stats
    )
    return vector, coef


def solution(mesh):
    in_specs = (P("sec", None, None), P("op", "sec", None, None), P("op", None, None), P("op"), P())
    out_specs = (P("sec", None, None), P())
    return jax.shard_map(
        on_device, mesh=mesh, in_specs=in_specs, out_specs=out_specs, check_vma=False
    )
```
